32 devices in a mesh: dp: 16 (over z, y, x), head: 2 (over core).
Axes of the slice: x: 2, y: 2, z: 4, core: 2. Of those that a mesh axis runs over, the one named last changes fastest.
Arguments:
- ids: int32 [16, 512], P('dp'), may hold values from 0 to 32127, as said below
- segments: int32 [16, 412], P('dp'), may hold values from 0 to 5, never falling along the last dimension, each value on 1 to 407 neighbouring positions
- valid_rows: int32 [16], P('dp'), may hold values from 1 to 412, as said below
- prompt: float32 [100, 768], replicated, may hold values from -6 to 6
- table: bfloat16 [32128, 768], P('dp'), may hold values from -6 to 6
- attn_gain: float32 [768], replicated, may hold values from 0.1 to 1.9
- w_qkv: bfloat16 [768, 3, 768], P(None, None, 'head'), may hold values from -0.21875 to 0.21875
- rel_bias: bfloat16 [32, 12], P(None, 'head'), may hold values from -4 to 4
- w_out: bfloat16 [768, 768], P('head'), may hold values from -1.75 to 1.75
- ff_gain: float32 [768], replicated, may hold values from 0.1 to 1.9
- w_in: bfloat16 [768, 3072], P(None, 'head'), may hold values from -0.21875 to 0.21875
- w_down: bfloat16 [3072, 768], P('head'), may hold values from -0.109375 to 0.109375
- cotangent: bfloat16 [8192, 768], P(('dp', 'head')), may hold values from -6 to 6
- first_moment: float32 [100, 768], replicated, may hold values from -3 to 3
- second_moment: float32 [100, 768], replicated, may hold values from 0.006666667 to 0.10666667
Outputs:
- layer_out: bfloat16 [8192, 768], P(('dp', 'head'))
- input_grad: float32 [8192, 768], P(('dp', 'head'))
- prompt_grad: float32 [100, 768], replicated
- grad_norm: float32 [], replicated
- prompt_new: float32 [100, 768], replicated
- first_out: float32 [100, 768], replicated
- second_out: float32 [100, 768], replicated
- prompt_low: bfloat16 [100, 768], replicated
The draws below stay inside these ranges and needn't reach their ends.
Inputs may be any that keep to these rules, and one draw needn't show every extreme that they name: `ids`: positions t < 100 of each slot hold a permutation of 0 to 100 - 1 (prompt rows); every other position holds a vocabulary row, whose owner is id // 2008. Among the vocabulary positions of one device's 256 rows (positions b * 256 to (b + 1) * 256 - 1 of a slot) no owner is named more than 32 times, and in every share without prompt rows some owner is named exactly 32 times. The text rows of slot s at t - 100 >= valid_rows[s] are padding. The last slot has 412.
All inputs are finite; a program needn't handle non-finite values.
Results may differ from the reference program's by a relative error of at most 0.012.
The reference program's roundings to bfloat16 on the way count: a program that leaves them out, or rounds other values in their place, can miss the bound.
Values may be sent and summed in bfloat16 or wider, within the bound.
A program may use at most 192 MiB of HBM per device.

```python
import math
import jax
import jax.numpy as jnp
import numpy as np
from jax import lax

D = 768
H = 12
HD = 64
FF = 3072
VOCAB = 32128
NB = 32
P_SIZE = 100
STEP = 10
SLOT = 512
INNER = 768
SLOTS = 16
TEXT = 412
SHARE = 256
VOCAB_DEV = 2008
CAP = 32
ROWS = 8192
N_DP = 16
N_HEAD = 2


def distinct_order(key, rows, count):
    scores = jax.random.randint(key, (rows, count), 1, 1 << 16) * count + jnp.arange(count, dtype=jnp.int32)[None, :]
    return jnp.argsort(scores, axis=1).astype(jnp.int32)


def draw_ids(key, part):
    key = jax.random.fold_in(key, 11)
    pick_key, favor_key, shuffle_key, row_key, prompt_key = jax.random.split(key, 5)
    blocks = SLOTS * N_HEAD
    spots = N_DP * CAP
    spot_index = jnp.arange(spots, dtype=jnp.int32)
    scores = jax.random.randint(pick_key, (blocks, spots), 1, 1 << 16) * spots + spot_index[None, :]
    favored = jax.random.randint(favor_key, (blocks, 1), 0, N_DP)
    scores = jnp.where(spot_index[None, :] // CAP == favored, spot_index[None, :], scores)
    chosen = jnp.argsort(scores, axis=1)[:, :SHARE].astype(jnp.int32)
    shuffle = distinct_order(shuffle_key, blocks, SHARE)
    owners = jnp.take_along_axis(chosen, shuffle, axis=1) // CAP
    rows = jax.random.randint(row_key, (blocks, SHARE), 0, VOCAB_DEV)
    vocab_ids = (owners * VOCAB_DEV + rows).reshape(SLOTS, SLOT)
    prompt_ids = distinct_order(prompt_key, SLOTS, P_SIZE)
    return vocab_ids.at[:, :P_SIZE].set(prompt_ids).astype(jnp.int32)


def draw_valid_rows(key, part):
    key = jax.random.fold_in(key, 23)
    index = jnp.arange(SLOTS, dtype=jnp.int32)
    base = TEXT // 3 + (TEXT - TEXT // 3) * index // max(SLOTS - 1, 1)
    jitter = jax.random.randint(key, (SLOTS,), 0, TEXT // 8 + 1)
    return jnp.where(index == SLOTS - 1, TEXT, jnp.maximum(base - jitter, 1)).astype(jnp.int32)


def level_of(key, extent, pieces, low, largest):
    level, own = 1.0, jax.random.fold_in(key, 6)
    for dim, blocks in pieces:
        draws = jnp.exp(jax.random.uniform(jax.random.fold_in(own, dim), (blocks,), jnp.float32, low / len(pieces), largest / len(pieces)))
        level = level * jnp.repeat(draws, extent[dim] // blocks).reshape([-1 if axis == dim else 1 for axis in range(len(extent))])
    return level


def length_profile(number_of, total, reach, slope):
    weights = [(1 << 20) // math.isqrt(standing ** slope) + 1 for standing in range(2, number_of + 1)]
    surplus, holding = total - reach - (number_of - 1), [1] * (number_of - 1)
    while surplus > 0:
        free = [i for i in range(number_of - 1) if holding[i] < reach]
        mass, remaining = sum([weights[i] for i in free]), surplus
        for i in free:
            extra = min(reach - holding[i], max(1, remaining * weights[i] // mass), surplus)
            holding[i] = holding[i] + extra
            surplus = surplus - extra
    return np.array([reach] + holding)


def uneven(rng, number_of, total, limit, slope):
    if number_of == 2:
        one = jax.random.randint(rng, (), max(1, total - limit), min(limit, total - 1) + 1)
        return jnp.stack([one, total - one])
    lengths = jnp.asarray(length_profile(number_of, total, limit, slope), jnp.int32)
    pairs = (number_of - 1) // 2
    donor, receiver = lengths[1:1 + 2 * pairs:2], lengths[2:2 + 2 * pairs:2]
    slack = jnp.minimum(donor - 1, limit - receiver)
    moved = jax.random.randint(jax.random.fold_in(rng, 1), (pairs,), 0, 1 << 20) % (slack + 1)
    lengths = lengths.at[1:1 + 2 * pairs:2].set(donor - moved).at[2:2 + 2 * pairs:2].set(receiver + moved)
    return lengths[jax.random.permutation(jax.random.fold_in(rng, 2), number_of)]


def bell_draw(stream_key, extent, scale, bound, pieces=(), held_as=jnp.bfloat16):
    array = scale * jax.random.normal(stream_key, extent, jnp.float32)
    if pieces:
        array = array * level_of(stream_key, extent, pieces, -0.22, 0.18)
    return jnp.clip(array, -bound, bound).astype(held_as)


def setup_inputs(seed: int = 0) -> dict:
    key_list = jax.random.split(jax.random.key(seed), 16)
    ids = draw_ids(jax.random.fold_in(key_list[15], 71), 0)
    segments = jax.vmap(lambda own: jnp.searchsorted(jnp.cumsum(uneven(own, max(2, TEXT // 64), TEXT, min(512, TEXT - max(2, TEXT // 64) + 1), 2)), jnp.arange(TEXT), side="right"))(jax.random.split(key_list[1], SLOTS)).reshape((SLOTS, TEXT)).astype(jnp.int32)
    valid_rows = draw_valid_rows(jax.random.fold_in(key_list[15], 71), 0)
    prompt = bell_draw(key_list[3], (P_SIZE, D), 1.0, 6.0, (), jnp.float32)
    table = bell_draw(key_list[4], (VOCAB, D), 1.0, 6.0, ((0, 16),))
    attn_gain = jnp.clip(1.0 + 0.18 * jax.random.normal(key_list[5], (D,), jnp.float32), 0.1, 1.9)
    w_qkv = bell_draw(key_list[6], (D, 3, INNER), D ** -0.5, 0.21875, ((2, 2),))
    rel_bias = bell_draw(key_list[7], (NB, H), 1.0, 4.0, ((1, 2),))
    w_out = bell_draw(key_list[8], (INNER, D), H ** -0.5, 1.75, ((0, 2),))
    ff_gain = jnp.clip(1.0 + 0.18 * jax.random.normal(key_list[9], (D,), jnp.float32), 0.1, 1.9)
    w_in = bell_draw(key_list[10], (D, FF), D ** -0.5, 0.21875, ((1, 2),))
    w_down = bell_draw(key_list[11], (FF, D), FF ** -0.5, 0.109375, ((0, 2),))
    cotangent = bell_draw(key_list[12], (ROWS, D), 1.0, 6.0, ((0, 32),))
    first_moment = bell_draw(key_list[13], (P_SIZE, D), (0.05 * SLOTS ** 0.5), 3.0, (), jnp.float32)
    second_moment = jnp.clip(jnp.exp(jax.random.uniform(key_list[14], (P_SIZE, D), jnp.float32, math.log(0.006666667), math.log(0.10666667))), 0.006666667, 0.10666667)
    return {"ids": ids, "segments": segments, "valid_rows": valid_rows, "prompt": prompt, "table": table, "attn_gain": attn_gain, "w_qkv": w_qkv, "rel_bias": rel_bias, "w_out": w_out, "ff_gain": ff_gain, "w_in": w_in, "w_down": w_down, "cotangent": cotangent, "first_moment": first_moment, "second_moment": second_moment}


norm_epsilon = 1e-06
thresholds = (12, 16, 23, 32, 46, 64, 91)
masked_score = -1000000000.0
learn_rate = 0.5
first_decay = 0.5
second_decay = 0.75
weight_decay = 0.01
adam_epsilon = 1e-08
clip_share = 0.05
exact_mode = lax.Precision.HIGHEST

@jax.custom_vjp
def low(v):
    return lax.optimization_barrier(v.astype(jnp.bfloat16)).astype(jnp.float32)

@jax.custom_vjp
def low_back(v):
    return v

def low_keep(v):
    return (low(v), None)

def low_pass(kept, grad):
    return (grad,)

def back_keep(v):
    return (v, None)

def back_low(kept, grad):
    return (low(grad),)
low.defvjp(low_keep, low_pass)
low_back.defvjp(back_keep, back_low)

def rms_scale(rows, gain):
    return rows * lax.rsqrt(lax.optimization_barrier(jnp.mean(rows * rows, axis=1, keepdims=True)) + norm_epsilon) * gain

def bucket_of(relative):
    magnitude = jnp.abs(relative)
    larger = 8 + sum(((magnitude >= cutoff).astype(jnp.int32) for cutoff in thresholds))
    return jnp.where(magnitude < 8, magnitude, larger) + 16 * (relative > 0).astype(jnp.int32)

def attend(queries, keys, values, seg_full, key_ok, rel_bias):
    block = min(512, SLOT)
    scale = HD ** (-0.5)
    key_pos = jnp.arange(SLOT, dtype=jnp.int32)
    bias_table = rel_bias.T

    def one_block(start):
        q_block = lax.dynamic_slice_in_dim(queries, start, block, 0)
        q_pos = start + jnp.arange(block, dtype=jnp.int32)
        bias = jnp.take(bias_table, bucket_of(key_pos[None, :] - q_pos[:, None]), axis=1)
        seg_q = lax.dynamic_slice_in_dim(seg_full, start, block, 0)
        allowed = (key_pos < P_SIZE)[None, :] | (seg_q[:, None] == seg_full[None, :]) & key_ok[None, :]
        scores = jnp.einsum('qhe,khe->hqk', q_block, keys, precision=exact_mode) * scale + bias
        scores = low_back(jnp.where(allowed[None], scores, masked_score))
        probs = jax.nn.softmax(scores, axis=-1)
        return jnp.einsum('hqk,khe->qhe', low(probs), values, precision=exact_mode)
    starts = jnp.arange(SLOT // block, dtype=jnp.int32) * block
    return lax.map(jax.checkpoint(one_block), starts).reshape(SLOT, H * HD)

def slot_layer(x_start, seg_row, valid, weights):
    attn_gain, w_qkv, rel_bias, w_out, ff_gain, w_in, w_down = weights
    seg_full = jnp.concatenate([jnp.full((P_SIZE,), -1, jnp.int32), seg_row.astype(jnp.int32)])
    key_ok = jnp.arange(SLOT, dtype=jnp.int32) < P_SIZE + valid
    normed = low(rms_scale(x_start, attn_gain))
    mixed = low_back(low(jnp.einsum('rd,dcf->rcf', normed, w_qkv, precision=exact_mode)))
    queries = mixed[:, 0].reshape(SLOT, H, HD)
    keys = mixed[:, 1].reshape(SLOT, H, HD)
    values = mixed[:, 2].reshape(SLOT, H, HD)
    attended = low_back(low(attend(queries, keys, values, seg_full, key_ok, rel_bias)))
    middle = x_start + low_back(jnp.dot(attended, w_out, precision=exact_mode))
    normed_ff = low(rms_scale(middle, ff_gain))
    hidden = low_back(jnp.dot(normed_ff, w_in, precision=exact_mode))
    active = low(jax.nn.gelu(hidden))
    return middle + low_back(jnp.dot(active, w_down, precision=exact_mode))

def reference(ids, segments, valid_rows, prompt, table, attn_gain, w_qkv, rel_bias, w_out, ff_gain, w_in, w_down, cotangent, first_moment, second_moment):
    weights = (attn_gain, w_qkv.astype(jnp.float32), rel_bias.astype(jnp.float32), w_out.astype(jnp.float32), ff_gain, w_in.astype(jnp.float32), w_down.astype(jnp.float32))
    text_rows = jnp.take(table, ids[:, P_SIZE:], axis=0).astype(jnp.float32)
    prompt_ids = ids[:, :P_SIZE]

    def assemble(prompt_value):
        return jnp.concatenate([jnp.take(prompt_value, prompt_ids, axis=0), text_rows], axis=1)
    start_rows, assemble_back = jax.vjp(assemble, prompt)

    def forward(rows_all):

        def step(carry, inputs):
            x_slot, seg_row, valid = inputs
            return (carry, jax.checkpoint(slot_layer)(x_slot, seg_row, valid, weights))
        return lax.scan(step, jnp.zeros((), jnp.float32), (rows_all, segments, valid_rows))[1]
    end_rows, forward_back = jax.vjp(forward, start_rows)
    live = jnp.arange(SLOT, dtype=jnp.int32)[None, :] < P_SIZE + valid_rows[:, None]
    grad_out = cotangent.astype(jnp.float32).reshape(SLOTS, SLOT, D) * live[..., None].astype(jnp.float32)
    grad_rows, = forward_back(grad_out)
    prompt_grad, = assemble_back(grad_rows)
    grad_norm = jnp.sqrt(jnp.sum(prompt_grad * prompt_grad))
    clip_at = clip_share * math.sqrt(P_SIZE * D * SLOTS)
    clipped = prompt_grad * jnp.minimum(1.0, clip_at / (grad_norm + 1e-06))
    first_out = first_decay * first_moment + (1.0 - first_decay) * clipped
    second_out = second_decay * second_moment + (1.0 - second_decay) * clipped * clipped
    first_hat = first_out / (1.0 - first_decay ** STEP)
    second_hat = second_out / (1.0 - second_decay ** STEP)
    prompt_new = prompt - learn_rate * (first_hat / (jnp.sqrt(second_hat) + adam_epsilon) + weight_decay * prompt)
    return (end_rows.reshape(ROWS, D).astype(jnp.bfloat16), grad_rows.reshape(ROWS, D), prompt_grad, grad_norm, prompt_new, first_out, second_out, prompt_new.astype(jnp.bfloat16))
```

```python
import math

import jax
import jax.numpy as jnp
from jax import lax
from jax.sharding import PartitionSpec as P

STEP = 10


norm_epsilon = 1e-06
thresholds = (12, 16, 23, 32, 46, 64, 91)
masked_score = -1000000000.0
learn_rate = 0.5
first_decay = 0.5
second_decay = 0.75
weight_decay = 0.01
adam_epsilon = 1e-08
clip_share = 0.05
exact_mode = lax.Precision.HIGHEST


def rms_scale(rows, gain):
    return rows * lax.rsqrt(jnp.mean(rows * rows, axis=1, keepdims=True) + norm_epsilon) * gain


def rms_back(rows, gain, grad):
    return jax.vjp(lambda inner: rms_scale(inner, gain), rows)[1](grad)[0]


def bucket_of(relative):
    magnitude = jnp.abs(relative)
    larger = 8 + sum(((magnitude >= cutoff).astype(jnp.int32) for cutoff in thresholds))
    return jnp.where(magnitude < 8, magnitude, larger) + 16 * (relative > 0).astype(jnp.int32)


def rows_dot(left, right):
    return jnp.dot(left, right, preferred_element_type=jnp.float32)


def per_device(
    ids,
    segments,
    valid_rows,
    prompt,
    table,
    attn_gain,
    w_qkv,
    rel_bias,
    w_out,
    ff_gain,
    w_in,
    w_down,
    cotangent,
    first_moment,
    second_moment,
):
    heads_count = lax.axis_size("head")
    head_index = lax.axis_index("head")
    groups = lax.axis_size("dp")
    slot_len = ids.shape[1]
    share = slot_len // heads_count
    prompt_len = prompt.shape[0]
    width = prompt.shape[1]
    vocab_share = table.shape[0]
    capacity = max(2, 2 * slot_len // (heads_count * groups))
    spots = groups * capacity
    positions = head_index * share + jnp.arange(share, dtype=jnp.int32)
    row_ids = lax.dynamic_slice_in_dim(ids[0], head_index * share, share, 0)
    prompt_ids = ids[0, :prompt_len]
    in_prompt = positions < prompt_len
    owners = jnp.where(in_prompt, groups, row_ids // vocab_share)
    onehot = (owners[:, None] == jnp.arange(groups, dtype=jnp.int32)[None, :]).astype(jnp.int32)
    ranks = jnp.sum(jnp.cumsum(onehot, axis=0) * onehot, axis=1) - 1
    places = jnp.where(in_prompt, spots, owners * capacity + ranks)
    requests = (
        jnp.zeros((spots,), jnp.int32)
        .at[places]
        .set(row_ids - owners * vocab_share, mode="drop")
        .reshape(groups, capacity)
    )
    found = jnp.take(
        table, lax.all_to_all(requests, "dp", split_axis=0, concat_axis=0, tiled=True), axis=0
    )
    fetched = lax.all_to_all(found, "dp", split_axis=0, concat_axis=0, tiled=True).reshape(
        spots, width
    )
    text_rows = jnp.take(fetched, jnp.minimum(places, spots - 1), axis=0).astype(jnp.float32)
    prompt_rows = jnp.take(prompt, jnp.minimum(row_ids, prompt_len - 1), axis=0)
    x_start = jnp.where(in_prompt[:, None], prompt_rows, text_rows)
    cot_start = cotangent.astype(jnp.float32)
    seg_full = jnp.concatenate([jnp.full((prompt_len,), -1, jnp.int32), segments[0]])
    limit = prompt_len + valid_rows[0]
    key_pos = jnp.arange(slot_len, dtype=jnp.int32)
    key_ok = key_pos < limit
    row_first = head_index * share

    def spread(values, project):
        return project(lax.all_gather(values, "head", axis=0, tiled=True), jnp.int32(0))

    def collect(part_fn):
        return lax.psum_scatter(
            part_fn(jnp.int32(0), share * lax.axis_size("head")),
            "head",
            scatter_dimension=0,
            tiled=True,
        )

    heads_here = rel_bias.shape[1]
    inner_here = w_qkv.shape[2]
    head_size = inner_here // heads_here
    scale = head_size ** (-0.5)
    bias_table = rel_bias.T
    normed = rms_scale(x_start, attn_gain).astype(jnp.bfloat16)
    mixed = spread(
        normed,
        lambda piece, start: jnp.einsum(
            "rd,dcf->rcf", piece, w_qkv, preferred_element_type=jnp.float32
        ),
    ).astype(jnp.bfloat16)
    query_len = mixed.shape[0]
    queries = mixed[:, 0].reshape(query_len, heads_here, head_size)
    keys = mixed[:, 1].reshape(slot_len, heads_here, head_size)
    values = mixed[:, 2].reshape(slot_len, heads_here, head_size)
    block = min(512, query_len)
    starts = jnp.arange(query_len // block, dtype=jnp.int32) * block

    def scores_of(start):
        q_pos = start + jnp.arange(block, dtype=jnp.int32)
        near = bucket_of(key_pos[None, :] - q_pos[:, None])[None]
        bias = jnp.zeros((heads_here, block, slot_len), jnp.float32)
        for b in range(rel_bias.shape[0]):
            bias = jnp.where(near == b, bias_table[:, b].astype(jnp.float32)[:, None, None], bias)
        allowed = (key_pos < prompt_len)[None, :] | (
            seg_full[:, None] == seg_full[None, :]
        ) & key_ok[None, :]
        raw = (
            jnp.einsum("qhe,khe->hqk", queries, keys, preferred_element_type=jnp.float32) * scale
            + bias
        )
        return (jnp.where(allowed[None], raw, masked_score), queries)

    def forward_block(start):
        scores, q_block = scores_of(start)
        top = jnp.max(scores, axis=-1, keepdims=True)
        expo = jnp.exp(scores - top)
        total = jnp.sum(expo, axis=-1, keepdims=True)
        probs = (expo / total).astype(jnp.bfloat16)
        result = jnp.einsum("hqk,khe->qhe", probs, values, preferred_element_type=jnp.float32)
        return (
            result.reshape(block, inner_here).astype(jnp.bfloat16),
            (top + jnp.log(total))[..., 0],
        )

    out_blocks, lse_blocks = lax.map(forward_block, starts)
    attended = out_blocks.reshape(query_len, inner_here)
    middle = x_start + collect(lambda start, count: rows_dot(attended, w_out))
    normed_ff = rms_scale(middle, ff_gain).astype(jnp.bfloat16)
    hidden = spread(
        normed_ff, lambda piece, start: jnp.dot(piece, w_in, preferred_element_type=jnp.float32)
    )
    active = jax.nn.gelu(hidden).astype(jnp.bfloat16)
    final = middle + collect(lambda start, count: rows_dot(active, w_down))
    live = row_first + jnp.arange(x_start.shape[0], dtype=jnp.int32) < limit
    grad_out = cot_start * live[:, None].astype(jnp.float32)
    d_active = spread(
        grad_out.astype(jnp.bfloat16),
        lambda piece, start: jnp.einsum(
            "rd,fd->rf", piece, w_down, preferred_element_type=jnp.float32
        ),
    )
    d_hidden = jax.vjp(jax.nn.gelu, hidden)[1](d_active)[0].astype(jnp.bfloat16)
    d_normed_ff = collect(
        lambda start, count: jnp.einsum(
            "rf,df->rd", d_hidden, w_in, preferred_element_type=jnp.float32
        )
    )
    d_middle = grad_out + rms_back(middle, ff_gain, d_normed_ff)
    d_attended = spread(
        d_middle.astype(jnp.bfloat16),
        lambda piece, start: jnp.einsum(
            "rd,fd->rf", piece, w_out, preferred_element_type=jnp.float32
        ),
    ).astype(jnp.bfloat16)
    d_heads = d_attended.reshape(query_len, heads_here, head_size)

    def back_block(carry, inputs):
        d_keys, d_values = carry
        start, lse = inputs
        scores, q_block = scores_of(start)
        probs = jnp.exp(scores - lse[..., None])
        d_values = d_values + jnp.einsum(
            "hqk,qhe->khe", probs.astype(jnp.bfloat16), d_heads, preferred_element_type=jnp.float32
        )
        d_probs = jnp.einsum("qhe,khe->hqk", d_heads, values, preferred_element_type=jnp.float32)
        d_scores = (probs * (d_probs - jnp.sum(probs * d_probs, axis=-1, keepdims=True))).astype(
            jnp.bfloat16
        )
        d_query = (
            jnp.einsum("hqk,khe->qhe", d_scores, keys, preferred_element_type=jnp.float32) * scale
        )
        d_keys = (
            d_keys
            + jnp.einsum("hqk,qhe->khe", d_scores, q_block, preferred_element_type=jnp.float32)
            * scale
        )
        return ((d_keys, d_values), d_query.astype(jnp.bfloat16))

    empty = jnp.zeros((slot_len, heads_here, head_size), jnp.float32)
    (d_keys, d_values), d_queries = lax.scan(back_block, (empty, empty), (starts, lse_blocks))
    d_mixed = jnp.stack(
        [
            d_queries.reshape(query_len, inner_here),
            d_keys.reshape(slot_len, inner_here).astype(jnp.bfloat16),
            d_values.reshape(slot_len, inner_here).astype(jnp.bfloat16),
        ],
        axis=1,
    )
    d_normed = collect(
        lambda start, count: jnp.einsum(
            "rcf,dcf->rd", d_mixed, w_qkv, preferred_element_type=jnp.float32
        )
    )
    d_start = d_middle + rms_back(x_start, attn_gain, d_normed)
    order_pick = (prompt_ids[:, None] == jnp.arange(prompt_len, dtype=jnp.int32)[None, :]).astype(
        jnp.float32
    )
    partial_value = jnp.einsum(
        "rcf,dcf->rd", d_mixed[:prompt_len], w_qkv, preferred_element_type=jnp.float32
    )
    x_prompt = jnp.take(prompt, prompt_ids, axis=0)
    residual_part = jnp.where(head_index == 0, d_middle[:prompt_len], 0.0)
    local_grad = jnp.einsum(
        "tr,td->rd",
        order_pick,
        residual_part + rms_back(x_prompt, attn_gain, partial_value),
        precision=exact_mode,
    )
    prompt_grad = lax.psum(local_grad, ("dp", "head"))
    grad_norm = jnp.sqrt(jnp.sum(prompt_grad * prompt_grad))
    clip_at = clip_share * math.sqrt(prompt_len * width * groups)
    clipped = prompt_grad * jnp.minimum(1.0, clip_at / (grad_norm + 1e-06))
    first_out = first_decay * first_moment + (1.0 - first_decay) * clipped
    second_out = second_decay * second_moment + (1.0 - second_decay) * clipped * clipped
    first_hat = first_out / (1.0 - first_decay**STEP)
    second_hat = second_out / (1.0 - second_decay**STEP)
    prompt_new = prompt - learn_rate * (
        first_hat / (jnp.sqrt(second_hat) + adam_epsilon) + weight_decay * prompt
    )
    return (
        final.astype(jnp.bfloat16),
        d_start,
        prompt_grad,
        grad_norm,
        prompt_new,
        first_out,
        second_out,
        prompt_new.astype(jnp.bfloat16),
    )


def solution(mesh):
    in_specs = (
        P("dp", None),
        P("dp", None),
        P("dp"),
        P(),
        P("dp", None),
        P(),
        P(None, None, "head"),
        P(None, "head"),
        P("head", None),
        P(),
        P(None, "head"),
        P("head", None),
        P(("dp", "head"), None),
        P(),
        P(),
    )
    out_specs = (P(("dp", "head"), None), P(("dp", "head"), None), P(), P(), P(), P(), P(), P())
    return jax.shard_map(
        per_device, mesh=mesh, in_specs=in_specs, out_specs=out_specs, check_vma=False
    )
```

```python
import functools
import math

import jax
import jax.numpy as jnp
from jax import lax
from jax.experimental import pallas as pl
from jax.experimental.pallas import tpu as pltpu
from jax.sharding import PartitionSpec as P

STEP = 10
norm_epsilon = 1e-06
thresholds = (12, 16, 23, 32, 46, 64, 91)
masked_score = -1000000000.0
learn_rate = 0.5
first_decay = 0.5
second_decay = 0.75
weight_decay = 0.01
adam_epsilon = 1e-08
clip_share = 0.05
exact_mode = lax.Precision.HIGHEST
MESH = pl.DeviceIdType.MESH
LANES = 128
SEND_ROWS = 8
NT = (((1,), (1,)), ((), ()))
NN = (((1,), (0,)), ((), ()))
TN = (((0,), (0,)), ((), ()))
f32 = jnp.float32
bf16 = jnp.bfloat16
GELU_C = math.sqrt(2.0 / math.pi)


def dot(left, right, dims=NN, precision=None):
    return lax.dot_general(left, right, dims, preferred_element_type=f32, precision=precision)


def rms_scale(rows, gain):
    return rows * lax.rsqrt(jnp.mean(rows * rows, axis=1, keepdims=True) + norm_epsilon) * gain


def rms_back(rows, gain, grad):
    r = lax.rsqrt(jnp.mean(rows * rows, axis=1, keepdims=True) + norm_epsilon)
    scaled = grad * gain
    return r * scaled - rows * (r * r * r * jnp.mean(rows * scaled, axis=1, keepdims=True))


def bucket_of(relative):
    magnitude = jnp.abs(relative)
    larger = 8 + sum(((magnitude >= cutoff).astype(jnp.int32) for cutoff in thresholds))
    return jnp.where(magnitude < 8, magnitude, larger) + 16 * (relative > 0).astype(jnp.int32)


def layer_kernel(
    x0_ref, cot_ref, mask_k_ref, mask_q_ref, bias_ref, order_ref, live_ref, ag_ref, fg_ref,
    wqkv_hbm, wout_hbm, win_hbm, wdown_hbm,
    out_ref, grad_ref, local_ref,
    wqkv, wout, win, wdown, k_all, v_all, kt, vt, qs, bias, probs, att_t, acc_out, acc_dn,
    dk_own, dv_own, dk_send, dv_send, dk_recv, dv_recv, dxb,
    wsem, kv_send, kv_recv, dkv_send, dkv_recv,
):
    dp = lax.axis_index("dp")
    head = lax.axis_index("head")
    other = (dp, 1 - head)
    share, width = x0_ref.shape
    slot = 2 * share
    pairs = width // LANES
    ff = win.shape[1]
    ff_block = 768
    mine = pl.ds(pl.multiple_of(head * share, share), share)
    theirs = pl.ds(pl.multiple_of((1 - head) * share, share), share)

    weight_copies = [
        pltpu.make_async_copy(src, dst, wsem.at[i])
        for i, (src, dst) in enumerate(
            ((wqkv_hbm, wqkv), (wout_hbm, wout), (win_hbm, win), (wdown_hbm, wdown))
        )
    ]
    for copy in weight_copies:
        copy.start()

    barrier = pltpu.get_barrier_semaphore()
    pl.semaphore_signal(barrier, inc=1, device_id=other, device_id_type=MESH)

    for h in range(2 * pairs):
        for d in range(5):
            base = jnp.broadcast_to(bias_ref[h, d : d + 1, :], (LANES, 2 * LANES))
            turned = pltpu.roll(base, 0, 1, stride=1, stride_axis=0)
            bias[h, d] = turned[:, :LANES]

    n1 = rms_scale(x0_ref[...], ag_ref[...]).astype(bf16)
    weight_copies[0].wait()
    k_all[mine, :] = dot(n1, wqkv[1]).astype(bf16)
    pl.semaphore_wait(barrier, 1)
    k_copy = pltpu.make_async_remote_copy(
        k_all.at[mine, :], k_all.at[mine, :], kv_send.at[0], kv_recv.at[0],
        device_id=other, device_id_type=MESH,
    )
    k_copy.start()
    v_all[mine, :] = dot(n1, wqkv[2]).astype(bf16)
    v_copy = pltpu.make_async_remote_copy(
        v_all.at[mine, :], v_all.at[mine, :], kv_send.at[1], kv_recv.at[1],
        device_id=other, device_id_type=MESH,
    )
    v_copy.start()
    q = dot(n1, wqkv[0]).astype(bf16) * jnp.asarray(0.125, bf16)
    lane = lax.broadcasted_iota(jnp.int32, (share, LANES), 1)
    for p in range(pairs):
        part = q[:, p * LANES : (p + 1) * LANES]
        qs[p, :share, :] = jnp.where(lane < LANES // 2, part, jnp.zeros_like(part))
        qs[p, share:, :] = jnp.where(lane >= LANES // 2, part, jnp.zeros_like(part))
    kt[head] = k_all[mine, :].T
    vt[head] = v_all[mine, :].T
    k_copy.wait()
    kt[1 - head] = k_all[theirs, :].T
    v_copy.wait()
    vt[1 - head] = v_all[theirs, :].T

    def forward(p, carry):
        cols = pl.ds(pl.multiple_of(p * LANES, LANES), LANES)
        left = jnp.concatenate([k_all[:, cols], mask_k_ref[...]], axis=1)
        mask_q = mask_q_ref[...]
        right = jnp.concatenate([qs[p], jnp.concatenate([mask_q, mask_q], axis=0)], axis=1)
        raw = dot(left, right, NT)
        rows = []
        for kb in range(slot // LANES):
            blocks = []
            for a in range(2):
                for qb in range(share // LANES):
                    apart = kb - (head * (share // LANES) + qb)
                    place = jnp.clip(apart, -2, 2) + 2
                    lo = a * share + qb * LANES
                    blocks.append(
                        raw[kb * LANES : (kb + 1) * LANES, lo : lo + LANES] + bias[2 * p + a, place]
                    )
            rows.append(jnp.concatenate(blocks, axis=1))
        scores = jnp.concatenate(rows, axis=0)
        expo = jnp.exp(scores - jnp.max(scores, axis=0, keepdims=True))
        prob = expo * (1.0 / jnp.sum(expo, axis=0, keepdims=True))
        probs[p] = prob
        low = prob.astype(bf16)
        half = LANES // 2
        for a in range(2):
            side = low[:, a * share : (a + 1) * share]
            feat = pl.ds(pl.multiple_of(p * LANES + a * half, half), half)
            att_t[feat, :] = (
                dot(vt[0, feat, :], side[:share]) + dot(vt[1, feat, :], side[share:])
            ).astype(bf16)
        return carry

    lax.fori_loop(0, pairs, forward, 0)
    weight_copies[1].wait()
    attended = att_t[...].T
    x1 = x0_ref[...] + dot(attended, wout[...])
    n2 = rms_scale(x1, fg_ref[...]).astype(bf16)
    dy = cot_ref[...] * live_ref[:, :1].astype(bf16)
    weight_copies[2].wait()
    weight_copies[3].wait()
    acc_out[...] = x1
    acc_dn[...] = jnp.zeros_like(acc_dn)

    def feed(i, carry):
        at = pl.ds(pl.multiple_of(i * ff_block, ff_block), ff_block)
        u = dot(n2, win[:, at])
        d_active = dot(dy, wdown[at, :], NT)
        square = u * u
        t = jnp.tanh(GELU_C * (u + 0.044715 * (u * square)))
        active = (0.5 * u * (1.0 + t)).astype(bf16)
        slope = 0.5 * (1.0 + t) + 0.5 * u * (1.0 - t * t) * (
            GELU_C * (1.0 + 3 * 0.044715 * square)
        )
        d_hidden = (d_active * slope).astype(bf16)
        acc_out[...] += dot(active, wdown[at, :])
        acc_dn[...] += dot(d_hidden, win[:, at], NT)
        return carry

    lax.fori_loop(0, ff // ff_block, feed, 0)
    out_ref[...] = acc_out[...].astype(bf16)
    dx1 = dy.astype(f32) + rms_back(x1, fg_ref[...], acc_dn[...])
    grad_ref[...] = dx1
    d_att = dot(dx1.astype(bf16), wout[...], NT).astype(bf16)
    for p in range(pairs):
        part = d_att[:, p * LANES : (p + 1) * LANES]
        dxb[p, :share, :] = jnp.where(lane < LANES // 2, part, jnp.zeros_like(part))
        dxb[p, share:, :] = jnp.where(lane >= LANES // 2, part, jnp.zeros_like(part))

    def send_of(p):
        return [
            pltpu.make_async_remote_copy(
                src.at[p], dst.at[p], dkv_send.at[i, p], dkv_recv.at[i, p],
                device_id=other, device_id_type=MESH,
            )
            for i, (src, dst) in enumerate(((dk_send, dk_recv), (dv_send, dv_recv)))
        ]

    def backward(p, carry):
        cols = pl.ds(pl.multiple_of(p * LANES, LANES), LANES)
        d_out = dxb[p]
        d_prob = dot(v_all[:, cols], d_out, NT)
        prob = probs[p]
        delta = jnp.sum(prob * d_prob, axis=0, keepdims=True)
        d_score = (prob * (d_prob - delta)).astype(bf16)
        low = prob.astype(bf16)
        half = LANES // 2
        for a in range(2):
            side = d_score[:, a * share : (a + 1) * share]
            feat = pl.ds(pl.multiple_of(p * LANES + a * half, half), half)
            att_t[feat, :] = (
                (dot(kt[0, feat, :], side[:share]) + dot(kt[1, feat, :], side[share:])) * 0.125
            ).astype(bf16)
        d_v = dot(low, d_out)
        d_k = dot(d_score, qs[p])
        first = head == 0
        dv_own[p] = jnp.where(first, d_v[:share], d_v[share:])
        dk_own[p] = jnp.where(first, d_k[:share], d_k[share:])
        dv_send[p] = jnp.where(first, d_v[share:], d_v[:share])
        dk_send[p] = jnp.where(first, d_k[share:], d_k[:share])
        for copy in send_of(p):
            copy.start()
        return carry

    lax.fori_loop(0, pairs, backward, 0)
    acc_dn[...] = dot(att_t[...].T, wqkv[0], NT)
    for p in range(pairs):
        for copy in send_of(p):
            copy.wait()
    d_k = jnp.concatenate([(dk_own[p] + dk_recv[p]).astype(bf16) for p in range(pairs)], axis=1)
    d_v = jnp.concatenate([(dv_own[p] + dv_recv[p]).astype(bf16) for p in range(pairs)], axis=1)
    d_n1 = acc_dn[...] + dot(d_k, wqkv[1], NT) + dot(d_v, wqkv[2], NT)
    total = grad_ref[...] + rms_back(x0_ref[...], ag_ref[...], d_n1)
    grad_ref[...] = total

    @pl.when(head == 0)
    def _():
        local_ref[...] = dot(order_ref[...], total[:LANES], TN, exact_mode)

    @pl.when(head != 0)
    def _():
        local_ref[...] = jnp.zeros_like(local_ref)


def vmem(*shape, dtype=f32):
    return pltpu.VMEM(shape, dtype)


def run_layer(x0, cot, mask_k, mask_q, bias, order, live, ag, fg, wqkv, wout, win, wdown):
    share, width = x0.shape
    ff = win.shape[1]
    pairs = width // LANES
    in_vmem = pl.BlockSpec(memory_space=pltpu.VMEM)
    in_hbm = pl.BlockSpec(memory_space=pl.ANY)
    return pl.pallas_call(
        layer_kernel,
        out_shape=(
            jax.ShapeDtypeStruct((share, width), bf16),
            jax.ShapeDtypeStruct((share, width), f32),
            jax.ShapeDtypeStruct((LANES, width), f32),
        ),
        in_specs=[in_vmem] * 9 + [in_hbm] * 4,
        out_specs=[in_vmem] * 3,
        scratch_shapes=[
            vmem(3, width, width, dtype=bf16),
            vmem(width, width, dtype=bf16),
            vmem(width, ff, dtype=bf16),
            vmem(ff, width, dtype=bf16),
            vmem(2 * share, width, dtype=bf16),
            vmem(2 * share, width, dtype=bf16),
            vmem(2, width, share, dtype=bf16),
            vmem(2, width, share, dtype=bf16),
            vmem(pairs, 2 * share, LANES, dtype=bf16),
            vmem(2 * pairs, 5, LANES, LANES),
            vmem(pairs, 2 * share, 2 * share),
            vmem(width, share, dtype=bf16),
            vmem(share, width),
            vmem(share, width),
        ]
        + [vmem(pairs, share, LANES)] * 6
        + [
            vmem(pairs, 2 * share, LANES, dtype=bf16),
            pltpu.SemaphoreType.DMA((4,)),
            pltpu.SemaphoreType.DMA((2,)),
            pltpu.SemaphoreType.DMA((2,)),
            pltpu.SemaphoreType.DMA((2, pairs)),
            pltpu.SemaphoreType.DMA((2, pairs)),
        ],
        compiler_params=pltpu.CompilerParams(
            collective_id=1, has_side_effects=True, vmem_limit_bytes=60 * 2**20
        ),
        name="layer",
    )(x0, cot, mask_k, mask_q, bias, order, live, ag, fg, wqkv, wout, win, wdown)


def update_kernel(
    inner, outer, clip_at,
    local_ref, prompt_ref, first_ref, second_ref,
    grad_ref, norm_ref, new_ref, first_out_ref, second_out_ref, low_ref,
    parts, group, total, send1, recv1, send2, recv2, send3, recv3, send4, recv4,
):
    dp = lax.axis_index("dp")
    head = lax.axis_index("head")
    rows = prompt_ref.shape[0]
    chunk = total.shape[0] // inner
    chunks = -(-rows // chunk)
    my_in = lax.rem(dp, inner)
    my_out = dp // inner
    barrier = pltpu.get_barrier_semaphore()

    def in_peer(k):
        return my_out * inner + lax.rem(my_in + k, inner)

    def out_peer(k):
        return lax.rem(my_out + k, outer) * inner + my_in

    def greet(device):
        pl.semaphore_signal(barrier, inc=1, device_id=device, device_id_type=MESH)

    greet((dp, 1 - head))

    def piece(index):
        return pl.ds(pl.multiple_of(index * chunk, chunk), chunk)

    def forward_of(index):
        return pltpu.make_async_remote_copy(
            total.at[piece(index), :], total.at[piece(index), :], send4.at[index], recv4.at[index],
            device_id=(dp, 1), device_id_type=MESH,
        )

    @pl.when(head == 0)
    def _():
        for k in range(1, inner):
            greet((in_peer(k), head))
        for k in range(1, outer):
            greet((out_peer(k), head))
        pl.semaphore_wait(barrier, inner + outer - 1)

        def scatter_to(k):
            target = lax.rem(my_in + k, inner)
            return target, pltpu.make_async_remote_copy(
                local_ref.at[piece(target), :], parts.at[my_in], send1.at[k], recv1.at[my_in],
                device_id=(in_peer(k), head), device_id_type=MESH,
            )

        def scatter_from(k):
            source = lax.rem(my_in + k, inner)
            return source, pltpu.make_async_remote_copy(
                local_ref.at[piece(source), :], parts.at[source], send1.at[k], recv1.at[source],
                device_id=(in_peer(k), head), device_id_type=MESH,
            )

        def gather_to(k):
            return pltpu.make_async_remote_copy(
                total.at[piece(my_in), :], total.at[piece(my_in), :], send2.at[k], recv2.at[my_in],
                device_id=(in_peer(k), head), device_id_type=MESH,
            )

        def gather_from(k):
            source = lax.rem(my_in + k, inner)
            return source, pltpu.make_async_remote_copy(
                total.at[piece(source), :], total.at[piece(source), :], send2.at[k],
                recv2.at[source], device_id=(in_peer(k), head), device_id_type=MESH,
            )

        def across(k):
            return pltpu.make_async_remote_copy(
                group.at[my_out], group.at[my_out], send3.at[k], recv3.at[my_out],
                device_id=(out_peer(k), head), device_id_type=MESH,
            )

        def across_from(k):
            source = lax.rem(my_out + k, outer)
            return pltpu.make_async_remote_copy(
                group.at[source], group.at[source], send3.at[k], recv3.at[source],
                device_id=(out_peer(k), head), device_id_type=MESH,
            )

        for k in range(1, inner):
            target, copy = scatter_to(k)

            @pl.when(target < chunks)
            def _():
                copy.start()

        @pl.when(my_in < chunks)
        def _():
            parts[my_in] = local_ref[piece(my_in), :]
            for k in range(1, inner):
                scatter_from(k)[1].wait_recv()
            summed = parts[0]
            for source in range(1, inner):
                summed = summed + parts[source]
            if outer > 1:
                group[my_out] = summed
                for k in range(1, outer):
                    across(k).start()
                for k in range(1, outer):
                    across_from(k).wait_recv()
                summed = group[0]
                for source in range(1, outer):
                    summed = summed + group[source]
                for k in range(1, outer):
                    across(k).wait_send()
            total[piece(my_in), :] = summed
            for k in range(1, inner):
                gather_to(k).start()
            forward_of(my_in).start()

        for k in range(1, inner):
            source, copy = gather_from(k)

            @pl.when(source < chunks)
            def _():
                copy.wait_recv()
                forward_of(source).start()

        for k in range(1, inner):
            target, copy = scatter_to(k)

            @pl.when(target < chunks)
            def _():
                copy.wait_send()

        @pl.when(my_in < chunks)
        def _():
            for k in range(1, inner):
                gather_to(k).wait_send()

    @pl.when(head == 1)
    def _():
        pl.semaphore_wait(barrier, 1)
        for index in range(chunks):
            forward_of(index).wait_recv()

    summed = total[:rows, :]
    grad_ref[...] = summed
    norm = jnp.sqrt(jnp.sum(summed * summed, keepdims=True))
    norm_ref[...] = norm
    clipped = summed * jnp.minimum(1.0, clip_at / (norm + 1e-06))
    first_out = first_decay * first_ref[...] + (1.0 - first_decay) * clipped
    second_out = second_decay * second_ref[...] + (1.0 - second_decay) * clipped * clipped
    first_hat = first_out / (1.0 - first_decay**STEP)
    second_hat = second_out / (1.0 - second_decay**STEP)
    prompt = prompt_ref[...]
    new = prompt - learn_rate * (
        first_hat / (jnp.sqrt(second_hat) + adam_epsilon) + weight_decay * prompt
    )
    first_out_ref[...] = first_out
    second_out_ref[...] = second_out
    new_ref[...] = new
    low_ref[...] = new.astype(bf16)

    @pl.when(head == 0)
    def _():
        for index in range(chunks):
            forward_of(index).wait_send()


def run_update(local, prompt, first, second, groups):
    inner = math.gcd(groups, 16)
    outer = groups // inner
    rows, width = prompt.shape
    padded = local.shape[0]
    chunk = padded // inner
    clip_at = clip_share * math.sqrt(rows * width * groups)
    shape = jax.ShapeDtypeStruct((rows, width), f32)
    spec = pl.BlockSpec(memory_space=pltpu.VMEM)
    return pl.pallas_call(
        functools.partial(update_kernel, inner, outer, clip_at),
        out_shape=(
            shape,
            jax.ShapeDtypeStruct((1, 1), f32),
            shape,
            shape,
            shape,
            jax.ShapeDtypeStruct((rows, width), bf16),
        ),
        in_specs=[spec] * 4,
        out_specs=[spec] * 6,
        scratch_shapes=[
            vmem(inner, chunk, width),
            vmem(outer, chunk, width),
            vmem(padded, width),
            pltpu.SemaphoreType.DMA((inner,)),
            pltpu.SemaphoreType.DMA((inner,)),
            pltpu.SemaphoreType.DMA((inner,)),
            pltpu.SemaphoreType.DMA((inner,)),
            pltpu.SemaphoreType.DMA((outer,)),
            pltpu.SemaphoreType.DMA((outer,)),
            pltpu.SemaphoreType.DMA((inner,)),
            pltpu.SemaphoreType.DMA((inner,)),
        ],
        compiler_params=pltpu.CompilerParams(
            collective_id=2, has_side_effects=True, vmem_limit_bytes=32 * 2**20
        ),
        name="update",
    )(local, prompt, first, second)


def per_device(
    ids,
    segments,
    valid_rows,
    prompt,
    table,
    attn_gain,
    w_qkv,
    rel_bias,
    w_out,
    ff_gain,
    w_in,
    w_down,
    cotangent,
    first_moment,
    second_moment,
):
    heads_count = lax.axis_size("head")
    head_index = lax.axis_index("head")
    groups = lax.axis_size("dp")
    slot_len = ids.shape[1]
    share = slot_len // heads_count
    prompt_len = prompt.shape[0]
    width = prompt.shape[1]
    vocab_share = table.shape[0]
    capacity = max(2, 2 * slot_len // (heads_count * groups))
    spots = groups * capacity
    positions = head_index * share + jnp.arange(share, dtype=jnp.int32)
    row_ids = lax.dynamic_slice_in_dim(ids[0], head_index * share, share, 0)
    prompt_ids = ids[0, :prompt_len]
    in_prompt = positions < prompt_len
    owners = jnp.where(in_prompt, groups, row_ids // vocab_share)
    onehot = (owners[:, None] == jnp.arange(groups, dtype=jnp.int32)[None, :]).astype(jnp.int32)
    ranks = jnp.sum(jnp.cumsum(onehot, axis=0) * onehot, axis=1) - 1
    places = jnp.where(in_prompt, spots, owners * capacity + ranks)
    requests = (
        jnp.zeros((spots,), jnp.int32)
        .at[places]
        .set(row_ids - owners * vocab_share, mode="drop")
        .reshape(groups, capacity)
    )
    found = jnp.take(
        table, lax.all_to_all(requests, "dp", split_axis=0, concat_axis=0, tiled=True), axis=0
    )
    fetched = lax.all_to_all(found, "dp", split_axis=0, concat_axis=0, tiled=True).reshape(
        spots, width
    )
    text_rows = jnp.take(fetched, jnp.minimum(places, spots - 1), axis=0).astype(jnp.float32)
    prompt_rows = jnp.take(prompt, jnp.minimum(row_ids, prompt_len - 1), axis=0)
    x_start = jnp.where(in_prompt[:, None], prompt_rows, text_rows)

    seg_full = jnp.concatenate([jnp.full((prompt_len,), -1, jnp.int32), segments[0]])
    limit = prompt_len + valid_rows[0]
    key_pos = jnp.arange(slot_len, dtype=jnp.int32)
    feature = jnp.arange(LANES, dtype=jnp.int32)[None, :] - 1
    allowed = (key_pos < prompt_len)[:, None] | (
        (seg_full[:, None] == feature) & (key_pos < limit)[:, None]
    )
    mask_k = jnp.where(allowed, 0.0, masked_score).astype(bf16)
    seg_here = lax.dynamic_slice_in_dim(seg_full, head_index * share, share, 0)
    mask_q = (seg_here[:, None] == feature).astype(bf16)
    live = jnp.broadcast_to((positions < limit)[:, None], (share, LANES)).astype(f32)
    full_bias = lax.all_gather(rel_bias.T, "head", axis=0, tiled=True).astype(f32)
    lag = (jnp.arange(2 * LANES, dtype=jnp.int32) + LANES) % (2 * LANES) - LANES
    apart = (jnp.arange(5, dtype=jnp.int32) - 2)[:, None] * LANES - lag[None, :]
    near = bucket_of(apart)
    near = jnp.where((jnp.arange(5) == 0)[:, None], 15, near)
    near = jnp.where((jnp.arange(5) == 4)[:, None], 31, near)
    pick = (near[:, :, None] == jnp.arange(rel_bias.shape[0])).astype(f32)
    bias_rows = jnp.einsum("djb,hb->hdj", pick, full_bias, precision=exact_mode)
    text = jnp.arange(LANES, dtype=jnp.int32)
    order = (
        (ids[0, :LANES][:, None] == text[None, :]) & (text < prompt_len)[:, None]
    ).astype(f32)

    full_qkv = lax.all_gather(jnp.transpose(w_qkv, (1, 0, 2)), "head", axis=2, tiled=True)
    full_out = lax.all_gather(w_out, "head", axis=0, tiled=True)
    full_in = lax.all_gather(w_in, "head", axis=1, tiled=True)
    full_down = lax.all_gather(w_down, "head", axis=0, tiled=True)

    final, d_start, local_grad = run_layer(
        x_start, cotangent, mask_k, mask_q, bias_rows, order, live,
        attn_gain.reshape(1, width), ff_gain.reshape(1, width),
        full_qkv, full_out, full_in, full_down,
    )
    prompt_grad, grad_norm, prompt_new, first_out, second_out, prompt_low = run_update(
        local_grad, prompt, first_moment, second_moment, groups
    )
    return (
        final,
        d_start,
        prompt_grad,
        grad_norm[0, 0],
        prompt_new,
        first_out,
        second_out,
        prompt_low,
    )


def solution(mesh):
    in_specs = (
        P("dp", None),
        P("dp", None),
        P("dp"),
        P(),
        P("dp", None),
        P(),
        P(None, None, "head"),
        P(None, "head"),
        P("head", None),
        P(),
        P(None, "head"),
        P("head", None),
        P(("dp", "head"), None),
        P(),
        P(),
    )
    out_specs = (P(("dp", "head"), None), P(("dp", "head"), None), P(), P(), P(), P(), P(), P())
    return jax.shard_map(
        per_device, mesh=mesh, in_specs=in_specs, out_specs=out_specs, check_vma=False
    )
```

```python
import functools
import math

import jax
import jax.numpy as jnp
from jax import lax
from jax.experimental import pallas as pl
from jax.experimental.pallas import tpu as pltpu
from jax.sharding import PartitionSpec as P

STEP = 10
norm_epsilon = 1e-06
thresholds = (12, 16, 23, 32, 46, 64, 91)
masked_score = -1000000000.0
learn_rate = 0.5
first_decay = 0.5
second_decay = 0.75
weight_decay = 0.01
adam_epsilon = 1e-08
clip_share = 0.05
exact_mode = lax.Precision.HIGHEST
MESH = pl.DeviceIdType.MESH
LANES = 128
NT = (((1,), (1,)), ((), ()))
NN = (((1,), (0,)), ((), ()))
TN = (((0,), (0,)), ((), ()))
f32 = jnp.float32
bf16 = jnp.bfloat16
GELU_C = math.sqrt(2.0 / math.pi)


def dot(left, right, dims=NN, precision=None):
    return lax.dot_general(left, right, dims, preferred_element_type=f32, precision=precision)


def rms_scale(rows, gain):
    return rows * lax.rsqrt(jnp.mean(rows * rows, axis=1, keepdims=True) + norm_epsilon) * gain


def rms_back(rows, gain, grad):
    r = lax.rsqrt(jnp.mean(rows * rows, axis=1, keepdims=True) + norm_epsilon)
    scaled = grad * gain
    return r * scaled - rows * (r * r * r * jnp.mean(rows * scaled, axis=1, keepdims=True))


def bucket_of(relative):
    magnitude = jnp.abs(relative)
    larger = 8 + sum(((magnitude >= cutoff).astype(jnp.int32) for cutoff in thresholds))
    return jnp.where(magnitude < 8, magnitude, larger) + 16 * (relative > 0).astype(jnp.int32)


def each(count, body):
    if count <= 16:
        for i in range(count):
            body(i)
    else:
        lax.fori_loop(0, count, lambda i, carry: (body(i), carry)[1], 0)


def layer_kernel(
    groups, inner, block, rows,
    ids_ref, seg_ref, valid_ref, prompt_ref, ag_ref, fg_ref, rel_ref, cot_ref,
    table_hbm, wqkv_hbm, wout_hbm, win_hbm, wdown_hbm,
    out_hbm, grad_hbm, total_hbm,
    table, wqkv, wout, win, wdown,
    req_out, req_in, found, fetched, rel_all, prompt_pad, seg_pad, mask_k, mask_q,
    x0, x0_prompt, d_act, out_buf, grad_buf,
    k_all, v_all, kt, vt, qs, bias, probs, att_t, acc_out, acc_dn,
    dk_own, dv_own, dk_send, dv_send, dk_recv, dv_recv, dxb,
    rs_send, parts, across_buf, total,
    load_sem, far_send, far_recv, req_send, req_recv, row_send, row_recv,
    kv_send, kv_recv, dkv_send, dkv_recv,
    send1, recv1, send2, recv2, send3, recv3, send4, recv4, out_sem,
):
    dp = lax.axis_index("dp")
    head = lax.axis_index("head")
    other = (dp, 1 - head)
    share, width = x0.shape
    slot = 2 * share
    pairs = width // LANES
    half_width = width // 2
    ff = win.shape[1]
    half_ff = ff // 2
    ff_block = d_act.shape[2]
    vocab = table.shape[0]
    spots = groups * block
    outer = groups // inner
    my_in = lax.rem(dp, inner)
    my_out = dp // inner
    mine = pl.ds(pl.multiple_of(head * share, share), share)
    theirs = pl.ds(pl.multiple_of((1 - head) * share, share), share)

    def remote(src, dst, send, recv, device):
        return pltpu.make_async_remote_copy(
            src, dst, send, recv, device_id=device, device_id_type=MESH
        )

    my_cols = pl.ds(pl.multiple_of(head * half_width, half_width), half_width)
    my_ff = pl.ds(pl.multiple_of(head * half_ff, half_ff), half_ff)
    weight_pairs = (
        (wdown_hbm, wdown.at[my_ff, :]),
        (wqkv_hbm, wqkv.at[:, :, my_cols]),
        (wout_hbm, wout.at[my_cols, :]),
        (win_hbm, win.at[:, my_ff]),
    )
    table_copy = pltpu.make_async_copy(table_hbm, table, load_sem.at[4])
    table_copy.start()
    local_copies = [
        pltpu.make_async_copy(src, dst, load_sem.at[i]) for i, (src, dst) in enumerate(weight_pairs)
    ]
    for copy in local_copies:
        copy.start()
    far_copies = [
        remote(src, dst, far_send.at[i], far_recv.at[i], other)
        for i, (src, dst) in enumerate(weight_pairs)
    ]

    barrier = pltpu.get_barrier_semaphore()

    def greet(k):
        pl.semaphore_signal(
            barrier, inc=1, device_id=(lax.rem(dp + 1 + k, groups), head), device_id_type=MESH
        )

    pl.semaphore_signal(barrier, inc=1, device_id=other, device_id_type=MESH)
    each(groups - 1, greet)

    lane = lax.broadcasted_iota(jnp.int32, (share, LANES), 1)
    row = lax.broadcasted_iota(jnp.int32, (share, LANES), 0) + head * share
    lane_f = lane.astype(f32)
    row_ids = ids_ref[:, mine].astype(f32)
    ids_col = jnp.concatenate(
        [
            jnp.broadcast_to(row_ids[:, i * LANES : (i + 1) * LANES], (LANES, LANES)).T
            for i in range(share // LANES)
        ],
        axis=0,
    )
    is_text = row >= rows
    owner = jnp.where(is_text, jnp.floor((ids_col + 0.5) * (1.0 / vocab)), -1.0)
    hot = (owner == lane_f).astype(f32)
    tri_row = lax.broadcasted_iota(jnp.int32, (share, share), 0)
    tri_col = lax.broadcasted_iota(jnp.int32, (share, share), 1)
    earlier = (tri_row > tri_col).astype(f32).astype(bf16)
    rank = jnp.sum(dot(earlier, hot.astype(bf16)) * hot, axis=1, keepdims=True)
    place = jnp.where(is_text[:, :1], owner[:, :1] * block + rank, -1.0)
    ranked = (rank == lane_f).astype(f32)
    wanted = dot(hot * (ids_col - owner * vocab), ranked, TN, exact_mode)
    for o in range(groups):
        req_out[o] = wanted[o : o + 1, :]

    order = jnp.where(is_text[:LANES], 0.0, (ids_col[:LANES] == lane_f[:LANES]).astype(f32))

    rel_all[head] = jnp.zeros((8, LANES), f32)
    rel_all[head, : rel_ref.shape[0], : rel_ref.shape[1]] = rel_ref[...].astype(f32)

    seg_pad[:, : seg_ref.shape[1]] = seg_ref[...]
    lanes_slot = lax.broadcasted_iota(jnp.int32, (1, slot), 1)
    seg_row = jnp.where(lanes_slot < rows, -1, pltpu.roll(seg_pad[...], rows, 1)).astype(f32)
    limit = valid_ref[0] + rows
    square_lane = lax.broadcasted_iota(jnp.int32, (LANES, LANES), 1).astype(f32) - 1.0
    square_row = lax.broadcasted_iota(jnp.int32, (LANES, LANES), 0)
    for kb in range(slot // LANES):
        at = kb * LANES
        seg_col = jnp.broadcast_to(seg_row[:, at : at + LANES], (LANES, LANES)).T
        same = seg_col == square_lane
        key = square_row + at
        allowed = (key < rows) | (same & (key < limit))
        mask_k[at : at + LANES, :] = jnp.where(allowed, 0.0, masked_score).astype(bf16)

        @pl.when(head == at // share)
        def _():
            mask_q[at % share : at % share + LANES, :] = same.astype(f32).astype(bf16)

    live = row[:, :1] < limit
    dy = jnp.where(live, cot_ref[...].astype(f32), 0.0).astype(bf16)

    pl.semaphore_wait(barrier, groups)
    req_in[dp] = req_out[dp]

    def request_to(k):
        peer = lax.rem(dp + 1 + k, groups)
        return remote(
            req_out.at[peer], req_in.at[dp], req_send.at[peer], req_recv.at[dp], (peer, head)
        )

    def request_from(k):
        peer = lax.rem(dp + 1 + k, groups)
        return remote(
            req_out.at[peer], req_in.at[peer], req_send.at[peer], req_recv.at[peer], (peer, head)
        )

    each(groups - 1, lambda k: request_to(k).start())
    rel_copy = remote(
        rel_all.at[head], rel_all.at[head], far_send.at[4], far_recv.at[4], other
    )
    rel_copy.start()
    for copy in far_copies:
        copy.start()

    local_copies[0].wait()

    def activation_grad(index):
        at = pl.ds(pl.multiple_of(index * ff_block, ff_block), ff_block)
        d_act[index] = dot(dy, wdown[at, :], NT)

    half_blocks = half_ff // ff_block
    for i in range(half_blocks):
        activation_grad(head * half_blocks + i)

    table_copy.wait()
    each(groups - 1, lambda k: request_from(k).wait_recv())
    vocab_lane = lax.broadcasted_iota(jnp.int32, (block, vocab), 1).astype(f32)
    bunch = 8

    def row_to(peer):
        return remote(
            found.at[peer], fetched.at[dp], row_send.at[peer], row_recv.at[dp], (peer, head)
        )

    def row_from(peer):
        return remote(
            found.at[peer], fetched.at[peer], row_send.at[peer], row_recv.at[peer], (peer, head)
        )

    def serve(g):
        base = lax.rem(dp // bunch + 1 + g, groups // bunch) * bunch
        wants = jnp.concatenate(
            [req_in[base + j] for j in range(bunch)] + [jnp.zeros((LANES - bunch, LANES), f32)],
            axis=0,
        ).T
        picks = jnp.concatenate(
            [
                (wants[:block, j : j + 1] == vocab_lane).astype(f32).astype(bf16)
                for j in range(bunch)
            ],
            axis=0,
        )
        picked = dot(picks, table[...]).astype(bf16)
        for j in range(bunch):
            found[base + j] = picked[j * block : (j + 1) * block]

            @pl.when(base + j != dp)
            def _():
                row_to(base + j).start()

    each(groups // bunch, serve)
    fetched[dp] = found[dp]

    @pl.when(head == 0)
    def _():
        prompt_pad[...] = jnp.zeros_like(prompt_pad)
        prompt_pad[:rows, :] = prompt_ref[...]
        x0_prompt[...] = dot(order, prompt_pad[...], NN, exact_mode)

    rel_copy.wait()
    spread = lax.broadcasted_iota(jnp.int32, (1, 2 * LANES), 1)
    lag = jnp.where(spread >= LANES, spread - 2 * LANES, spread)
    bucket_row = lax.broadcasted_iota(jnp.int32, (LANES, 2 * LANES), 0)
    for d in range(5):
        if d == 0:
            near = jnp.full((1, 2 * LANES), 15, jnp.int32)
        elif d == 4:
            near = jnp.full((1, 2 * LANES), 31, jnp.int32)
        else:
            near = bucket_of((d - 2) * LANES - lag)
        pick = (bucket_row == near).astype(f32).astype(bf16)
        for side in range(2):
            lines = dot(rel_all[side].astype(bf16), pick)
            for h in range(pairs):
                line = jnp.broadcast_to(lines[h : h + 1, :], (LANES, 2 * LANES))
                if d not in (0, 4):
                    line = pltpu.roll(line, 0, 1, stride=1, stride_axis=0)
                bias[side * pairs + h, d] = line[:, :LANES]

    far_copies[0].wait()
    for i in range(half_blocks):
        activation_grad((1 - head) * half_blocks + i)
    for copy in local_copies[1:]:
        copy.wait()
    far_copies[1].wait()

    for peer in range(groups) if groups <= 16 else ():

        @pl.when(peer != dp)
        def _():
            row_from(peer).wait_recv()

    if groups > 16:
        each(groups - 1, lambda k: row_from(lax.rem(dp + 1 + k, groups)).wait_recv())
    spot_lane = lax.broadcasted_iota(jnp.int32, (share, spots), 1).astype(f32)
    take = (place == spot_lane).astype(f32).astype(bf16)
    x0[...] = dot(take, fetched[...].reshape(spots, width))

    @pl.when(head == 0)
    def _():
        x0[:LANES, :] = x0[:LANES, :] + x0_prompt[...]

    attn_gain = ag_ref[...].reshape(1, width)
    ff_gain = fg_ref[...].reshape(1, width)
    n1 = rms_scale(x0[...], attn_gain).astype(bf16)
    k_all[mine, :] = dot(n1, wqkv[1]).astype(bf16)
    k_copy = remote(
        k_all.at[mine, :], k_all.at[mine, :], kv_send.at[0], kv_recv.at[0], other
    )
    k_copy.start()
    v_all[mine, :] = dot(n1, wqkv[2]).astype(bf16)
    v_copy = remote(
        v_all.at[mine, :], v_all.at[mine, :], kv_send.at[1], kv_recv.at[1], other
    )
    v_copy.start()
    q = dot(n1, wqkv[0]).astype(bf16) * jnp.asarray(0.125, bf16)
    for p in range(pairs):
        part = q[:, p * LANES : (p + 1) * LANES]
        qs[p, :share, :] = jnp.where(lane < LANES // 2, part, jnp.zeros_like(part))
        qs[p, share:, :] = jnp.where(lane >= LANES // 2, part, jnp.zeros_like(part))
    kt[head] = k_all[mine, :].T
    vt[head] = v_all[mine, :].T
    k_copy.wait()
    kt[1 - head] = k_all[theirs, :].T
    v_copy.wait()
    vt[1 - head] = v_all[theirs, :].T

    def forward(p, carry):
        cols = pl.ds(pl.multiple_of(p * LANES, LANES), LANES)
        left = jnp.concatenate([k_all[:, cols], mask_k[...]], axis=1)
        right = jnp.concatenate(
            [qs[p], jnp.concatenate([mask_q[...], mask_q[...]], axis=0)], axis=1
        )
        raw = dot(left, right, NT)
        bands = []
        for kb in range(slot // LANES):
            blocks = []
            for a in range(2):
                for qb in range(share // LANES):
                    apart = kb - (head * (share // LANES) + qb)
                    spot = jnp.clip(apart, -2, 2) + 2
                    lo = a * share + qb * LANES
                    blocks.append(
                        raw[kb * LANES : (kb + 1) * LANES, lo : lo + LANES] + bias[2 * p + a, spot]
                    )
            bands.append(jnp.concatenate(blocks, axis=1))
        scores = jnp.concatenate(bands, axis=0)
        expo = jnp.exp(scores - jnp.max(scores, axis=0, keepdims=True))
        prob = expo * (1.0 / jnp.sum(expo, axis=0, keepdims=True))
        probs[p] = prob
        low = prob.astype(bf16)
        half = LANES // 2
        for a in range(2):
            side = low[:, a * share : (a + 1) * share]
            feat = pl.ds(pl.multiple_of(p * LANES + a * half, half), half)
            att_t[feat, :] = (
                dot(vt[0, feat, :], side[:share]) + dot(vt[1, feat, :], side[share:])
            ).astype(bf16)
        return carry

    lax.fori_loop(0, pairs, forward, 0)
    far_copies[2].wait()
    x1 = x0[...] + dot(att_t[...].T, wout[...])
    n2 = rms_scale(x1, ff_gain).astype(bf16)
    far_copies[3].wait()
    acc_out[...] = x1
    acc_dn[...] = jnp.zeros_like(acc_dn)

    def feed(i, carry):
        at = pl.ds(pl.multiple_of(i * ff_block, ff_block), ff_block)
        u = dot(n2, win[:, at])
        square = u * u
        t = jnp.tanh(GELU_C * (u + 0.044715 * (u * square)))
        active = (0.5 * u * (1.0 + t)).astype(bf16)
        slope = 0.5 * (1.0 + t) + 0.5 * u * (1.0 - t * t) * (
            GELU_C * (1.0 + 3 * 0.044715 * square)
        )
        d_hidden = (d_act[i] * slope).astype(bf16)
        acc_out[...] += dot(active, wdown[at, :])
        acc_dn[...] += dot(d_hidden, win[:, at], NT)
        return carry

    lax.fori_loop(0, ff // ff_block, feed, 0)
    out_buf[...] = acc_out[...].astype(bf16)
    out_copy = pltpu.make_async_copy(out_buf, out_hbm, out_sem.at[0])
    out_copy.start()
    dx1 = dy.astype(f32) + rms_back(x1, ff_gain, acc_dn[...])
    grad_buf[...] = dx1
    d_att = dot(dx1.astype(bf16), wout[...], NT).astype(bf16)
    for p in range(pairs):
        part = d_att[:, p * LANES : (p + 1) * LANES]
        dxb[p, :share, :] = jnp.where(lane < LANES // 2, part, jnp.zeros_like(part))
        dxb[p, share:, :] = jnp.where(lane >= LANES // 2, part, jnp.zeros_like(part))

    def send_of(p):
        return [
            remote(src.at[p], dst.at[p], dkv_send.at[i, p], dkv_recv.at[i, p], other)
            for i, (src, dst) in enumerate(((dk_send, dk_recv), (dv_send, dv_recv)))
        ]

    def backward(p, carry):
        cols = pl.ds(pl.multiple_of(p * LANES, LANES), LANES)
        d_out = dxb[p]
        d_prob = dot(v_all[:, cols], d_out, NT)
        prob = probs[p]
        delta = jnp.sum(prob * d_prob, axis=0, keepdims=True)
        d_score = (prob * (d_prob - delta)).astype(bf16)
        low = prob.astype(bf16)
        half = LANES // 2
        for a in range(2):
            side = d_score[:, a * share : (a + 1) * share]
            feat = pl.ds(pl.multiple_of(p * LANES + a * half, half), half)
            att_t[feat, :] = (
                (dot(kt[0, feat, :], side[:share]) + dot(kt[1, feat, :], side[share:])) * 0.125
            ).astype(bf16)
        d_v = dot(low, d_out)
        d_k = dot(d_score, qs[p])
        first = head == 0
        dv_own[p] = jnp.where(first, d_v[:share], d_v[share:])
        dk_own[p] = jnp.where(first, d_k[:share], d_k[share:])
        dv_send[p] = jnp.where(first, d_v[share:], d_v[:share])
        dk_send[p] = jnp.where(first, d_k[share:], d_k[:share])
        for copy in send_of(p):
            copy.start()
        return carry

    lax.fori_loop(0, pairs, backward, 0)
    acc_dn[...] = dot(att_t[...].T, wqkv[0], NT)
    for p in range(pairs):
        for copy in send_of(p):
            copy.wait()
    d_k = jnp.concatenate([(dk_own[p] + dk_recv[p]).astype(bf16) for p in range(pairs)], axis=1)
    d_v = jnp.concatenate([(dv_own[p] + dv_recv[p]).astype(bf16) for p in range(pairs)], axis=1)
    d_n1 = acc_dn[...] + dot(d_k, wqkv[1], NT) + dot(d_v, wqkv[2], NT)
    grad_buf[...] = grad_buf[...] + rms_back(x0[...], attn_gain, d_n1)
    grad_copy = pltpu.make_async_copy(grad_buf, grad_hbm, out_sem.at[1])
    grad_copy.start()

    chunks, chunk_rows, chunk_cols = total.shape

    def forward_of(index):
        return remote(
            total.at[index], total.at[index], send4.at[index], recv4.at[index], (dp, 1)
        )

    def in_peer(k):
        target = lax.rem(my_in + k, inner)
        return target, (my_out * inner + target, head)

    def out_peer(k):
        target = lax.rem(my_out + k, outer)
        return target, (target * inner + my_in, head)

    @pl.when(head == 0)
    def _():
        local = dot(order, grad_buf[:LANES, :], TN, exact_mode).astype(bf16)
        for c in range(chunks):
            top, left = (c // 2) * chunk_rows, (c % 2) * chunk_cols
            rs_send[c] = local[top : top + chunk_rows, left : left + chunk_cols]

        def scatter_to(k):
            target, device = in_peer(k)
            return target, remote(
                rs_send.at[jnp.minimum(target, chunks - 1)], parts.at[my_in], send1.at[k], recv1.at[my_in], device
            )

        def scatter_from(k):
            source, device = in_peer(k)
            return remote(
                rs_send.at[0], parts.at[source], send1.at[k], recv1.at[source], device
            )

        mine_in = jnp.minimum(my_in, chunks - 1)

        def gather_to(k):
            return remote(
                total.at[mine_in], total.at[mine_in], send2.at[k], recv2.at[mine_in], in_peer(k)[1]
            )

        def gather_from(k):
            source, device = in_peer(k)
            at = jnp.minimum(source, chunks - 1)
            return source, at, remote(
                total.at[at], total.at[at], send2.at[k], recv2.at[at], device
            )

        def across(k):
            return remote(
                across_buf.at[my_out], across_buf.at[my_out], send3.at[k], recv3.at[my_out],
                out_peer(k)[1],
            )

        def across_from(k):
            source, device = out_peer(k)
            return remote(
                across_buf.at[source], across_buf.at[source], send3.at[k], recv3.at[source], device
            )

        for k in range(1, inner):
            target, copy = scatter_to(k)

            @pl.when(target < chunks)
            def _():
                copy.start()

        @pl.when(my_in < chunks)
        def _():
            parts[my_in] = rs_send[mine_in]
            for k in range(1, inner):
                scatter_from(k).wait_recv()
            summed = parts[0].astype(f32)
            for source in range(1, inner):
                summed = summed + parts[source].astype(f32)
            if outer > 1:
                across_buf[my_out] = summed
                for k in range(1, outer):
                    across(k).start()
                for k in range(1, outer):
                    across_from(k).wait_recv()
                summed = across_buf[0]
                for source in range(1, outer):
                    summed = summed + across_buf[source]
                for k in range(1, outer):
                    across(k).wait_send()
            total[mine_in] = summed
            for k in range(1, inner):
                gather_to(k).start()
            forward_of(mine_in).start()

        for k in range(1, inner):
            source, at, copy = gather_from(k)

            @pl.when(source < chunks)
            def _():
                copy.wait_recv()
                forward_of(at).start()

    @pl.when(head == 1)
    def _():
        for index in range(chunks):
            forward_of(index).wait_recv()

    total_copy = pltpu.make_async_copy(total, total_hbm, out_sem.at[2])
    total_copy.start()

    each(groups - 1, lambda k: request_to(k).wait_send())
    each(groups - 1, lambda k: row_to(lax.rem(dp + 1 + k, groups)).wait_send())

    @pl.when(head == 0)
    def _():
        for k in range(1, inner):
            target, device = in_peer(k)

            @pl.when(target < chunks)
            def _():
                remote(
                    rs_send.at[0], parts.at[my_in], send1.at[k], recv1.at[my_in], device
                ).wait_send()

        @pl.when(my_in < chunks)
        def _():
            for k in range(1, inner):
                remote(
                    total.at[0], total.at[0], send2.at[k], recv2.at[0], in_peer(k)[1]
                ).wait_send()

        for index in range(chunks):
            forward_of(index).wait_send()

    out_copy.wait()
    grad_copy.wait()
    total_copy.wait()


def vmem(*shape, dtype=f32):
    return pltpu.VMEM(shape, dtype)


def run_layer(
    groups, ids, segments, valid, prompt, ag, fg, rel, cot, table, wqkv, wout, win, wdown
):
    share, width = cot.shape
    ff = 2 * win.shape[1]
    slot = 2 * share
    pairs = width // LANES
    rows = prompt.shape[0]
    ff_block = 768
    capacity = max(2, 2 * slot // (2 * groups))
    block = -(-capacity // 16) * 16
    inner = math.gcd(groups, 16)
    outer = groups // inner
    chunk_rows, chunk_cols = 16, width // 2
    chunks = 2 * -(-rows // chunk_rows)
    in_vmem = pl.BlockSpec(memory_space=pltpu.VMEM)
    in_smem = pl.BlockSpec(memory_space=pltpu.SMEM)
    in_hbm = pl.BlockSpec(memory_space=pl.ANY)
    dma = pltpu.SemaphoreType.DMA
    return pl.pallas_call(
        functools.partial(layer_kernel, groups, inner, block, rows),
        out_shape=(
            jax.ShapeDtypeStruct((share, width), bf16),
            jax.ShapeDtypeStruct((share, width), f32),
            jax.ShapeDtypeStruct((chunks, chunk_rows, chunk_cols), f32),
        ),
        in_specs=[in_vmem, in_vmem, in_smem] + [in_vmem] * 5 + [in_hbm] * 5,
        out_specs=[in_hbm] * 3,
        scratch_shapes=[
            vmem(*table.shape, dtype=bf16),
            vmem(3, width, width, dtype=bf16),
            vmem(width, width, dtype=bf16),
            vmem(width, ff, dtype=bf16),
            vmem(ff, width, dtype=bf16),
            vmem(groups, 1, LANES),
            vmem(groups, 1, LANES),
            vmem(groups, block, width, dtype=bf16),
            vmem(groups, block, width, dtype=bf16),
            vmem(2, 8, LANES),
            vmem(LANES, width),
            vmem(1, slot, dtype=jnp.int32),
            vmem(slot, LANES, dtype=bf16),
            vmem(share, LANES, dtype=bf16),
            vmem(share, width),
            vmem(LANES, width),
            vmem(ff // ff_block, share, ff_block),
            vmem(share, width, dtype=bf16),
            vmem(share, width),
            vmem(slot, width, dtype=bf16),
            vmem(slot, width, dtype=bf16),
            vmem(2, width, share, dtype=bf16),
            vmem(2, width, share, dtype=bf16),
            vmem(pairs, slot, LANES, dtype=bf16),
            vmem(2 * pairs, 5, LANES, LANES),
            vmem(pairs, slot, slot),
            vmem(width, share, dtype=bf16),
            vmem(share, width),
            vmem(share, width),
        ]
        + [vmem(pairs, share, LANES)] * 6
        + [
            vmem(pairs, slot, LANES, dtype=bf16),
            vmem(chunks, chunk_rows, chunk_cols, dtype=bf16),
            vmem(inner, chunk_rows, chunk_cols, dtype=bf16),
            vmem(outer, chunk_rows, chunk_cols),
            vmem(chunks, chunk_rows, chunk_cols),
            dma((5,)),
            dma((5,)),
            dma((5,)),
            dma((groups,)),
            dma((groups,)),
            dma((groups,)),
            dma((groups,)),
            dma((2,)),
            dma((2,)),
            dma((2, pairs)),
            dma((2, pairs)),
            dma((inner,)),
            dma((inner,)),
            dma((inner,)),
            dma((inner,)),
            dma((outer,)),
            dma((outer,)),
            dma((chunks,)),
            dma((chunks,)),
            dma((3,)),
        ],
        compiler_params=pltpu.CompilerParams(
            collective_id=1, has_side_effects=True, vmem_limit_bytes=60 * 2**20
        ),
        name="layer",
    )(ids, segments, valid, prompt, ag, fg, rel, cot, table, wqkv, wout, win, wdown)


def finish_kernel(
    clip_at, total_ref, prompt_ref, first_ref, second_ref, out_in, grad_in,
    out_ref, d_start_ref, grad_ref, norm_ref, new_ref, first_out_ref, second_out_ref, low_ref,
    sem,
):
    copies = [
        pltpu.make_async_copy(src, dst, sem.at[i])
        for i, (src, dst) in enumerate(((out_in, out_ref), (grad_in, d_start_ref)))
    ]
    for copy in copies:
        copy.start()
    rows = prompt_ref.shape[0]
    chunks = total_ref.shape[0]
    summed = jnp.concatenate(
        [
            jnp.concatenate([total_ref[c], total_ref[c + 1]], axis=1)
            for c in range(0, chunks, 2)
        ],
        axis=0,
    )[:rows]
    grad_ref[...] = summed
    norm = jnp.sqrt(jnp.sum(summed * summed, keepdims=True))
    norm_ref[...] = norm
    clipped = summed * jnp.minimum(1.0, clip_at / (norm + 1e-06))
    first_out = first_decay * first_ref[...] + (1.0 - first_decay) * clipped
    second_out = second_decay * second_ref[...] + (1.0 - second_decay) * clipped * clipped
    first_hat = first_out / (1.0 - first_decay**STEP)
    second_hat = second_out / (1.0 - second_decay**STEP)
    prompt = prompt_ref[...]
    new = prompt - learn_rate * (
        first_hat / (jnp.sqrt(second_hat) + adam_epsilon) + weight_decay * prompt
    )
    first_out_ref[...] = first_out
    second_out_ref[...] = second_out
    new_ref[...] = new
    low_ref[...] = new.astype(bf16)
    for copy in copies:
        copy.wait()


def run_finish(clip_at, total, prompt, first, second, out, grad):
    rows, width = prompt.shape
    shape = jax.ShapeDtypeStruct((rows, width), f32)
    in_vmem = pl.BlockSpec(memory_space=pltpu.VMEM)
    in_hbm = pl.BlockSpec(memory_space=pl.ANY)
    return pl.pallas_call(
        functools.partial(finish_kernel, clip_at),
        out_shape=(
            jax.ShapeDtypeStruct(out.shape, out.dtype),
            jax.ShapeDtypeStruct(grad.shape, grad.dtype),
            shape,
            jax.ShapeDtypeStruct((1, 1), f32),
            shape,
            shape,
            shape,
            jax.ShapeDtypeStruct((rows, width), bf16),
        ),
        in_specs=[in_vmem] * 4 + [in_hbm] * 2,
        out_specs=[in_hbm] * 2 + [in_vmem] * 6,
        scratch_shapes=[pltpu.SemaphoreType.DMA((2,))],
        compiler_params=pltpu.CompilerParams(vmem_limit_bytes=16 * 2**20),
        name="finish",
    )(total, prompt, first, second, out, grad)


def per_device(
    ids,
    segments,
    valid_rows,
    prompt,
    table,
    attn_gain,
    w_qkv,
    rel_bias,
    w_out,
    ff_gain,
    w_in,
    w_down,
    cotangent,
    first_moment,
    second_moment,
):
    groups = lax.axis_size("dp")
    rows, width = prompt.shape
    out, grad, total = run_layer(
        groups, ids, segments, valid_rows, prompt, attn_gain, ff_gain, rel_bias.T, cotangent,
        table, jnp.transpose(w_qkv, (1, 0, 2)), w_out, w_in, w_down,
    )
    clip_at = clip_share * math.sqrt(rows * width * groups)
    final, d_start, prompt_grad, norm, prompt_new, first_out, second_out, low = run_finish(
        clip_at, total, prompt, first_moment, second_moment, out, grad
    )
    return (final, d_start, prompt_grad, norm[0, 0], prompt_new, first_out, second_out, low)


def solution(mesh):
    in_specs = (
        P("dp", None),
        P("dp", None),
        P("dp"),
        P(),
        P("dp", None),
        P(),
        P(None, None, "head"),
        P(None, "head"),
        P("head", None),
        P(),
        P(None, "head"),
        P("head", None),
        P(("dp", "head"), None),
        P(),
        P(),
    )
    out_specs = (P(("dp", "head"), None), P(("dp", "head"), None), P(), P(), P(), P(), P(), P())
    return jax.shard_map(
        per_device, mesh=mesh, in_specs=in_specs, out_specs=out_specs, check_vma=False
    )
```

```python
import functools
import math

import jax
import jax.numpy as jnp
from jax import lax
from jax.experimental import pallas as pl
from jax.experimental.pallas import tpu as pltpu
from jax.sharding import PartitionSpec as P

STEP = 10
norm_epsilon = 1e-06
thresholds = (12, 16, 23, 32, 46, 64, 91)
masked_score = -1000000000.0
learn_rate = 0.5
first_decay = 0.5
second_decay = 0.75
weight_decay = 0.01
adam_epsilon = 1e-08
clip_share = 0.05
exact_mode = lax.Precision.HIGHEST
MESH = pl.DeviceIdType.MESH
LANES = 128
NT = (((1,), (1,)), ((), ()))
NN = (((1,), (0,)), ((), ()))
TN = (((0,), (0,)), ((), ()))
f32 = jnp.float32
bf16 = jnp.bfloat16
GELU_C = math.sqrt(2.0 / math.pi)


def dot(left, right, dims=NN, precision=None):
    return lax.dot_general(left, right, dims, preferred_element_type=f32, precision=precision)


def rms_scale(rows, gain):
    return rows * lax.rsqrt(jnp.mean(rows * rows, axis=1, keepdims=True) + norm_epsilon) * gain


def rms_back(rows, gain, grad):
    r = lax.rsqrt(jnp.mean(rows * rows, axis=1, keepdims=True) + norm_epsilon)
    scaled = grad * gain
    return r * scaled - rows * (r * r * r * jnp.mean(rows * scaled, axis=1, keepdims=True))


def bucket_of(relative):
    magnitude = jnp.abs(relative)
    larger = 8 + sum(((magnitude >= cutoff).astype(jnp.int32) for cutoff in thresholds))
    return jnp.where(magnitude < 8, magnitude, larger) + 16 * (relative > 0).astype(jnp.int32)


def each(count, body):
    if count <= 16:
        for i in range(count):
            body(i)
    else:
        lax.fori_loop(0, count, lambda i, carry: (body(i), carry)[1], 0)


def layer_kernel(
    groups, inner, block, rows,
    ids_ref, seg_ref, ag_ref, fg_ref, rel_ref, valid_ref,
    prompt_hbm, cot_hbm, table_hbm, wqkv_hbm, wout_hbm, win_hbm, wdown_hbm,
    out_hbm, grad_hbm, total_hbm,
    table, wqkv, wout, win, wdown,
    req_out, req_in, found, fetched, rel_all, prompt_in, prompt_pad, cot, seg_pad, seg_here, mask_k, mask_q,
    x0, x0_prompt, d_act, act, d_scores, out_buf, grad_buf,
    k_all, v_all, kt, vt, qs, bias, probs, att_t, acc_dn, out_low,
    dk_own, dv_own, dk_send, dv_send, dk_recv, dv_recv, dxb,
    rs_send, parts, across_buf, total,
    load_sem, far_send, far_recv, req_send, req_recv, row_send, row_recv,
    kv_send, kv_recv, dkv_send, dkv_recv,
    send1, recv1, send2, recv2, send3, recv3, send4, recv4, out_sem,
):
    dp = lax.axis_index("dp")
    head = lax.axis_index("head")
    other = (dp, 1 - head)
    share, width = x0.shape
    slot = 2 * share
    pairs = width // LANES
    half_width = width // 2
    ff = win.shape[1]
    half_ff = ff // 2
    ff_block = d_act.shape[2]
    vocab = table.shape[0]
    spots = groups * block
    outer = groups // inner
    my_in = lax.rem(dp, inner)
    my_out = dp // inner
    mine = pl.ds(pl.multiple_of(head * share, share), share)
    theirs = pl.ds(pl.multiple_of((1 - head) * share, share), share)

    def remote(src, dst, send, recv, device):
        return pltpu.make_async_remote_copy(
            src, dst, send, recv, device_id=device, device_id_type=MESH
        )

    barrier = pltpu.get_barrier_semaphore()

    def peer_of(k):
        if groups > 16:
            return lax.rem(dp + 1 + k, groups)
        flip, peer = groups - 1 - k, dp
        for bit in range(groups.bit_length() - 1):
            if flip >> bit & 1:
                peer = peer + (1 - 2 * lax.rem(dp // (1 << bit), 2)) * (1 << bit)
        return peer

    def greet(k):
        pl.semaphore_signal(barrier, inc=1, device_id=(peer_of(k), head), device_id_type=MESH)

    each(groups - 1, greet)
    pl.semaphore_signal(barrier, inc=1, device_id=other, device_id_type=MESH)

    my_cols = pl.ds(pl.multiple_of(head * half_width, half_width), half_width)
    my_ff = pl.ds(pl.multiple_of(head * half_ff, half_ff), half_ff)
    weight_pairs = (
        (wdown_hbm, wdown.at[my_ff, :]),
        (wqkv_hbm, wqkv.at[:, :, my_cols]),
        (wout_hbm, wout.at[my_cols, :]),
        (win_hbm, win.at[:, my_ff]),
    )
    cot_copy = pltpu.make_async_copy(cot_hbm, cot, load_sem.at[4])
    cot_copy.start()
    table_copy = pltpu.make_async_copy(table_hbm, table, load_sem.at[5])
    table_copy.start()
    local_copies = [
        pltpu.make_async_copy(src, dst, load_sem.at[i]) for i, (src, dst) in enumerate(weight_pairs)
    ]
    for copy in local_copies:
        copy.start()
    prompt_copy = pltpu.make_async_copy(prompt_hbm, prompt_in, load_sem.at[6])
    prompt_copy.start()
    far_copies = [
        remote(src, dst, far_send.at[i], far_recv.at[i], other)
        for i, (src, dst) in enumerate(weight_pairs)
    ]

    lane = lax.broadcasted_iota(jnp.int32, (share, LANES), 1)
    row = lax.broadcasted_iota(jnp.int32, (share, LANES), 0) + head * share
    lane_f = lane.astype(f32)
    row_ids = ids_ref[:, mine].astype(f32)
    ids_col = jnp.concatenate(
        [
            jnp.broadcast_to(row_ids[:, i * LANES : (i + 1) * LANES], (LANES, LANES)).T
            for i in range(share // LANES)
        ],
        axis=0,
    )
    is_text = row >= rows
    owner = jnp.where(is_text, jnp.floor((ids_col + 0.5) * (1.0 / vocab)), -1.0)
    hot = (owner == lane_f).astype(f32)
    tri_row = lax.broadcasted_iota(jnp.int32, (share, share), 0)
    tri_col = lax.broadcasted_iota(jnp.int32, (share, share), 1)
    earlier = (tri_row > tri_col).astype(f32).astype(bf16)
    rank = jnp.sum(dot(earlier, hot.astype(bf16)) * hot, axis=1, keepdims=True)
    place = jnp.where(is_text[:, :1], owner[:, :1] * block + rank, -1.0)
    ranked = (rank == lane_f).astype(f32)
    wanted = dot(hot * (ids_col - owner * vocab), ranked, TN, exact_mode)
    for o in range(groups):
        req_out[o] = wanted[o : o + 1, :]

    order = jnp.where(is_text[:LANES], 0.0, (ids_col[:LANES] == lane_f[:LANES]).astype(f32))

    rel_all[head] = jnp.zeros((8, LANES), f32)
    rel_all[head, : rel_ref.shape[0], : rel_ref.shape[1]] = rel_ref[...].astype(f32)

    seg_pad[:, : seg_ref.shape[1]] = seg_ref[...]
    lanes_slot = lax.broadcasted_iota(jnp.int32, (1, slot), 1)
    seg_row = jnp.where(lanes_slot < rows, -1, pltpu.roll(seg_pad[...], rows, 1)).astype(f32)
    seg_here[...] = seg_row
    limit = valid_ref[0] + rows
    square_lane = lax.broadcasted_iota(jnp.int32, (LANES, LANES), 1).astype(f32) - 1.0
    square_row = lax.broadcasted_iota(jnp.int32, (LANES, LANES), 0)
    for qb in range(share // LANES):
        spot = pl.ds(pl.multiple_of(head * share + qb * LANES, LANES), LANES)
        seg_col = jnp.broadcast_to(seg_here[:, spot], (LANES, LANES)).T
        mask_q[qb * LANES : (qb + 1) * LANES, :] = (
            (seg_col == square_lane).astype(f32).astype(bf16)
        )
    for kb in range(slot // LANES):
        at = kb * LANES
        seg_col = jnp.broadcast_to(seg_row[:, at : at + LANES], (LANES, LANES)).T
        same = seg_col == square_lane
        key = square_row + at
        allowed = (key < rows) | (same & (key < limit))
        mask_k[at : at + LANES, :] = jnp.where(allowed, 0.0, masked_score).astype(bf16)

    live = row[:, :1] < limit
    cot_copy.wait()
    dy = jnp.where(live, cot[...].astype(f32), 0.0).astype(bf16)

    pl.semaphore_wait(barrier, groups)
    req_in[dp] = req_out[dp]

    def request_to(k):
        peer = peer_of(k)
        return remote(
            req_out.at[peer], req_in.at[dp], req_send.at[peer], req_recv.at[dp], (peer, head)
        )

    def request_from(k):
        peer = peer_of(k)
        return remote(
            req_out.at[peer], req_in.at[peer], req_send.at[peer], req_recv.at[peer], (peer, head)
        )

    each(groups - 1, lambda k: request_to(k).start())
    rel_copy = remote(
        rel_all.at[head], rel_all.at[head], far_send.at[4], far_recv.at[4], other
    )
    rel_copy.start()
    for copy in far_copies:
        copy.start()

    local_copies[0].wait()

    def activation_grad(index):
        at = pl.ds(pl.multiple_of(index * ff_block, ff_block), ff_block)
        d_act[index] = dot(dy, wdown[at, :], NT)

    half_blocks = half_ff // ff_block
    for i in range(half_blocks):
        activation_grad(head * half_blocks + i)

    table_copy.wait()
    each(groups - 1, lambda k: request_from(k).wait_recv())
    vocab_lane = lax.broadcasted_iota(jnp.int32, (block, vocab), 1).astype(f32)
    bunch = max(4, groups // 16)
    bunches = groups // bunch
    half_bunches = bunches // 2
    half_groups = groups // 2
    side_of = dp // half_groups

    def row_to(peer):
        return remote(
            found.at[peer], fetched.at[dp], row_send.at[peer], row_recv.at[dp], (peer, head)
        )

    def row_from(peer):
        return remote(
            found.at[peer], fetched.at[peer], row_send.at[peer], row_recv.at[peer], (peer, head)
        )

    def serve(g):
        side = jnp.where(g < half_bunches, 1 - side_of, side_of)
        base = (side * half_bunches + lax.rem(g, half_bunches)) * bunch
        wants = jnp.concatenate(
            [req_in[base + j] for j in range(bunch)] + [jnp.zeros((LANES - bunch, LANES), f32)],
            axis=0,
        ).T
        picks = jnp.concatenate(
            [
                (wants[:block, j : j + 1] == vocab_lane).astype(f32).astype(bf16)
                for j in range(bunch)
            ],
            axis=0,
        )
        picked = dot(picks, table[...]).astype(bf16)
        for j in range(bunch):
            found[base + j] = picked[j * block : (j + 1) * block]

            @pl.when(base + j != dp)
            def _():
                row_to(base + j).start()

    each(bunches, serve)
    fetched[dp] = found[dp]

    prompt_copy.wait()

    prompt_pad[...] = jnp.zeros_like(prompt_pad)
    prompt_pad[:rows, :] = prompt_in[...]
    x0_prompt[...] = dot(order, prompt_pad[...], NN, exact_mode)

    rel_copy.wait()
    spread = lax.broadcasted_iota(jnp.int32, (1, 2 * LANES), 1)
    lag = jnp.where(spread >= LANES, spread - 2 * LANES, spread)
    bucket_row = lax.broadcasted_iota(jnp.int32, (LANES, 2 * LANES), 0)
    for d in range(5):
        if d == 0:
            near = jnp.full((1, 2 * LANES), 15, jnp.int32)
        elif d == 4:
            near = jnp.full((1, 2 * LANES), 31, jnp.int32)
        else:
            near = bucket_of((d - 2) * LANES - lag)
        pick = (bucket_row == near).astype(f32).astype(bf16)
        for side in range(2):
            lines = dot(rel_all[side].astype(bf16), pick)
            for h in range(pairs):
                line = jnp.broadcast_to(lines[h : h + 1, :], (LANES, 2 * LANES))
                if d not in (0, 4):
                    line = pltpu.roll(line, 0, 1, stride=1, stride_axis=0)
                bias[side * pairs + h, d] = line[:, :LANES]

    far_copies[0].wait()
    for i in range(half_blocks):
        activation_grad((1 - head) * half_blocks + i)
    for copy in local_copies[1:]:
        copy.wait()
    far_copies[1].wait()

    spot_lane = lax.broadcasted_iota(jnp.int32, (share, half_groups * block), 1).astype(f32)

    def rows_of(side):
        base = side * half_groups
        take = (place - (base * block).astype(f32) == spot_lane).astype(f32).astype(bf16)
        return dot(
            take, fetched[pl.ds(base, half_groups)].reshape(half_groups * block, width)
        )

    def near_wait(j):
        peer = side_of * half_groups + j

        @pl.when(peer != dp)
        def _():
            row_from(peer).wait_recv()

    each(half_groups, near_wait)
    near_rows = rows_of(side_of)
    x0[...] = near_rows
    x0[:LANES, :] = near_rows[:LANES] + x0_prompt[...]

    each(half_groups, lambda j: row_from((1 - side_of) * half_groups + j).wait_recv())
    x0[...] = x0[...] + rows_of(1 - side_of)

    attn_gain = ag_ref[...].reshape(1, width)
    ff_gain = fg_ref[...].reshape(1, width)
    n1 = rms_scale(x0[...], attn_gain).astype(bf16)
    k_all[mine, :] = dot(n1, wqkv[1]).astype(bf16)
    k_copy = remote(
        k_all.at[mine, :], k_all.at[mine, :], kv_send.at[0], kv_recv.at[0], other
    )
    k_copy.start()
    v_all[mine, :] = dot(n1, wqkv[2]).astype(bf16)
    v_copy = remote(
        v_all.at[mine, :], v_all.at[mine, :], kv_send.at[1], kv_recv.at[1], other
    )
    v_copy.start()
    q = dot(n1, wqkv[0]).astype(bf16) * jnp.asarray(0.125, bf16)
    for p in range(pairs):
        part = q[:, p * LANES : (p + 1) * LANES]
        qs[p, :share, :] = jnp.where(lane < LANES // 2, part, jnp.zeros_like(part))
        qs[p, share:, :] = jnp.where(lane >= LANES // 2, part, jnp.zeros_like(part))
    kt[head] = k_all[mine, :].T
    vt[head] = v_all[mine, :].T
    k_copy.wait()
    kt[1 - head] = k_all[theirs, :].T
    v_copy.wait()
    vt[1 - head] = v_all[theirs, :].T

    def forward(p, carry):
        cols = pl.ds(pl.multiple_of(p * LANES, LANES), LANES)
        left = jnp.concatenate([k_all[:, cols], mask_k[...]], axis=1)
        right = jnp.concatenate(
            [qs[p], jnp.concatenate([mask_q[...], mask_q[...]], axis=0)], axis=1
        )
        raw = dot(left, right, NT)
        bands = []
        for kb in range(slot // LANES):
            blocks = []
            for a in range(2):
                for qb in range(share // LANES):
                    apart = kb - (head * (share // LANES) + qb)
                    spot = jnp.clip(apart, -2, 2) + 2
                    lo = a * share + qb * LANES
                    blocks.append(
                        raw[kb * LANES : (kb + 1) * LANES, lo : lo + LANES] + bias[2 * p + a, spot]
                    )
            bands.append(jnp.concatenate(blocks, axis=1))
        scores = jnp.concatenate(bands, axis=0)
        expo = jnp.exp(scores - jnp.max(scores, axis=0, keepdims=True))
        prob = expo * (1.0 / jnp.sum(expo, axis=0, keepdims=True))
        probs[p] = prob
        low = prob.astype(bf16)
        half = LANES // 2
        for a in range(2):
            side = low[:, a * share : (a + 1) * share]
            feat = pl.ds(pl.multiple_of(p * LANES + a * half, half), half)
            att_t[feat, :] = (
                dot(vt[0, feat, :], side[:share]) + dot(vt[1, feat, :], side[share:])
            ).astype(bf16)
        return carry

    lax.fori_loop(0, pairs, forward, 0, unroll=True)
    far_copies[2].wait()
    x1 = x0[...] + dot(att_t[...].T, wout[...])
    n2 = rms_scale(x1, ff_gain).astype(bf16)
    far_copies[3].wait()
    out_buf[...] = x1
    acc_dn[...] = jnp.zeros_like(acc_dn)

    def feed(i, carry):
        at = pl.ds(pl.multiple_of(i * ff_block, ff_block), ff_block)
        u = dot(n2, win[:, at])
        square = u * u
        t = jnp.tanh(GELU_C * (u + 0.044715 * (u * square)))
        act[i] = (0.5 * u * (1.0 + t)).astype(bf16)
        slope = 0.5 * (1.0 + t) + 0.5 * u * (1.0 - t * t) * (
            GELU_C * (1.0 + 3 * 0.044715 * square)
        )
        d_hidden = (d_act[i] * slope).astype(bf16)
        acc_dn[...] += dot(d_hidden, win[:, at], NT)
        return carry

    lax.fori_loop(0, ff // ff_block, feed, 0, unroll=True)
    dx1 = dy.astype(f32) + rms_back(x1, ff_gain, acc_dn[...])
    grad_buf[...] = dx1
    d_att = dot(dx1.astype(bf16), wout[...], NT).astype(bf16)
    for p in range(pairs):
        part = d_att[:, p * LANES : (p + 1) * LANES]
        dxb[p, :share, :] = jnp.where(lane < LANES // 2, part, jnp.zeros_like(part))
        dxb[p, share:, :] = jnp.where(lane >= LANES // 2, part, jnp.zeros_like(part))

    def send_of(p):
        return [
            remote(src.at[p], dst.at[p], dkv_send.at[i, p], dkv_recv.at[i, p], other)
            for i, (src, dst) in enumerate(((dk_send, dk_recv), (dv_send, dv_recv)))
        ]

    def query_grad(p, d_score, begin, end):
        half = LANES // 2
        for a in range(2):
            side = d_score[:, a * share + begin : a * share + end]
            feat = pl.ds(pl.multiple_of(p * LANES + a * half, half), half)
            att_t[feat, begin:end] = (
                (dot(kt[0, feat, :], side[:share]) + dot(kt[1, feat, :], side[share:])) * 0.125
            ).astype(bf16)

    def backward(p, carry):
        cols = pl.ds(pl.multiple_of(p * LANES, LANES), LANES)
        d_out = dxb[p]
        d_prob = dot(v_all[:, cols], d_out, NT)
        prob = probs[p]
        delta = jnp.sum(prob * d_prob, axis=0, keepdims=True)
        d_score = (prob * (d_prob - delta)).astype(bf16)
        low = prob.astype(bf16)
        d_scores[p] = d_score
        query_grad(p, d_score, 0, LANES)
        d_v = dot(low, d_out)
        d_k = dot(d_score, qs[p])
        first = head == 0
        dv_own[p] = jnp.where(first, d_v[:share], d_v[share:])
        dk_own[p] = jnp.where(first, d_k[:share], d_k[share:])
        dv_send[p] = jnp.where(first, d_v[share:], d_v[:share])
        dk_send[p] = jnp.where(first, d_k[share:], d_k[:share])
        for copy in send_of(p):
            copy.start()
        return carry

    lax.fori_loop(0, pairs, backward, 0, unroll=True)

    def input_grad(part):
        d_k = jnp.concatenate(
            [(dk_own[p, part] + dk_recv[p, part]).astype(bf16) for p in range(pairs)], axis=1
        )
        d_v = jnp.concatenate(
            [(dv_own[p, part] + dv_recv[p, part]).astype(bf16) for p in range(pairs)], axis=1
        )
        d_n1 = acc_dn[part] + dot(d_k, wqkv[1], NT) + dot(d_v, wqkv[2], NT)
        grad_buf[part] = grad_buf[part] + rms_back(x0[part], attn_gain, d_n1)

    first_rows, last_rows = slice(0, LANES), slice(LANES, share)
    acc_dn[first_rows] = dot(att_t[:, first_rows].T, wqkv[0], NT)
    for p in range(pairs):
        for copy in send_of(p):
            copy.wait()
    input_grad(first_rows)

    chunks, chunk_rows, chunk_cols = total.shape

    def forward_of(index):
        return remote(
            total.at[index], total.at[index], send4.at[index], recv4.at[index], (dp, 1)
        )

    def in_peer(k):
        target, flip = my_in, inner - k
        for bit in range(inner.bit_length() - 1):
            if flip >> bit & 1:
                target = target + (1 - 2 * lax.rem(my_in // (1 << bit), 2)) * (1 << bit)
        return target, (my_out * inner + target, head)

    def out_peer(k):
        target = lax.rem(my_out + k, outer)
        return target, (target * inner + my_in, head)

    mine_in = jnp.minimum(my_in, chunks - 1)

    def scatter_to(k):
        target, device = in_peer(k)
        at = jnp.minimum(target, chunks - 1)
        return target, remote(rs_send.at[at], parts.at[my_in], send1.at[k], recv1.at[my_in], device)

    def scatter_from(k):
        source, device = in_peer(k)
        return remote(rs_send.at[0], parts.at[source], send1.at[k], recv1.at[source], device)

    def gather_to(k):
        return remote(
            total.at[mine_in], total.at[mine_in], send2.at[k], recv2.at[mine_in], in_peer(k)[1]
        )

    def gather_from(k):
        source, device = in_peer(k)
        at = jnp.minimum(source, chunks - 1)
        return source, at, remote(total.at[at], total.at[at], send2.at[k], recv2.at[at], device)

    def across(k):
        return remote(
            across_buf.at[my_out], across_buf.at[my_out], send3.at[k], recv3.at[my_out],
            out_peer(k)[1],
        )

    def across_from(k):
        source, device = out_peer(k)
        return remote(
            across_buf.at[source], across_buf.at[source], send3.at[k], recv3.at[source], device
        )

    @pl.when(head == 0)
    def _():
        local = dot(order, grad_buf[first_rows], TN, exact_mode).astype(bf16)
        for c in range(chunks):
            top, left = (c // 2) * chunk_rows, (c % 2) * chunk_cols
            rs_send[c] = local[top : top + chunk_rows, left : left + chunk_cols]

        for k in range(1, inner):
            target, copy = scatter_to(k)

            @pl.when(target < chunks)
            def _():
                copy.start()

    for p in range(pairs):
        query_grad(p, d_scores[p], LANES, share)
    for i in range(ff // ff_block):
        out_buf[...] = out_buf[...] + dot(act[i], wdown[i * ff_block : (i + 1) * ff_block, :])
    out_low[...] = out_buf[...].astype(bf16)
    out_copy = pltpu.make_async_copy(out_low, out_hbm, out_sem.at[0])
    out_copy.start()

    @pl.when((head == 0) & (my_in < chunks))
    def _():
        parts[my_in] = rs_send[mine_in]
        for k in range(1, inner):
            scatter_from(k).wait_recv()
        summed = parts[0].astype(f32)
        for source in range(1, inner):
            summed = summed + parts[source].astype(f32)
        if outer > 1:
            across_buf[my_out] = summed
            for k in range(1, outer):
                across(k).start()
            for k in range(1, outer):
                across_from(k).wait_recv()
            summed = across_buf[0]
            for source in range(1, outer):
                summed = summed + across_buf[source]
            for k in range(1, outer):
                across(k).wait_send()
        total[mine_in] = summed.astype(bf16)
        for k in range(1, inner):
            gather_to(k).start()
        forward_of(mine_in).start()

    acc_dn[last_rows] = dot(att_t[:, last_rows].T, wqkv[0], NT)
    input_grad(last_rows)
    grad_copy = pltpu.make_async_copy(grad_buf, grad_hbm, out_sem.at[1])
    grad_copy.start()

    @pl.when(head == 0)
    def _():
        for k in range(1, inner):
            source, at, copy = gather_from(k)

            @pl.when(source < chunks)
            def _():
                copy.wait_recv()
                forward_of(at).start()

    @pl.when(head == 1)
    def _():
        for index in range(chunks):
            forward_of(index).wait_recv()

    total_copy = pltpu.make_async_copy(total, total_hbm, out_sem.at[2])
    total_copy.start()

    each(groups - 1, lambda k: request_to(k).wait_send())
    each(groups - 1, lambda k: row_to(peer_of(k)).wait_send())

    @pl.when(head == 0)
    def _():
        for k in range(1, inner):
            target, device = in_peer(k)

            @pl.when(target < chunks)
            def _():
                scatter_to(k)[1].wait_send()

        @pl.when(my_in < chunks)
        def _():
            for k in range(1, inner):
                gather_to(k).wait_send()

        for index in range(chunks):
            forward_of(index).wait_send()

    out_copy.wait()
    grad_copy.wait()
    total_copy.wait()


def vmem(*shape, dtype=f32):
    return pltpu.VMEM(shape, dtype)


def run_layer(
    groups, ids, segments, ag, fg, rel, valid, prompt, cot, table, wqkv, wout, win, wdown
):
    share, width = cot.shape
    ff = 2 * win.shape[1]
    slot = 2 * share
    pairs = width // LANES
    rows = prompt.shape[0]
    ff_block = 768
    capacity = max(2, 2 * slot // (2 * groups))
    block = -(-capacity // 16) * 16
    inner = math.gcd(groups, 16)
    outer = groups // inner
    chunk_rows, chunk_cols = 16, width // 2
    chunks = 2 * -(-rows // chunk_rows)
    in_vmem = pl.BlockSpec(memory_space=pltpu.VMEM)
    in_hbm = pl.BlockSpec(memory_space=pl.ANY)
    dma = pltpu.SemaphoreType.DMA
    return pl.pallas_call(
        functools.partial(layer_kernel, groups, inner, block, rows),
        out_shape=(
            jax.ShapeDtypeStruct((share, width), bf16),
            jax.ShapeDtypeStruct((share, width), f32),
            jax.ShapeDtypeStruct((chunks, chunk_rows, chunk_cols), bf16),
        ),
        in_specs=[in_vmem] * 5 + [pl.BlockSpec(memory_space=pltpu.SMEM)] + [in_hbm] * 7,
        out_specs=[in_hbm] * 3,
        scratch_shapes=[
            vmem(*table.shape, dtype=bf16),
            vmem(3, width, width, dtype=bf16),
            vmem(width, width, dtype=bf16),
            vmem(width, ff, dtype=bf16),
            vmem(ff, width, dtype=bf16),
            vmem(groups, 1, LANES),
            vmem(groups, 1, LANES),
            vmem(groups, block, width, dtype=bf16),
            vmem(groups, block, width, dtype=bf16),
            vmem(2, 8, LANES),
            vmem(rows, width),
            vmem(LANES, width),
            vmem(share, width, dtype=bf16),
            vmem(1, slot, dtype=jnp.int32),
            vmem(1, slot),
            vmem(slot, LANES, dtype=bf16),
            vmem(share, LANES, dtype=bf16),
            vmem(share, width),
            vmem(LANES, width),
            vmem(ff // ff_block, share, ff_block),
            vmem(ff // ff_block, share, ff_block, dtype=bf16),
            vmem(pairs, slot, slot, dtype=bf16),
            vmem(share, width),
            vmem(share, width),
            vmem(slot, width, dtype=bf16),
            vmem(slot, width, dtype=bf16),
            vmem(2, width, share, dtype=bf16),
            vmem(2, width, share, dtype=bf16),
            vmem(pairs, slot, LANES, dtype=bf16),
            vmem(2 * pairs, 5, LANES, LANES),
            vmem(pairs, slot, slot),
            vmem(width, share, dtype=bf16),
            vmem(share, width),
            vmem(share, width, dtype=bf16),
        ]
        + [vmem(pairs, share, LANES)] * 6
        + [
            vmem(pairs, slot, LANES, dtype=bf16),
            vmem(chunks, chunk_rows, chunk_cols, dtype=bf16),
            vmem(inner, chunk_rows, chunk_cols, dtype=bf16),
            vmem(outer, chunk_rows, chunk_cols),
            vmem(chunks, chunk_rows, chunk_cols, dtype=bf16),
            dma((7,)),
            dma((5,)),
            dma((5,)),
            dma((groups,)),
            dma((groups,)),
            dma((groups,)),
            dma((groups,)),
            dma((2,)),
            dma((2,)),
            dma((2, pairs)),
            dma((2, pairs)),
            dma((inner,)),
            dma((inner,)),
            dma((inner,)),
            dma((inner,)),
            dma((outer,)),
            dma((outer,)),
            dma((chunks,)),
            dma((chunks,)),
            dma((3,)),
        ],
        compiler_params=pltpu.CompilerParams(
            collective_id=1, has_side_effects=True, vmem_limit_bytes=60 * 2**20
        ),
        name="layer",
    )(ids, segments, ag, fg, rel, valid, prompt, cot, table, wqkv, wout, win, wdown)


def finish_kernel(
    clip_at, prompt_hbm, first_hbm, second_hbm, total_hbm, out_hbm, grad_hbm,
    *refs,
):
    results, (prompt_ref, first_ref, second_ref, total_ref, out_buf, grad_buf), (
        grad_ref, norm_ref, new_ref, first_out_ref, second_out_ref, low_ref,
    ), (load_sem, store_sem) = refs[:8], refs[8:14], refs[14:20], refs[20:]
    loads = [
        pltpu.make_async_copy(src, dst, load_sem.at[i])
        for i, (src, dst) in enumerate(
            (
                (total_hbm, total_ref), (first_hbm, first_ref), (second_hbm, second_ref),
                (prompt_hbm, prompt_ref), (out_hbm, out_buf), (grad_hbm, grad_buf),
            )
        )
    ]
    for copy in loads:
        copy.start()
    stores = []

    def store(src, index):
        stores.append(pltpu.make_async_copy(src, results[index], store_sem.at[index]))
        stores[-1].start()

    rows = prompt_ref.shape[0]
    chunks = total_ref.shape[0]
    loads[0].wait()
    summed = jnp.concatenate(
        [
            jnp.concatenate([total_ref[c], total_ref[c + 1]], axis=1)
            for c in range(0, chunks, 2)
        ],
        axis=0,
    ).astype(f32)[:rows]
    grad_ref[...] = summed
    store(grad_ref, 2)
    norm = jnp.sqrt(jnp.sum(summed * summed, keepdims=True))
    norm_ref[...] = norm
    store(norm_ref, 3)
    clipped = summed * jnp.minimum(1.0, clip_at / (norm + 1e-06))
    loads[1].wait()
    first_out = first_decay * first_ref[...] + (1.0 - first_decay) * clipped
    first_out_ref[...] = first_out
    store(first_out_ref, 5)
    loads[2].wait()
    second_out = second_decay * second_ref[...] + (1.0 - second_decay) * clipped * clipped
    second_out_ref[...] = second_out
    store(second_out_ref, 6)
    loads[4].wait()
    store(out_buf, 0)
    loads[5].wait()
    store(grad_buf, 1)
    first_hat = first_out / (1.0 - first_decay**STEP)
    second_hat = second_out / (1.0 - second_decay**STEP)
    loads[3].wait()
    prompt = prompt_ref[...]
    new = prompt - learn_rate * (
        first_hat / (jnp.sqrt(second_hat) + adam_epsilon) + weight_decay * prompt
    )
    new_ref[...] = new
    store(new_ref, 4)
    low_ref[...] = new.astype(bf16)
    store(low_ref, 7)
    for copy in stores:
        copy.wait()


def run_finish(clip_at, total, prompt, first, second, out, grad):
    rows, width = prompt.shape
    shape = jax.ShapeDtypeStruct((rows, width), f32)
    in_hbm = pl.BlockSpec(memory_space=pl.ANY)
    return pl.pallas_call(
        functools.partial(finish_kernel, clip_at),
        out_shape=(
            jax.ShapeDtypeStruct(out.shape, out.dtype),
            jax.ShapeDtypeStruct(grad.shape, grad.dtype),
            shape,
            jax.ShapeDtypeStruct((1, 1), f32),
            shape,
            shape,
            shape,
            jax.ShapeDtypeStruct((rows, width), bf16),
        ),
        in_specs=[in_hbm] * 6,
        out_specs=[in_hbm] * 8,
        scratch_shapes=[
            vmem(rows, width),
            vmem(rows, width),
            vmem(rows, width),
            vmem(*total.shape, dtype=bf16),
            vmem(*out.shape, dtype=bf16),
            vmem(*grad.shape),
            vmem(rows, width),
            vmem(1, 1),
            vmem(rows, width),
            vmem(rows, width),
            vmem(rows, width),
            vmem(rows, width, dtype=bf16),
            pltpu.SemaphoreType.DMA((6,)),
            pltpu.SemaphoreType.DMA((8,)),
        ],
        compiler_params=pltpu.CompilerParams(vmem_limit_bytes=63 * 2**20),
        name="finish",
    )(prompt, first, second, total, out, grad)


def per_device(
    ids,
    segments,
    valid_rows,
    prompt,
    table,
    attn_gain,
    w_qkv,
    rel_bias,
    w_out,
    ff_gain,
    w_in,
    w_down,
    cotangent,
    first_moment,
    second_moment,
):
    groups = lax.axis_size("dp")
    rows, width = prompt.shape
    out, grad, total = run_layer(
        groups, ids, segments, attn_gain, ff_gain, rel_bias.T, valid_rows, prompt, cotangent, table,
        jnp.transpose(w_qkv, (1, 0, 2)), w_out, w_in, w_down,
    )
    clip_at = clip_share * math.sqrt(rows * width * groups)
    final, d_start, prompt_grad, norm, prompt_new, first_out, second_out, low = run_finish(
        clip_at, total, prompt, first_moment, second_moment, out, grad
    )
    return (final, d_start, prompt_grad, norm[0, 0], prompt_new, first_out, second_out, low)


def solution(mesh):
    in_specs = (
        P("dp", None),
        P("dp", None),
        P("dp"),
        P(),
        P("dp", None),
        P(),
        P(None, None, "head"),
        P(None, "head"),
        P("head", None),
        P(),
        P(None, "head"),
        P("head", None),
        P(("dp", "head"), None),
        P(),
        P(),
    )
    out_specs = (P(("dp", "head"), None), P(("dp", "head"), None), P(), P(), P(), P(), P(), P())
    return jax.shard_map(
        per_device, mesh=mesh, in_specs=in_specs, out_specs=out_specs, check_vma=False
    )
```

```python
import functools
import math

import jax
import jax.numpy as jnp
from jax import lax
from jax.experimental import pallas as pl
from jax.experimental.pallas import tpu as pltpu
from jax.sharding import PartitionSpec as P

STEP = 10
norm_epsilon = 1e-06
thresholds = (12, 16, 23, 32, 46, 64, 91)
masked_score = -1000000000.0
learn_rate = 0.5
first_decay = 0.5
second_decay = 0.75
weight_decay = 0.01
adam_epsilon = 1e-08
clip_share = 0.05
exact_mode = lax.Precision.HIGHEST
MESH = pl.DeviceIdType.MESH
LANES = 128
NT = (((1,), (1,)), ((), ()))
NN = (((1,), (0,)), ((), ()))
TN = (((0,), (0,)), ((), ()))
f32 = jnp.float32
bf16 = jnp.bfloat16
GELU_C = math.sqrt(2.0 / math.pi)


def dot(left, right, dims=NN, precision=None):
    return lax.dot_general(left, right, dims, preferred_element_type=f32, precision=precision)


def rms_scale(rows, gain):
    return rows * lax.rsqrt(jnp.mean(rows * rows, axis=1, keepdims=True) + norm_epsilon) * gain


def rms_back(rows, gain, grad):
    r = lax.rsqrt(jnp.mean(rows * rows, axis=1, keepdims=True) + norm_epsilon)
    scaled = grad * gain
    return r * scaled - rows * (r * r * r * jnp.mean(rows * scaled, axis=1, keepdims=True))


def bucket_of(relative):
    magnitude = jnp.abs(relative)
    larger = 8 + sum(((magnitude >= cutoff).astype(jnp.int32) for cutoff in thresholds))
    return jnp.where(magnitude < 8, magnitude, larger) + 16 * (relative > 0).astype(jnp.int32)


def each(count, body):
    if count <= 16:
        for i in range(count):
            body(i)
    else:
        lax.fori_loop(0, count, lambda i, carry: (body(i), carry)[1], 0)


def layer_kernel(
    groups, inner, block, rows,
    valid_ref, ids_hbm, seg_hbm, ag_hbm, fg_hbm, rel_hbm, prompt_hbm, cot_hbm, table_hbm, wqkv_hbm, wout_hbm, win_hbm, wdown_hbm,
    out_hbm, grad_hbm, total_hbm,
    ids_ref, seg_ref, ag_ref, fg_ref, rel_ref,
    table, wqkv, wout, win, wdown,
    req_out, req_in, found, fetched, rel_all, prompt_in, prompt_pad, cot, seg_pad, seg_here, mask_k, mask_q,
    x0, x0_prompt, d_act, act, d_scores, out_buf, grad_buf,
    k_all, v_all, kt, vt, qs, bias, probs, att_t, acc_dn, out_low,
    dk_own, dv_own, dk_send, dv_send, dk_recv, dv_recv, dxb,
    rs_send, parts, across_buf, total,
    load_sem, far_send, far_recv, req_send, req_recv, row_send, row_recv,
    kv_send, kv_recv, dkv_send, dkv_recv,
    send1, recv1, send2, recv2, send3, recv3, send4, recv4, out_sem,
):
    dp = lax.axis_index("dp")
    head = lax.axis_index("head")
    other = (dp, 1 - head)
    share, width = x0.shape
    slot = 2 * share
    pairs = width // LANES
    half_width = width // 2
    ff = win.shape[1]
    half_ff = ff // 2
    ff_block = d_act.shape[2]
    vocab = table.shape[0]
    spots = groups * block
    outer = groups // inner
    my_in = lax.rem(dp, inner)
    my_out = dp // inner
    mine = pl.ds(pl.multiple_of(head * share, share), share)

    def remote(src, dst, send, recv, device):
        return pltpu.make_async_remote_copy(
            src, dst, send, recv, device_id=device, device_id_type=MESH
        )

    barrier = pltpu.get_barrier_semaphore()

    def peer_of(k):
        if groups > 16:
            return lax.rem(dp + 1 + k, groups)
        flip, peer = groups - 1 - k, dp
        for bit in range(groups.bit_length() - 1):
            if flip >> bit & 1:
                peer = peer + (1 - 2 * lax.rem(dp // (1 << bit), 2)) * (1 << bit)
        return peer

    def greet(k):
        pl.semaphore_signal(barrier, inc=1, device_id=(peer_of(k), head), device_id_type=MESH)

    each(groups - 1, greet)
    pl.semaphore_signal(barrier, inc=1, device_id=other, device_id_type=MESH)

    small_copies = [
        pltpu.make_async_copy(src, dst, load_sem.at[7 + i])
        for i, (src, dst) in enumerate(
            (
                (ids_hbm, ids_ref), (seg_hbm, seg_ref), (rel_hbm, rel_ref), (ag_hbm, ag_ref),
                (fg_hbm, fg_ref),
            )
        )
    ]
    for copy in small_copies:
        copy.start()
    my_cols = pl.ds(pl.multiple_of(head * half_width, half_width), half_width)
    my_ff = pl.ds(pl.multiple_of(head * half_ff, half_ff), half_ff)
    weight_pairs = (
        (wdown_hbm, wdown.at[my_ff, :]),
        (wqkv_hbm, wqkv.at[:, :, my_cols]),
        (wout_hbm, wout.at[my_cols, :]),
        (win_hbm, win.at[:, my_ff]),
    )
    cot_copy = pltpu.make_async_copy(cot_hbm, cot, load_sem.at[4])
    cot_copy.start()
    table_copy = pltpu.make_async_copy(table_hbm, table, load_sem.at[5])
    table_copy.start()
    local_copies = [
        pltpu.make_async_copy(src, dst, load_sem.at[i]) for i, (src, dst) in enumerate(weight_pairs)
    ]
    for copy in local_copies:
        copy.start()
    prompt_copy = pltpu.make_async_copy(prompt_hbm, prompt_in, load_sem.at[6])
    prompt_copy.start()
    far_copies = [
        remote(src, dst, far_send.at[i], far_recv.at[i], other)
        for i, (src, dst) in enumerate(weight_pairs)
    ]

    lane = lax.broadcasted_iota(jnp.int32, (share, LANES), 1)
    row = lax.broadcasted_iota(jnp.int32, (share, LANES), 0) + head * share
    lane_f = lane.astype(f32)
    small_copies[0].wait()
    row_ids = ids_ref[:, mine].astype(f32)
    ids_col = jnp.concatenate(
        [
            jnp.broadcast_to(row_ids[:, i * LANES : (i + 1) * LANES], (LANES, LANES)).T
            for i in range(share // LANES)
        ],
        axis=0,
    )
    is_text = row >= rows
    owner = jnp.where(is_text, jnp.floor((ids_col + 0.5) * (1.0 / vocab)), -1.0)
    hot = (owner == lane_f).astype(f32)
    tri_row = lax.broadcasted_iota(jnp.int32, (share, share), 0)
    tri_col = lax.broadcasted_iota(jnp.int32, (share, share), 1)
    earlier = (tri_row > tri_col).astype(f32).astype(bf16)
    rank = jnp.sum(dot(earlier, hot.astype(bf16)) * hot, axis=1, keepdims=True)
    place = jnp.where(is_text[:, :1], owner[:, :1] * block + rank, -1.0)
    ranked = (rank == lane_f).astype(f32)
    wanted = dot(hot * (ids_col - owner * vocab), ranked, TN, exact_mode)
    for o in range(groups):
        req_out[o] = wanted[o : o + 1, :]

    order = jnp.where(is_text[:LANES], 0.0, (ids_col[:LANES] == lane_f[:LANES]).astype(f32))

    small_copies[2].wait()
    rel_all[head] = jnp.zeros((8, LANES), f32)
    rel_all[head, : rel_ref.shape[0], : rel_ref.shape[1]] = rel_ref[...].astype(f32)

    small_copies[1].wait()
    seg_pad[:, : seg_ref.shape[1]] = seg_ref[...]
    lanes_slot = lax.broadcasted_iota(jnp.int32, (1, slot), 1)
    seg_row = jnp.where(lanes_slot < rows, -1, pltpu.roll(seg_pad[...], rows, 1)).astype(f32)
    seg_here[...] = seg_row
    limit = valid_ref[0] + rows
    square_lane = lax.broadcasted_iota(jnp.int32, (LANES, LANES), 1).astype(f32) - 1.0
    square_row = lax.broadcasted_iota(jnp.int32, (LANES, LANES), 0)
    for qb in range(share // LANES):
        spot = pl.ds(pl.multiple_of(head * share + qb * LANES, LANES), LANES)
        seg_col = jnp.broadcast_to(seg_here[:, spot], (LANES, LANES)).T
        mask_q[qb * LANES : (qb + 1) * LANES, :] = (
            (seg_col == square_lane).astype(f32).astype(bf16)
        )
    for kb in range(slot // LANES):
        at = kb * LANES
        seg_col = jnp.broadcast_to(seg_row[:, at : at + LANES], (LANES, LANES)).T
        same = seg_col == square_lane
        key = square_row + at
        allowed = (key < rows) | (same & (key < limit))
        mask_k[at // share, at % share : at % share + LANES, :] = jnp.where(allowed, 0.0, masked_score).astype(bf16)

    live = row[:, :1] < limit
    cot_copy.wait()
    dy = jnp.where(live, cot[...].astype(f32), 0.0).astype(bf16)

    pl.semaphore_wait(barrier, groups)
    req_in[dp] = req_out[dp]

    def request_to(k):
        peer = peer_of(k)
        return remote(
            req_out.at[peer], req_in.at[dp], req_send.at[peer], req_recv.at[dp], (peer, head)
        )

    def request_from(k):
        peer = peer_of(k)
        return remote(
            req_out.at[peer], req_in.at[peer], req_send.at[peer], req_recv.at[peer], (peer, head)
        )

    each(groups - 1, lambda k: request_to(k).start())
    rel_copy = remote(
        rel_all.at[head], rel_all.at[head], far_send.at[4], far_recv.at[4], other
    )
    rel_copy.start()
    for copy in far_copies:
        copy.start()

    local_copies[0].wait()

    def activation_grad(index):
        at = pl.ds(pl.multiple_of(index * ff_block, ff_block), ff_block)
        d_act[index] = dot(dy, wdown[at, :], NT)

    half_blocks = half_ff // ff_block
    for i in range(half_blocks):
        activation_grad(head * half_blocks + i)

    table_copy.wait()
    each(groups - 1, lambda k: request_from(k).wait_recv())
    vocab_lane = lax.broadcasted_iota(jnp.int32, (block, vocab), 1).astype(f32)
    bunch = max(4, groups // 16)
    bunches = groups // bunch
    half_bunches = bunches // 2
    half_groups = groups // 2
    side_of = dp // half_groups

    def row_to(peer):
        return remote(
            found.at[peer], fetched.at[dp], row_send.at[peer], row_recv.at[dp], (peer, head)
        )

    def row_from(peer):
        return remote(
            found.at[peer], fetched.at[peer], row_send.at[peer], row_recv.at[peer], (peer, head)
        )

    def serve(g):
        side = jnp.where(g < half_bunches, 1 - side_of, side_of)
        base = (side * half_bunches + lax.rem(g, half_bunches)) * bunch
        wants = jnp.concatenate(
            [req_in[base + j] for j in range(bunch)] + [jnp.zeros((LANES - bunch, LANES), f32)],
            axis=0,
        ).T
        picks = jnp.concatenate(
            [
                (wants[:block, j : j + 1] == vocab_lane).astype(f32).astype(bf16)
                for j in range(bunch)
            ],
            axis=0,
        )
        picked = dot(picks, table[...]).astype(bf16)
        for j in range(bunch):
            found[base + j] = picked[j * block : (j + 1) * block]

            @pl.when(base + j != dp)
            def _():
                row_to(base + j).start()

    each(bunches, serve)
    fetched[dp] = found[dp]

    prompt_copy.wait()

    prompt_pad[...] = jnp.zeros_like(prompt_pad)
    prompt_pad[:rows, :] = prompt_in[...]
    x0_prompt[...] = dot(order, prompt_pad[...], NN, exact_mode)

    rel_copy.wait()
    spread = lax.broadcasted_iota(jnp.int32, (1, 2 * LANES), 1)
    lag = jnp.where(spread >= LANES, spread - 2 * LANES, spread)
    bucket_row = lax.broadcasted_iota(jnp.int32, (LANES, 2 * LANES), 0)
    for d in range(5):
        if d == 0:
            near = jnp.full((1, 2 * LANES), 15, jnp.int32)
        elif d == 4:
            near = jnp.full((1, 2 * LANES), 31, jnp.int32)
        else:
            near = bucket_of((d - 2) * LANES - lag)
        pick = (bucket_row == near).astype(f32).astype(bf16)
        for side in range(2):
            lines = dot(rel_all[side].astype(bf16), pick)
            for h in range(pairs):
                line = jnp.broadcast_to(lines[h : h + 1, :], (LANES, 2 * LANES))
                if d not in (0, 4):
                    line = pltpu.roll(line, 0, 1, stride=1, stride_axis=0)
                bias[side * pairs + h, d] = line[:, :LANES]

    far_copies[0].wait()
    for i in range(half_blocks):
        activation_grad((1 - head) * half_blocks + i)
    for copy in local_copies[1:]:
        copy.wait()
    far_copies[1].wait()

    spot_lane = lax.broadcasted_iota(jnp.int32, (share, half_groups * block), 1).astype(f32)

    def rows_of(side):
        base = side * half_groups
        take = (place - (base * block).astype(f32) == spot_lane).astype(f32).astype(bf16)
        return dot(
            take, fetched[pl.ds(base, half_groups)].reshape(half_groups * block, width)
        )

    def near_wait(j):
        peer = side_of * half_groups + j

        @pl.when(peer != dp)
        def _():
            row_from(peer).wait_recv()

    each(half_groups, near_wait)
    near_rows = rows_of(side_of)
    x0[...] = near_rows
    x0[:LANES, :] = near_rows[:LANES] + x0_prompt[...]

    each(half_groups, lambda j: row_from((1 - side_of) * half_groups + j).wait_recv())
    x0[...] = x0[...] + rows_of(1 - side_of)

    small_copies[3].wait()
    small_copies[4].wait()
    attn_gain = ag_ref[...].reshape(1, width)
    ff_gain = fg_ref[...].reshape(1, width)
    n1 = rms_scale(x0[...], attn_gain).astype(bf16)
    k_all[head] = dot(n1, wqkv[1]).astype(bf16)
    k_copy = remote(k_all.at[head], k_all.at[head], kv_send.at[0], kv_recv.at[0], other)
    k_copy.start()
    v_all[head] = dot(n1, wqkv[2]).astype(bf16)
    v_copy = remote(v_all.at[head], v_all.at[head], kv_send.at[1], kv_recv.at[1], other)
    v_copy.start()
    q = dot(n1, wqkv[0]).astype(bf16) * jnp.asarray(0.125, bf16)
    for p in range(pairs):
        part = q[:, p * LANES : (p + 1) * LANES]
        qs[p, :share, :] = jnp.where(lane < LANES // 2, part, jnp.zeros_like(part))
        qs[p, share:, :] = jnp.where(lane >= LANES // 2, part, jnp.zeros_like(part))

    far = 1 - head
    blocks = share // LANES
    half = LANES // 2

    def raw_scores(p, side, shift):
        left = jnp.concatenate(
            [k_all[side, :, p * LANES : (p + 1) * LANES], mask_k[side]], axis=1
        )
        right = jnp.concatenate(
            [qs[p], jnp.concatenate([mask_q[...], mask_q[...]], axis=0)], axis=1
        )
        raw = dot(left, right, NT)
        bands = []
        for kb in range(blocks):
            parts_of = []
            for a in range(2):
                for qb in range(blocks):
                    apart = shift + (kb - qb)
                    if isinstance(apart, int):
                        spot = min(max(apart, -2), 2) + 2
                    else:
                        spot = jnp.clip(apart, -2, 2) + 2
                    lo = a * share + qb * LANES
                    parts_of.append(
                        raw[kb * LANES : (kb + 1) * LANES, lo : lo + LANES] + bias[2 * p + a, spot]
                    )
            bands.append(jnp.concatenate(parts_of, axis=1))
        return jnp.concatenate(bands, axis=0)

    for p in range(pairs):
        probs[p, head] = raw_scores(p, head, 0)
    kt[head] = k_all[head].T
    vt[head] = v_all[head].T
    k_copy.wait()
    kt[far] = k_all[far].T
    v_copy.wait()
    vt[far] = v_all[far].T

    for p in range(pairs):
        near_raw = probs[p, head]
        far_raw = raw_scores(p, far, (1 - 2 * head) * blocks)
        top = jnp.maximum(
            jnp.max(near_raw, axis=0, keepdims=True), jnp.max(far_raw, axis=0, keepdims=True)
        )
        near_exp, far_exp = jnp.exp(near_raw - top), jnp.exp(far_raw - top)
        inverse = 1.0 / (
            jnp.sum(near_exp, axis=0, keepdims=True) + jnp.sum(far_exp, axis=0, keepdims=True)
        )
        near_prob, far_prob = near_exp * inverse, far_exp * inverse
        probs[p, head] = near_prob
        probs[p, far] = far_prob
        near_low, far_low = near_prob.astype(bf16), far_prob.astype(bf16)
        for a in range(2):
            feat = slice(p * LANES + a * half, p * LANES + (a + 1) * half)
            side = slice(a * share, (a + 1) * share)
            att_t[feat, :] = (
                dot(vt[head, feat, :], near_low[:, side]) + dot(vt[far, feat, :], far_low[:, side])
            ).astype(bf16)

    far_copies[2].wait()
    x1 = x0[...] + dot(att_t[...].T, wout[...])
    n2 = rms_scale(x1, ff_gain).astype(bf16)
    far_copies[3].wait()
    out_buf[...] = x1
    acc_dn[...] = jnp.zeros_like(acc_dn)

    def feed(i, carry):
        at = pl.ds(pl.multiple_of(i * ff_block, ff_block), ff_block)
        u = dot(n2, win[:, at])
        square = u * u
        t = jnp.tanh(GELU_C * (u + 0.044715 * (u * square)))
        act[i] = (0.5 * u * (1.0 + t)).astype(bf16)
        slope = 0.5 * (1.0 + t) + 0.5 * u * (1.0 - t * t) * (
            GELU_C * (1.0 + 3 * 0.044715 * square)
        )
        d_hidden = (d_act[i] * slope).astype(bf16)
        acc_dn[...] += dot(d_hidden, win[:, at], NT)
        return carry

    lax.fori_loop(0, ff // ff_block, feed, 0, unroll=True)
    dx1 = dy.astype(f32) + rms_back(x1, ff_gain, acc_dn[...])
    grad_buf[...] = dx1
    d_att = dot(dx1.astype(bf16), wout[...], NT).astype(bf16)
    for p in range(pairs):
        part = d_att[:, p * LANES : (p + 1) * LANES]
        dxb[p, :share, :] = jnp.where(lane < LANES // 2, part, jnp.zeros_like(part))
        dxb[p, share:, :] = jnp.where(lane >= LANES // 2, part, jnp.zeros_like(part))

    def first_sends(p):
        return [
            remote(src.at[0, p], dst.at[0, p], dkv_send.at[i, p], dkv_recv.at[i, p], other)
            for i, (src, dst) in enumerate(((dk_send, dk_recv), (dv_send, dv_recv)))
        ]

    last_sends = [
        remote(src.at[1], dst.at[1], dkv_send.at[i, pairs], dkv_recv.at[i, pairs], other)
        for i, (src, dst) in enumerate(((dk_send, dk_recv), (dv_send, dv_recv)))
    ]
    first_rows, last_rows = slice(0, LANES), slice(LANES, share)

    def query_grad(p, begin, end):
        for a in range(2):
            feat = slice(p * LANES + a * half, p * LANES + (a + 1) * half)
            side = slice(a * share + begin, a * share + end)
            att_t[feat, begin:end] = (
                (
                    dot(kt[head, feat, :], d_scores[p, head, :, side])
                    + dot(kt[far, feat, :], d_scores[p, far, :, side])
                )
                * 0.125
            ).astype(bf16)

    for p in range(pairs):
        cols = slice(p * LANES, (p + 1) * LANES)
        d_out = dxb[p]
        near_d = dot(v_all[head, :, cols], d_out, NT)
        far_d = dot(v_all[far, :, cols], d_out, NT)
        near_prob, far_prob = probs[p, head], probs[p, far]
        delta = jnp.sum(near_prob * near_d, axis=0, keepdims=True) + jnp.sum(
            far_prob * far_d, axis=0, keepdims=True
        )
        far_score = (far_prob * (far_d - delta)).astype(bf16)
        d_scores[p, far] = far_score
        d_scores[p, head] = (near_prob * (near_d - delta)).astype(bf16)
        dv_send[0, p] = dot(far_prob[first_rows].astype(bf16), d_out)
        dk_send[0, p] = dot(far_score[first_rows], qs[p])
        for copy in first_sends(p):
            copy.start()
    for p in range(pairs):
        dv_own[0, p] = dot(probs[p, head, first_rows].astype(bf16), dxb[p])
        dk_own[0, p] = dot(d_scores[p, head, first_rows], qs[p])
        query_grad(p, 0, LANES)

    def input_grad(index, part):
        d_k = jnp.concatenate(
            [(dk_own[index, p] + dk_recv[index, p]).astype(bf16) for p in range(pairs)], axis=1
        )
        d_v = jnp.concatenate(
            [(dv_own[index, p] + dv_recv[index, p]).astype(bf16) for p in range(pairs)], axis=1
        )
        d_n1 = acc_dn[part] + dot(d_k, wqkv[1], NT) + dot(d_v, wqkv[2], NT)
        grad_buf[part] = grad_buf[part] + rms_back(x0[part], attn_gain, d_n1)

    acc_dn[first_rows] = dot(att_t[:, first_rows].T, wqkv[0], NT)
    for p in range(pairs):
        for copy in first_sends(p):
            copy.wait()
    input_grad(0, first_rows)

    chunks, chunk_rows, chunk_cols = total.shape

    def forward_of(index):
        return remote(
            total.at[index], total.at[index], send4.at[index], recv4.at[index], (dp, 1)
        )

    def in_peer(k):
        target, flip = my_in, inner - k
        for bit in range(inner.bit_length() - 1):
            if flip >> bit & 1:
                target = target + (1 - 2 * lax.rem(my_in // (1 << bit), 2)) * (1 << bit)
        return target, (my_out * inner + target, head)

    def out_peer(k):
        target = lax.rem(my_out + k, outer)
        return target, (target * inner + my_in, head)

    skip = (inner - chunks) // 2

    def chunk_of(place):
        index = place - skip
        return jnp.clip(index, 0, chunks - 1), (index >= 0) & (index < chunks)

    mine_in, sums = chunk_of(my_in)

    def scatter_to(k):
        target, device = in_peer(k)
        at, holds = chunk_of(target)
        return holds, remote(rs_send.at[at], parts.at[my_in], send1.at[k], recv1.at[my_in], device)

    def scatter_from(k):
        source, device = in_peer(k)
        return remote(rs_send.at[0], parts.at[source], send1.at[k], recv1.at[source], device)

    def gather_to(k):
        return remote(
            total.at[mine_in], total.at[mine_in], send2.at[k], recv2.at[mine_in], in_peer(k)[1]
        )

    def gather_from(k):
        source, device = in_peer(k)
        at, holds = chunk_of(source)
        return holds, at, remote(total.at[at], total.at[at], send2.at[k], recv2.at[at], device)

    def across(k):
        return remote(
            across_buf.at[my_out], across_buf.at[my_out], send3.at[k], recv3.at[my_out],
            out_peer(k)[1],
        )

    def across_from(k):
        source, device = out_peer(k)
        return remote(
            across_buf.at[source], across_buf.at[source], send3.at[k], recv3.at[source], device
        )

    @pl.when(head == 0)
    def _():
        rounded = grad_buf[first_rows].astype(bf16)
        local = dot(order.astype(bf16), rounded, TN).astype(bf16)
        for c in range(chunks):
            rs_send[c] = local[c * chunk_rows : (c + 1) * chunk_rows]

        for k in range(1, inner):
            holds, copy = scatter_to(k)

            @pl.when(holds)
            def _():
                copy.start()

    for p in range(pairs):
        dv_send[1, p] = dot(probs[p, far, last_rows].astype(bf16), dxb[p])
        dk_send[1, p] = dot(d_scores[p, far, last_rows], qs[p])
    for copy in last_sends:
        copy.start()
    for p in range(pairs):
        dv_own[1, p] = dot(probs[p, head, last_rows].astype(bf16), dxb[p])
        dk_own[1, p] = dot(d_scores[p, head, last_rows], qs[p])
        query_grad(p, LANES, share)
    for i in range(ff // ff_block):
        out_buf[...] = out_buf[...] + dot(act[i], wdown[i * ff_block : (i + 1) * ff_block, :])
    out_low[...] = out_buf[...].astype(bf16)
    out_copy = pltpu.make_async_copy(out_low, out_hbm, out_sem.at[0])
    out_copy.start()

    @pl.when((head == 0) & sums)
    def _():
        parts[my_in] = rs_send[mine_in]
        for k in range(1, inner):
            scatter_from(k).wait_recv()
        summed = parts[0].astype(f32)
        for source in range(1, inner):
            summed = summed + parts[source].astype(f32)
        if outer > 1:
            across_buf[my_out] = summed
            for k in range(1, outer):
                across(k).start()
            for k in range(1, outer):
                across_from(k).wait_recv()
            summed = across_buf[0]
            for source in range(1, outer):
                summed = summed + across_buf[source]
            for k in range(1, outer):
                across(k).wait_send()
        total[mine_in] = summed.astype(bf16)
        for k in range(1, inner):
            gather_to(k).start()
        forward_of(mine_in).start()

    acc_dn[last_rows] = dot(att_t[:, last_rows].T, wqkv[0], NT)
    for copy in last_sends:
        copy.wait()
    input_grad(1, last_rows)
    grad_copy = pltpu.make_async_copy(grad_buf, grad_hbm, out_sem.at[1])
    grad_copy.start()

    @pl.when(head == 0)
    def _():
        for k in range(1, inner):
            holds, at, copy = gather_from(k)

            @pl.when(holds)
            def _():
                copy.wait_recv()
                forward_of(at).start()

    @pl.when(head == 1)
    def _():
        for index in range(chunks):
            forward_of(index).wait_recv()

    total_copy = pltpu.make_async_copy(total, total_hbm, out_sem.at[2])
    total_copy.start()

    each(groups - 1, lambda k: request_to(k).wait_send())
    each(groups - 1, lambda k: row_to(peer_of(k)).wait_send())

    @pl.when(head == 0)
    def _():
        for k in range(1, inner):
            holds, copy = scatter_to(k)

            @pl.when(holds)
            def _():
                copy.wait_send()

        @pl.when(sums)
        def _():
            for k in range(1, inner):
                gather_to(k).wait_send()

        for index in range(chunks):
            forward_of(index).wait_send()

    out_copy.wait()
    grad_copy.wait()
    total_copy.wait()


def vmem(*shape, dtype=f32):
    return pltpu.VMEM(shape, dtype)


def run_layer(
    groups, valid, ids, segments, ag, fg, rel, prompt, cot, table, wqkv, wout, win, wdown
):
    share, width = cot.shape
    ff = 2 * win.shape[1]
    slot = 2 * share
    pairs = width // LANES
    rows = prompt.shape[0]
    ff_block = 768
    capacity = max(2, 2 * slot // (2 * groups))
    block = -(-capacity // 16) * 16
    inner = math.gcd(groups, 16)
    outer = groups // inner
    chunk_rows, chunk_cols = 16, width
    chunks = -(-rows // chunk_rows)
    in_vmem = pl.BlockSpec(memory_space=pltpu.VMEM)
    in_hbm = pl.BlockSpec(memory_space=pl.ANY)
    dma = pltpu.SemaphoreType.DMA
    return pl.pallas_call(
        functools.partial(layer_kernel, groups, inner, block, rows),
        out_shape=(
            jax.ShapeDtypeStruct((share, width), bf16),
            jax.ShapeDtypeStruct((share, width), f32),
            jax.ShapeDtypeStruct((chunks, chunk_rows, chunk_cols), bf16),
        ),
        in_specs=[pl.BlockSpec(memory_space=pltpu.SMEM)] + [in_hbm] * 12,
        out_specs=[in_hbm] * 3,
        scratch_shapes=[
            vmem(*ids.shape, dtype=jnp.int32),
            vmem(*segments.shape, dtype=jnp.int32),
            vmem(*ag.shape),
            vmem(*fg.shape),
            vmem(*rel.shape, dtype=bf16),
            vmem(*table.shape, dtype=bf16),
            vmem(3, width, width, dtype=bf16),
            vmem(width, width, dtype=bf16),
            vmem(width, ff, dtype=bf16),
            vmem(ff, width, dtype=bf16),
            vmem(groups, 1, LANES),
            vmem(groups, 1, LANES),
            vmem(groups, block, width, dtype=bf16),
            vmem(groups, block, width, dtype=bf16),
            vmem(2, 8, LANES),
            vmem(rows, width),
            vmem(LANES, width),
            vmem(share, width, dtype=bf16),
            vmem(1, slot, dtype=jnp.int32),
            vmem(1, slot),
            vmem(2, share, LANES, dtype=bf16),
            vmem(share, LANES, dtype=bf16),
            vmem(share, width),
            vmem(LANES, width),
            vmem(ff // ff_block, share, ff_block),
            vmem(ff // ff_block, share, ff_block, dtype=bf16),
            vmem(pairs, 2, share, slot, dtype=bf16),
            vmem(share, width),
            vmem(share, width),
            vmem(2, share, width, dtype=bf16),
            vmem(2, share, width, dtype=bf16),
            vmem(2, width, share, dtype=bf16),
            vmem(2, width, share, dtype=bf16),
            vmem(pairs, slot, LANES, dtype=bf16),
            vmem(2 * pairs, 5, LANES, LANES),
            vmem(pairs, 2, share, slot),
            vmem(width, share, dtype=bf16),
            vmem(share, width),
            vmem(share, width, dtype=bf16),
        ]
        + [vmem(2, pairs, LANES, LANES)] * 6
        + [
            vmem(pairs, slot, LANES, dtype=bf16),
            vmem(chunks, chunk_rows, chunk_cols, dtype=bf16),
            vmem(inner, chunk_rows, chunk_cols, dtype=bf16),
            vmem(outer, chunk_rows, chunk_cols),
            vmem(chunks, chunk_rows, chunk_cols, dtype=bf16),
            dma((12,)),
            dma((5,)),
            dma((5,)),
            dma((groups,)),
            dma((groups,)),
            dma((groups,)),
            dma((groups,)),
            dma((2,)),
            dma((2,)),
            dma((2, pairs + 1)),
            dma((2, pairs + 1)),
            dma((inner,)),
            dma((inner,)),
            dma((inner,)),
            dma((inner,)),
            dma((outer,)),
            dma((outer,)),
            dma((chunks,)),
            dma((chunks,)),
            dma((3,)),
        ],
        compiler_params=pltpu.CompilerParams(
            collective_id=1, has_side_effects=True, vmem_limit_bytes=60 * 2**20
        ),
        name="layer",
    )(valid, ids, segments, ag, fg, rel, prompt, cot, table, wqkv, wout, win, wdown)


def finish_kernel(
    clip_at, prompt_hbm, first_hbm, second_hbm, total_hbm, out_hbm, grad_hbm,
    *refs,
):
    results, (prompt_ref, first_ref, second_ref, total_ref, out_buf, grad_buf), (
        grad_ref, norm_ref, new_ref, first_out_ref, second_out_ref, low_ref,
    ), (load_sem, store_sem) = refs[:8], refs[8:14], refs[14:20], refs[20:]
    loads = [
        pltpu.make_async_copy(src, dst, load_sem.at[i])
        for i, (src, dst) in enumerate(
            (
                (total_hbm, total_ref), (first_hbm, first_ref), (second_hbm, second_ref),
                (prompt_hbm, prompt_ref), (out_hbm, out_buf), (grad_hbm, grad_buf),
            )
        )
    ]
    for copy in loads:
        copy.start()
    stores = []

    def store(src, index):
        stores.append(pltpu.make_async_copy(src, results[index], store_sem.at[index]))
        stores[-1].start()

    rows = prompt_ref.shape[0]
    loads[0].wait()
    summed = total_ref[...].reshape(-1, total_ref.shape[2]).astype(f32)[:rows]
    grad_ref[...] = summed
    store(grad_ref, 2)
    norm = jnp.sqrt(jnp.sum(summed * summed, keepdims=True))
    norm_ref[...] = norm
    store(norm_ref, 3)
    clipped = summed * jnp.minimum(1.0, clip_at / (norm + 1e-06))
    loads[1].wait()
    first_out = first_decay * first_ref[...] + (1.0 - first_decay) * clipped
    first_out_ref[...] = first_out
    store(first_out_ref, 5)
    loads[2].wait()
    second_out = second_decay * second_ref[...] + (1.0 - second_decay) * clipped * clipped
    second_out_ref[...] = second_out
    store(second_out_ref, 6)
    loads[4].wait()
    store(out_buf, 0)
    loads[5].wait()
    store(grad_buf, 1)
    first_hat = first_out / (1.0 - first_decay**STEP)
    second_hat = second_out / (1.0 - second_decay**STEP)
    loads[3].wait()
    prompt = prompt_ref[...]
    new = prompt - learn_rate * (
        first_hat / (jnp.sqrt(second_hat) + adam_epsilon) + weight_decay * prompt
    )
    new_ref[...] = new
    store(new_ref, 4)
    low_ref[...] = new.astype(bf16)
    store(low_ref, 7)
    for copy in stores:
        copy.wait()


def run_finish(clip_at, total, prompt, first, second, out, grad):
    rows, width = prompt.shape
    shape = jax.ShapeDtypeStruct((rows, width), f32)
    in_hbm = pl.BlockSpec(memory_space=pl.ANY)
    return pl.pallas_call(
        functools.partial(finish_kernel, clip_at),
        out_shape=(
            jax.ShapeDtypeStruct(out.shape, out.dtype),
            jax.ShapeDtypeStruct(grad.shape, grad.dtype),
            shape,
            jax.ShapeDtypeStruct((1, 1), f32),
            shape,
            shape,
            shape,
            jax.ShapeDtypeStruct((rows, width), bf16),
        ),
        in_specs=[in_hbm] * 6,
        out_specs=[in_hbm] * 8,
        scratch_shapes=[
            vmem(rows, width),
            vmem(rows, width),
            vmem(rows, width),
            vmem(*total.shape, dtype=bf16),
            vmem(*out.shape, dtype=bf16),
            vmem(*grad.shape),
            vmem(rows, width),
            vmem(1, 1),
            vmem(rows, width),
            vmem(rows, width),
            vmem(rows, width),
            vmem(rows, width, dtype=bf16),
            pltpu.SemaphoreType.DMA((6,)),
            pltpu.SemaphoreType.DMA((8,)),
        ],
        compiler_params=pltpu.CompilerParams(vmem_limit_bytes=63 * 2**20),
        name="finish",
    )(prompt, first, second, total, out, grad)


def per_device(
    ids,
    segments,
    valid_rows,
    prompt,
    table,
    attn_gain,
    w_qkv,
    rel_bias,
    w_out,
    ff_gain,
    w_in,
    w_down,
    cotangent,
    first_moment,
    second_moment,
):
    groups = lax.axis_size("dp")
    rows, width = prompt.shape
    out, grad, total = run_layer(
        groups, valid_rows, ids, segments, attn_gain, ff_gain, rel_bias.T, prompt, cotangent, table,
        jnp.transpose(w_qkv, (1, 0, 2)), w_out, w_in, w_down,
    )
    clip_at = clip_share * math.sqrt(rows * width * groups)
    final, d_start, prompt_grad, norm, prompt_new, first_out, second_out, low = run_finish(
        clip_at, total, prompt, first_moment, second_moment, out, grad
    )
    return (final, d_start, prompt_grad, norm[0, 0], prompt_new, first_out, second_out, low)


def solution(mesh):
    in_specs = (
        P("dp", None),
        P("dp", None),
        P("dp"),
        P(),
        P("dp", None),
        P(),
        P(None, None, "head"),
        P(None, "head"),
        P("head", None),
        P(),
        P(None, "head"),
        P("head", None),
        P(("dp", "head"), None),
        P(),
        P(),
    )
    out_specs = (P(("dp", "head"), None), P(("dp", "head"), None), P(), P(), P(), P(), P(), P())
    return jax.shard_map(
        per_device, mesh=mesh, in_specs=in_specs, out_specs=out_specs, check_vma=False
    )
```

```python
import functools
import math

import jax
import jax.numpy as jnp
from jax import lax
from jax.experimental import pallas as pl
from jax.experimental.pallas import tpu as pltpu
from jax.sharding import PartitionSpec as P

STEP = 10
norm_epsilon = 1e-06
thresholds = (12, 16, 23, 32, 46, 64, 91)
masked_score = -1000000000.0
learn_rate = 0.5
first_decay = 0.5
second_decay = 0.75
weight_decay = 0.01
adam_epsilon = 1e-08
clip_share = 0.05
exact_mode = lax.Precision.HIGHEST
MESH = pl.DeviceIdType.MESH
LANES = 128
NT = (((1,), (1,)), ((), ()))
NN = (((1,), (0,)), ((), ()))
TN = (((0,), (0,)), ((), ()))
f32 = jnp.float32
bf16 = jnp.bfloat16
GELU_C = math.sqrt(2.0 / math.pi)


def dot(left, right, dims=NN, precision=None):
    return lax.dot_general(left, right, dims, preferred_element_type=f32, precision=precision)


def rms_scale(rows, gain):
    return rows * lax.rsqrt(jnp.mean(rows * rows, axis=1, keepdims=True) + norm_epsilon) * gain


def rms_back(rows, gain, grad):
    r = lax.rsqrt(jnp.mean(rows * rows, axis=1, keepdims=True) + norm_epsilon)
    scaled = grad * gain
    return r * scaled - rows * (r * r * r * jnp.mean(rows * scaled, axis=1, keepdims=True))


def bucket_of(relative):
    magnitude = jnp.abs(relative)
    larger = 8 + sum(((magnitude >= cutoff).astype(jnp.int32) for cutoff in thresholds))
    return jnp.where(magnitude < 8, magnitude, larger) + 16 * (relative > 0).astype(jnp.int32)


def each(count, body):
    if count <= 16:
        for i in range(count):
            body(i)
    else:
        lax.fori_loop(0, count, lambda i, carry: (body(i), carry)[1], 0)


def layer_kernel(
    groups, inner, block, rows,
    valid_ref, ids_hbm, seg_hbm, ag_hbm, fg_hbm, rel_hbm, prompt_hbm, cot_hbm, table_hbm, wqkv_hbm, wout_hbm, win_hbm, wdown_hbm,
    out_hbm, grad_hbm, total_hbm,
    ids_ref, seg_ref, ag_ref, fg_ref, rel_ref,
    table, wqkv, wout, win, wdown,
    req_out, req_in, found, fetched, rel_all, prompt_in, prompt_pad, cot, seg_pad, seg_here, mask_k, mask_q,
    x0, x0_prompt, d_act, act, d_scores, out_buf, grad_buf,
    k_all, v_all, kt, vt, qs, bias, probs, att_t, acc_dn, out_low,
    dk_own, dv_own, dk_send, dv_send, dk_recv, dv_recv, dxb,
    rs_send, parts, across_buf, total,
    load_sem, far_send, far_recv, req_send, req_recv, row_send, row_recv,
    kv_send, kv_recv, dkv_send, dkv_recv,
    send1, recv1, send2, recv2, send3, recv3, send4, recv4, out_sem,
):
    dp = lax.axis_index("dp")
    head = lax.axis_index("head")
    other = (dp, 1 - head)
    share, width = x0.shape
    slot = 2 * share
    pairs = width // LANES
    half_width = width // 2
    ff = win.shape[1]
    half_ff = ff // 2
    ff_block = d_act.shape[2]
    vocab = table.shape[0]
    spots = groups * block
    outer = groups // inner
    my_in = lax.rem(dp, inner)
    my_out = dp // inner
    mine = pl.ds(pl.multiple_of(head * share, share), share)

    def remote(src, dst, send, recv, device):
        return pltpu.make_async_remote_copy(
            src, dst, send, recv, device_id=device, device_id_type=MESH
        )

    barrier = pltpu.get_barrier_semaphore()

    def peer_of(k):
        if groups > 16:
            return lax.rem(dp + 1 + k, groups)
        flip, peer = groups - 1 - k, dp
        for bit in range(groups.bit_length() - 1):
            if flip >> bit & 1:
                peer = peer + (1 - 2 * lax.rem(dp // (1 << bit), 2)) * (1 << bit)
        return peer

    def greet(k):
        pl.semaphore_signal(barrier, inc=1, device_id=(peer_of(k), head), device_id_type=MESH)

    each(groups - 1, greet)
    pl.semaphore_signal(barrier, inc=1, device_id=other, device_id_type=MESH)

    small_copies = [
        pltpu.make_async_copy(src, dst, load_sem.at[7 + i])
        for i, (src, dst) in enumerate(
            (
                (ids_hbm, ids_ref), (seg_hbm, seg_ref), (rel_hbm, rel_ref), (ag_hbm, ag_ref),
                (fg_hbm, fg_ref),
            )
        )
    ]
    for copy in small_copies:
        copy.start()
    my_cols = pl.ds(pl.multiple_of(head * half_width, half_width), half_width)
    my_ff = pl.ds(pl.multiple_of(head * half_ff, half_ff), half_ff)
    weight_pairs = (
        (wdown_hbm, wdown.at[my_ff, :]),
        (wqkv_hbm, wqkv.at[:, :, my_cols]),
        (wout_hbm, wout.at[my_cols, :]),
        (win_hbm, win.at[:, my_ff]),
    )
    cot_copy = pltpu.make_async_copy(cot_hbm, cot, load_sem.at[4])
    cot_copy.start()
    table_copy = pltpu.make_async_copy(table_hbm, table, load_sem.at[5])
    table_copy.start()
    local_copies = [
        pltpu.make_async_copy(src, dst, load_sem.at[i]) for i, (src, dst) in enumerate(weight_pairs)
    ]
    for copy in local_copies:
        copy.start()
    prompt_copy = pltpu.make_async_copy(prompt_hbm, prompt_in, load_sem.at[6])
    prompt_copy.start()
    far_copies = [
        remote(src, dst, far_send.at[i], far_recv.at[i], other)
        for i, (src, dst) in enumerate(weight_pairs)
    ]

    lane = lax.broadcasted_iota(jnp.int32, (share, LANES), 1)
    row = lax.broadcasted_iota(jnp.int32, (share, LANES), 0) + head * share
    lane_f = lane.astype(f32)
    small_copies[0].wait()
    row_ids = ids_ref[:, mine].astype(f32)
    ids_col = jnp.concatenate(
        [
            jnp.broadcast_to(row_ids[:, i * LANES : (i + 1) * LANES], (LANES, LANES)).T
            for i in range(share // LANES)
        ],
        axis=0,
    )
    is_text = row >= rows
    owner = jnp.where(is_text, jnp.floor((ids_col + 0.5) * (1.0 / vocab)), -1.0)
    hot = (owner == lane_f).astype(f32)
    tri_row = lax.broadcasted_iota(jnp.int32, (share, share), 0)
    tri_col = lax.broadcasted_iota(jnp.int32, (share, share), 1)
    earlier = (tri_row > tri_col).astype(f32).astype(bf16)
    rank = jnp.sum(dot(earlier, hot.astype(bf16)) * hot, axis=1, keepdims=True)
    place = jnp.where(is_text[:, :1], owner[:, :1] * block + rank, -1.0)
    ranked = (rank == lane_f).astype(f32)
    wanted = dot(hot * (ids_col - owner * vocab), ranked, TN, exact_mode)
    for o in range(groups):
        req_out[o] = wanted[o : o + 1, :]

    order = jnp.where(is_text[:LANES], 0.0, (ids_col[:LANES] == lane_f[:LANES]).astype(f32))

    small_copies[2].wait()
    rel_all[head] = jnp.zeros((8, LANES), f32)
    rel_all[head, : rel_ref.shape[0], : rel_ref.shape[1]] = rel_ref[...].astype(f32)

    small_copies[1].wait()
    seg_pad[:, : seg_ref.shape[1]] = seg_ref[...]
    lanes_slot = lax.broadcasted_iota(jnp.int32, (1, slot), 1)
    seg_row = jnp.where(lanes_slot < rows, -1, pltpu.roll(seg_pad[...], rows, 1)).astype(f32)
    seg_here[...] = seg_row
    limit = valid_ref[0] + rows
    square_lane = lax.broadcasted_iota(jnp.int32, (LANES, LANES), 1).astype(f32) - 1.0
    square_row = lax.broadcasted_iota(jnp.int32, (LANES, LANES), 0)
    for qb in range(share // LANES):
        spot = pl.ds(pl.multiple_of(head * share + qb * LANES, LANES), LANES)
        seg_col = jnp.broadcast_to(seg_here[:, spot], (LANES, LANES)).T
        mask_q[qb * LANES : (qb + 1) * LANES, :] = (
            (seg_col == square_lane).astype(f32).astype(bf16)
        )
    for kb in range(slot // LANES):
        at = kb * LANES
        seg_col = jnp.broadcast_to(seg_row[:, at : at + LANES], (LANES, LANES)).T
        same = seg_col == square_lane
        key = square_row + at
        allowed = (key < rows) | (same & (key < limit))
        mask_k[at // share, at % share : at % share + LANES, :] = jnp.where(allowed, 0.0, masked_score).astype(bf16)

    live = row[:, :1] < limit
    cot_copy.wait()
    dy = jnp.where(live, cot[...].astype(f32), 0.0).astype(bf16)

    pl.semaphore_wait(barrier, groups)
    req_in[dp] = req_out[dp]

    def request_to(k):
        peer = peer_of(k)
        return remote(
            req_out.at[peer], req_in.at[dp], req_send.at[peer], req_recv.at[dp], (peer, head)
        )

    def request_from(k):
        peer = peer_of(k)
        return remote(
            req_out.at[peer], req_in.at[peer], req_send.at[peer], req_recv.at[peer], (peer, head)
        )

    each(groups - 1, lambda k: request_to(k).start())
    rel_copy = remote(
        rel_all.at[head], rel_all.at[head], far_send.at[4], far_recv.at[4], other
    )
    rel_copy.start()
    for copy in far_copies:
        copy.start()

    local_copies[0].wait()

    def activation_grad(index):
        at = pl.ds(pl.multiple_of(index * ff_block, ff_block), ff_block)
        d_act[index] = dot(dy, wdown[at, :], NT)

    half_blocks = half_ff // ff_block
    for i in range(half_blocks):
        activation_grad(head * half_blocks + i)

    table_copy.wait()
    each(groups - 1, lambda k: request_from(k).wait_recv())
    vocab_lane = lax.broadcasted_iota(jnp.int32, (block, vocab), 1).astype(f32)
    bunch = max(4, groups // 16)
    bunches = groups // bunch
    half_bunches = bunches // 2
    half_groups = groups // 2
    side_of = dp // half_groups

    def row_to(peer):
        return remote(
            found.at[peer], fetched.at[dp], row_send.at[peer], row_recv.at[dp], (peer, head)
        )

    def row_from(peer):
        return remote(
            found.at[peer], fetched.at[peer], row_send.at[peer], row_recv.at[peer], (peer, head)
        )

    def serve(g):
        side = jnp.where(g < half_bunches, 1 - side_of, side_of)
        base = (side * half_bunches + lax.rem(g, half_bunches)) * bunch
        wants = jnp.concatenate(
            [req_in[base + j] for j in range(bunch)] + [jnp.zeros((LANES - bunch, LANES), f32)],
            axis=0,
        ).T
        picks = jnp.concatenate(
            [
                (wants[:block, j : j + 1] == vocab_lane).astype(f32).astype(bf16)
                for j in range(bunch)
            ],
            axis=0,
        )
        picked = dot(picks, table[...]).astype(bf16)
        for j in range(bunch):
            found[base + j] = picked[j * block : (j + 1) * block]

            @pl.when(base + j != dp)
            def _():
                row_to(base + j).start()

    each(bunches, serve)
    fetched[dp] = found[dp]

    prompt_copy.wait()

    prompt_pad[...] = jnp.zeros_like(prompt_pad)
    prompt_pad[:rows, :] = prompt_in[...]
    x0_prompt[...] = dot(order, prompt_pad[...], NN, exact_mode)

    rel_copy.wait()
    spread = lax.broadcasted_iota(jnp.int32, (1, 2 * LANES), 1)
    lag = jnp.where(spread >= LANES, spread - 2 * LANES, spread)
    bucket_row = lax.broadcasted_iota(jnp.int32, (LANES, 2 * LANES), 0)
    for d in range(5):
        if d == 0:
            near = jnp.full((1, 2 * LANES), 15, jnp.int32)
        elif d == 4:
            near = jnp.full((1, 2 * LANES), 31, jnp.int32)
        else:
            near = bucket_of((d - 2) * LANES - lag)
        pick = (bucket_row == near).astype(f32).astype(bf16)
        for side in range(2):
            lines = dot(rel_all[side].astype(bf16), pick)
            for h in range(pairs):
                line = jnp.broadcast_to(lines[h : h + 1, :], (LANES, 2 * LANES))
                if d not in (0, 4):
                    line = pltpu.roll(line, 0, 1, stride=1, stride_axis=0)
                bias[side * pairs + h, d] = line[:, :LANES]

    far_copies[0].wait()
    for i in range(half_blocks):
        activation_grad((1 - head) * half_blocks + i)
    for copy in local_copies[1:]:
        copy.wait()
    far_copies[1].wait()

    spot_lane = lax.broadcasted_iota(jnp.int32, (share, half_groups * block), 1).astype(f32)

    def rows_of(side):
        base = side * half_groups
        take = (place - (base * block).astype(f32) == spot_lane).astype(f32).astype(bf16)
        return dot(
            take, fetched[pl.ds(base, half_groups)].reshape(half_groups * block, width)
        )

    def near_wait(j):
        peer = side_of * half_groups + j

        @pl.when(peer != dp)
        def _():
            row_from(peer).wait_recv()

    each(half_groups, near_wait)
    near_rows = rows_of(side_of)
    x0[...] = near_rows
    x0[:LANES, :] = near_rows[:LANES] + x0_prompt[...]

    each(half_groups, lambda j: row_from((1 - side_of) * half_groups + j).wait_recv())
    x0[...] = x0[...] + rows_of(1 - side_of)

    small_copies[3].wait()
    small_copies[4].wait()
    attn_gain = ag_ref[...].reshape(1, width)
    ff_gain = fg_ref[...].reshape(1, width)
    n1 = rms_scale(x0[...], attn_gain).astype(bf16)
    k_all[head] = dot(n1, wqkv[1]).astype(bf16)
    k_copy = remote(k_all.at[head], k_all.at[head], kv_send.at[0], kv_recv.at[0], other)
    k_copy.start()
    v_all[head] = dot(n1, wqkv[2]).astype(bf16)
    v_copy = remote(v_all.at[head], v_all.at[head], kv_send.at[1], kv_recv.at[1], other)
    v_copy.start()
    q = dot(n1, wqkv[0]).astype(bf16) * jnp.asarray(0.125, bf16)
    for p in range(pairs):
        part = q[:, p * LANES : (p + 1) * LANES]
        qs[p, :share, :] = jnp.where(lane < LANES // 2, part, jnp.zeros_like(part))
        qs[p, share:, :] = jnp.where(lane >= LANES // 2, part, jnp.zeros_like(part))

    far = 1 - head
    blocks = share // LANES
    half = LANES // 2

    def raw_scores(p, side, shift):
        left = jnp.concatenate(
            [k_all[side, :, p * LANES : (p + 1) * LANES], mask_k[side]], axis=1
        )
        right = jnp.concatenate(
            [qs[p], jnp.concatenate([mask_q[...], mask_q[...]], axis=0)], axis=1
        )
        raw = dot(left, right, NT)
        bands = []
        for kb in range(blocks):
            parts_of = []
            for a in range(2):
                for qb in range(blocks):
                    apart = shift + (kb - qb)
                    if isinstance(apart, int):
                        spot = min(max(apart, -2), 2) + 2
                    else:
                        spot = jnp.clip(apart, -2, 2) + 2
                    lo = a * share + qb * LANES
                    parts_of.append(
                        raw[kb * LANES : (kb + 1) * LANES, lo : lo + LANES] + bias[2 * p + a, spot]
                    )
            bands.append(jnp.concatenate(parts_of, axis=1))
        return jnp.concatenate(bands, axis=0)

    for p in range(pairs):
        probs[p, head] = raw_scores(p, head, 0)
    kt[head] = k_all[head].T
    vt[head] = v_all[head].T
    k_copy.wait()
    kt[far] = k_all[far].T
    v_copy.wait()
    vt[far] = v_all[far].T

    far_next = raw_scores(0, far, (1 - 2 * head) * blocks)
    for p in range(pairs):
        near_raw, far_raw = probs[p, head], far_next
        if p + 1 < pairs:
            far_next = raw_scores(p + 1, far, (1 - 2 * head) * blocks)
        top = jnp.maximum(
            jnp.max(near_raw, axis=0, keepdims=True), jnp.max(far_raw, axis=0, keepdims=True)
        )
        near_exp, far_exp = jnp.exp(near_raw - top), jnp.exp(far_raw - top)
        inverse = 1.0 / (
            jnp.sum(near_exp, axis=0, keepdims=True) + jnp.sum(far_exp, axis=0, keepdims=True)
        )
        near_prob, far_prob = near_exp * inverse, far_exp * inverse
        probs[p, head] = near_prob
        probs[p, far] = far_prob
        near_low, far_low = near_prob.astype(bf16), far_prob.astype(bf16)
        for a in range(2):
            feat = slice(p * LANES + a * half, p * LANES + (a + 1) * half)
            side = slice(a * share, (a + 1) * share)
            att_t[feat, :] = (
                dot(vt[head, feat, :], near_low[:, side]) + dot(vt[far, feat, :], far_low[:, side])
            ).astype(bf16)

    far_copies[2].wait()
    x1 = x0[...] + dot(att_t[...].T, wout[...])
    n2 = rms_scale(x1, ff_gain).astype(bf16)
    far_copies[3].wait()
    out_buf[...] = x1
    d_n2 = None
    ff_blocks = ff // ff_block
    units = [slice(i * ff_block, (i + 1) * ff_block) for i in range(ff_blocks)]
    u_next = dot(n2, win[:, units[0]])
    for i in range(ff_blocks):
        u = u_next
        if i + 1 < ff_blocks:
            u_next = dot(n2, win[:, units[i + 1]])
        square = u * u
        t = jnp.tanh(u * (GELU_C + (GELU_C * 0.044715) * square))
        half_u = 0.5 * u
        act[i] = (half_u + half_u * t).astype(bf16)
        slope = (0.5 + 0.5 * t) + (half_u * (1.0 - t * t)) * (
            GELU_C + (GELU_C * 3 * 0.044715) * square
        )
        d_hidden = (d_act[i] * slope).astype(bf16)
        piece = dot(d_hidden, win[:, units[i]], NT)
        d_n2 = piece if d_n2 is None else d_n2 + piece
    dx1 = dy.astype(f32) + rms_back(x1, ff_gain, d_n2)
    grad_buf[...] = dx1
    d_att = dot(dx1.astype(bf16), wout[...], NT).astype(bf16)
    for p in range(pairs):
        part = d_att[:, p * LANES : (p + 1) * LANES]
        dxb[p, :share, :] = jnp.where(lane < LANES // 2, part, jnp.zeros_like(part))
        dxb[p, share:, :] = jnp.where(lane >= LANES // 2, part, jnp.zeros_like(part))

    def first_sends(p):
        return [
            remote(src.at[0, p], dst.at[0, p], dkv_send.at[i, p], dkv_recv.at[i, p], other)
            for i, (src, dst) in enumerate(((dk_send, dk_recv), (dv_send, dv_recv)))
        ]

    last_sends = [
        remote(src.at[1], dst.at[1], dkv_send.at[i, pairs], dkv_recv.at[i, pairs], other)
        for i, (src, dst) in enumerate(((dk_send, dk_recv), (dv_send, dv_recv)))
    ]
    first_rows, last_rows = slice(0, LANES), slice(LANES, share)

    def query_grad(p, begin, end):
        for a in range(2):
            feat = slice(p * LANES + a * half, p * LANES + (a + 1) * half)
            side = slice(a * share + begin, a * share + end)
            att_t[feat, begin:end] = (
                (
                    dot(kt[head, feat, :], d_scores[p, head, :, side])
                    + dot(kt[far, feat, :], d_scores[p, far, :, side])
                )
                * 0.125
            ).astype(bf16)

    def prob_grads(p):
        cols = slice(p * LANES, (p + 1) * LANES)
        return [dot(v_all[side, :, cols], dxb[p], NT) for side in (head, far)]

    d_next = prob_grads(0)
    for p in range(pairs):
        d_out = dxb[p]
        near_d, far_d = d_next
        if p + 1 < pairs:
            d_next = prob_grads(p + 1)
        near_prob, far_prob = probs[p, head], probs[p, far]
        delta = jnp.sum(near_prob * near_d, axis=0, keepdims=True) + jnp.sum(
            far_prob * far_d, axis=0, keepdims=True
        )
        far_score = (far_prob * (far_d - delta)).astype(bf16)
        d_scores[p, far] = far_score
        d_scores[p, head] = (near_prob * (near_d - delta)).astype(bf16)
        dv_send[0, p] = dot(far_prob[first_rows].astype(bf16), d_out)
        dk_send[0, p] = dot(far_score[first_rows], qs[p])
        for copy in first_sends(p):
            copy.start()
    for p in range(pairs):
        dv_own[0, p] = dot(probs[p, head, first_rows].astype(bf16), dxb[p])
        dk_own[0, p] = dot(d_scores[p, head, first_rows], qs[p])
        query_grad(p, 0, LANES)

    def input_grad(index, part):
        d_k = jnp.concatenate(
            [(dk_own[index, p] + dk_recv[index, p]).astype(bf16) for p in range(pairs)], axis=1
        )
        d_v = jnp.concatenate(
            [(dv_own[index, p] + dv_recv[index, p]).astype(bf16) for p in range(pairs)], axis=1
        )
        d_n1 = acc_dn[part] + dot(d_k, wqkv[1], NT) + dot(d_v, wqkv[2], NT)
        grad_buf[part] = grad_buf[part] + rms_back(x0[part], attn_gain, d_n1)

    acc_dn[first_rows] = dot(att_t[:, first_rows].T, wqkv[0], NT)
    for p in range(pairs):
        for copy in first_sends(p):
            copy.wait()
    input_grad(0, first_rows)

    chunks, chunk_rows, chunk_cols = total.shape

    def forward_of(index):
        return remote(
            total.at[index], total.at[index], send4.at[index], recv4.at[index], (dp, 1)
        )

    def in_peer(k):
        target, flip = my_in, inner - k
        for bit in range(inner.bit_length() - 1):
            if flip >> bit & 1:
                target = target + (1 - 2 * lax.rem(my_in // (1 << bit), 2)) * (1 << bit)
        return target, (my_out * inner + target, head)

    def out_peer(k):
        target = lax.rem(my_out + k, outer)
        return target, (target * inner + my_in, head)

    skip = (inner - chunks) // 2

    def chunk_of(place):
        index = place - skip
        return jnp.clip(index, 0, chunks - 1), (index >= 0) & (index < chunks)

    mine_in, sums = chunk_of(my_in)

    def scatter_to(k):
        target, device = in_peer(k)
        at, holds = chunk_of(target)
        return holds, remote(rs_send.at[at], parts.at[my_in], send1.at[k], recv1.at[my_in], device)

    def scatter_from(k):
        source, device = in_peer(k)
        return remote(rs_send.at[0], parts.at[source], send1.at[k], recv1.at[source], device)

    def gather_to(k):
        return remote(
            total.at[mine_in], total.at[mine_in], send2.at[k], recv2.at[mine_in], in_peer(k)[1]
        )

    def gather_from(k):
        source, device = in_peer(k)
        at, holds = chunk_of(source)
        return holds, at, remote(total.at[at], total.at[at], send2.at[k], recv2.at[at], device)

    def across(k):
        return remote(
            across_buf.at[my_out], across_buf.at[my_out], send3.at[k], recv3.at[my_out],
            out_peer(k)[1],
        )

    def across_from(k):
        source, device = out_peer(k)
        return remote(
            across_buf.at[source], across_buf.at[source], send3.at[k], recv3.at[source], device
        )

    @pl.when(head == 0)
    def _():
        rounded = grad_buf[first_rows].astype(bf16)
        local = dot(order.astype(bf16), rounded, TN).astype(bf16)
        for c in range(chunks):
            rs_send[c] = local[c * chunk_rows : (c + 1) * chunk_rows]

        for k in range(1, inner):
            holds, copy = scatter_to(k)

            @pl.when(holds)
            def _():
                copy.start()

    for p in range(pairs):
        dv_send[1, p] = dot(probs[p, far, last_rows].astype(bf16), dxb[p])
        dk_send[1, p] = dot(d_scores[p, far, last_rows], qs[p])
    for copy in last_sends:
        copy.start()
    for p in range(pairs):
        dv_own[1, p] = dot(probs[p, head, last_rows].astype(bf16), dxb[p])
        dk_own[1, p] = dot(d_scores[p, head, last_rows], qs[p])
        query_grad(p, LANES, share)
    for i in range(ff // ff_block):
        out_buf[...] = out_buf[...] + dot(act[i], wdown[i * ff_block : (i + 1) * ff_block, :])
    out_low[...] = out_buf[...].astype(bf16)
    out_copy = pltpu.make_async_copy(out_low, out_hbm, out_sem.at[0])
    out_copy.start()

    @pl.when((head == 0) & sums)
    def _():
        parts[my_in] = rs_send[mine_in]
        for k in range(1, inner):
            scatter_from(k).wait_recv()
        summed = parts[0].astype(f32)
        for source in range(1, inner):
            summed = summed + parts[source].astype(f32)
        if outer > 1:
            across_buf[my_out] = summed
            for k in range(1, outer):
                across(k).start()
            for k in range(1, outer):
                across_from(k).wait_recv()
            summed = across_buf[0]
            for source in range(1, outer):
                summed = summed + across_buf[source]
            for k in range(1, outer):
                across(k).wait_send()
        total[mine_in] = summed.astype(bf16)
        for k in range(1, inner):
            gather_to(k).start()
        forward_of(mine_in).start()

    acc_dn[last_rows] = dot(att_t[:, last_rows].T, wqkv[0], NT)
    for copy in last_sends:
        copy.wait()
    input_grad(1, last_rows)
    grad_copy = pltpu.make_async_copy(grad_buf, grad_hbm, out_sem.at[1])
    grad_copy.start()

    @pl.when(head == 0)
    def _():
        for k in range(1, inner):
            holds, at, copy = gather_from(k)

            @pl.when(holds)
            def _():
                copy.wait_recv()
                forward_of(at).start()

    @pl.when(head == 1)
    def _():
        for index in range(chunks):
            forward_of(index).wait_recv()

    total_copy = pltpu.make_async_copy(total, total_hbm, out_sem.at[2])
    total_copy.start()

    each(groups - 1, lambda k: request_to(k).wait_send())
    each(groups - 1, lambda k: row_to(peer_of(k)).wait_send())

    @pl.when(head == 0)
    def _():
        for k in range(1, inner):
            holds, copy = scatter_to(k)

            @pl.when(holds)
            def _():
                copy.wait_send()

        @pl.when(sums)
        def _():
            for k in range(1, inner):
                gather_to(k).wait_send()

        for index in range(chunks):
            forward_of(index).wait_send()

    out_copy.wait()
    grad_copy.wait()
    total_copy.wait()


def vmem(*shape, dtype=f32):
    return pltpu.VMEM(shape, dtype)


def run_layer(
    groups, valid, ids, segments, ag, fg, rel, prompt, cot, table, wqkv, wout, win, wdown
):
    share, width = cot.shape
    ff = 2 * win.shape[1]
    slot = 2 * share
    pairs = width // LANES
    rows = prompt.shape[0]
    ff_block = 768
    capacity = max(2, 2 * slot // (2 * groups))
    block = -(-capacity // 16) * 16
    inner = math.gcd(groups, 16)
    outer = groups // inner
    chunk_rows, chunk_cols = 16, width
    chunks = -(-rows // chunk_rows)
    in_vmem = pl.BlockSpec(memory_space=pltpu.VMEM)
    in_hbm = pl.BlockSpec(memory_space=pl.ANY)
    dma = pltpu.SemaphoreType.DMA
    return pl.pallas_call(
        functools.partial(layer_kernel, groups, inner, block, rows),
        out_shape=(
            jax.ShapeDtypeStruct((share, width), bf16),
            jax.ShapeDtypeStruct((share, width), f32),
            jax.ShapeDtypeStruct((chunks, chunk_rows, chunk_cols), bf16),
        ),
        in_specs=[pl.BlockSpec(memory_space=pltpu.SMEM)] + [in_hbm] * 12,
        out_specs=[in_hbm] * 3,
        scratch_shapes=[
            vmem(*ids.shape, dtype=jnp.int32),
            vmem(*segments.shape, dtype=jnp.int32),
            vmem(*ag.shape),
            vmem(*fg.shape),
            vmem(*rel.shape, dtype=bf16),
            vmem(*table.shape, dtype=bf16),
            vmem(3, width, width, dtype=bf16),
            vmem(width, width, dtype=bf16),
            vmem(width, ff, dtype=bf16),
            vmem(ff, width, dtype=bf16),
            vmem(groups, 1, LANES),
            vmem(groups, 1, LANES),
            vmem(groups, block, width, dtype=bf16),
            vmem(groups, block, width, dtype=bf16),
            vmem(2, 8, LANES),
            vmem(rows, width),
            vmem(LANES, width),
            vmem(share, width, dtype=bf16),
            vmem(1, slot, dtype=jnp.int32),
            vmem(1, slot),
            vmem(2, share, LANES, dtype=bf16),
            vmem(share, LANES, dtype=bf16),
            vmem(share, width),
            vmem(LANES, width),
            vmem(ff // ff_block, share, ff_block),
            vmem(ff // ff_block, share, ff_block, dtype=bf16),
            vmem(pairs, 2, share, slot, dtype=bf16),
            vmem(share, width),
            vmem(share, width),
            vmem(2, share, width, dtype=bf16),
            vmem(2, share, width, dtype=bf16),
            vmem(2, width, share, dtype=bf16),
            vmem(2, width, share, dtype=bf16),
            vmem(pairs, slot, LANES, dtype=bf16),
            vmem(2 * pairs, 5, LANES, LANES),
            vmem(pairs, 2, share, slot),
            vmem(width, share, dtype=bf16),
            vmem(share, width),
            vmem(share, width, dtype=bf16),
        ]
        + [vmem(2, pairs, LANES, LANES)] * 6
        + [
            vmem(pairs, slot, LANES, dtype=bf16),
            vmem(chunks, chunk_rows, chunk_cols, dtype=bf16),
            vmem(inner, chunk_rows, chunk_cols, dtype=bf16),
            vmem(outer, chunk_rows, chunk_cols),
            vmem(chunks, chunk_rows, chunk_cols, dtype=bf16),
            dma((12,)),
            dma((5,)),
            dma((5,)),
            dma((groups,)),
            dma((groups,)),
            dma((groups,)),
            dma((groups,)),
            dma((2,)),
            dma((2,)),
            dma((2, pairs + 1)),
            dma((2, pairs + 1)),
            dma((inner,)),
            dma((inner,)),
            dma((inner,)),
            dma((inner,)),
            dma((outer,)),
            dma((outer,)),
            dma((chunks,)),
            dma((chunks,)),
            dma((3,)),
        ],
        compiler_params=pltpu.CompilerParams(
            collective_id=1, has_side_effects=True, vmem_limit_bytes=60 * 2**20
        ),
        name="layer",
    )(valid, ids, segments, ag, fg, rel, prompt, cot, table, wqkv, wout, win, wdown)


def finish_kernel(
    clip_at, prompt_hbm, first_hbm, second_hbm, total_hbm, out_hbm, grad_hbm,
    *refs,
):
    results, (prompt_ref, first_ref, second_ref, total_ref, out_buf, grad_buf), (
        grad_ref, norm_ref, new_ref, first_out_ref, second_out_ref, low_ref,
    ), (load_sem, store_sem) = refs[:8], refs[8:14], refs[14:20], refs[20:]
    loads = [
        pltpu.make_async_copy(src, dst, load_sem.at[i])
        for i, (src, dst) in enumerate(
            (
                (total_hbm, total_ref), (first_hbm, first_ref), (second_hbm, second_ref),
                (prompt_hbm, prompt_ref), (out_hbm, out_buf), (grad_hbm, grad_buf),
            )
        )
    ]
    for copy in loads:
        copy.start()
    stores = []

    def store(src, index):
        stores.append(pltpu.make_async_copy(src, results[index], store_sem.at[index]))
        stores[-1].start()

    rows = prompt_ref.shape[0]
    loads[0].wait()
    summed = total_ref[...].reshape(-1, total_ref.shape[2]).astype(f32)[:rows]
    grad_ref[...] = summed
    store(grad_ref, 2)
    norm = jnp.sqrt(jnp.sum(summed * summed, keepdims=True))
    norm_ref[...] = norm
    store(norm_ref, 3)
    clipped = summed * jnp.minimum(1.0, clip_at / (norm + 1e-06))
    loads[1].wait()
    first_out = first_decay * first_ref[...] + (1.0 - first_decay) * clipped
    first_out_ref[...] = first_out
    store(first_out_ref, 5)
    loads[2].wait()
    second_out = second_decay * second_ref[...] + (1.0 - second_decay) * clipped * clipped
    second_out_ref[...] = second_out
    store(second_out_ref, 6)
    loads[4].wait()
    store(out_buf, 0)
    loads[5].wait()
    store(grad_buf, 1)
    first_hat = first_out / (1.0 - first_decay**STEP)
    second_hat = second_out / (1.0 - second_decay**STEP)
    loads[3].wait()
    prompt = prompt_ref[...]
    new = prompt - learn_rate * (
        first_hat / (jnp.sqrt(second_hat) + adam_epsilon) + weight_decay * prompt
    )
    new_ref[...] = new
    store(new_ref, 4)
    low_ref[...] = new.astype(bf16)
    store(low_ref, 7)
    for copy in stores:
        copy.wait()


def run_finish(clip_at, total, prompt, first, second, out, grad):
    rows, width = prompt.shape
    shape = jax.ShapeDtypeStruct((rows, width), f32)
    in_hbm = pl.BlockSpec(memory_space=pl.ANY)
    return pl.pallas_call(
        functools.partial(finish_kernel, clip_at),
        out_shape=(
            jax.ShapeDtypeStruct(out.shape, out.dtype),
            jax.ShapeDtypeStruct(grad.shape, grad.dtype),
            shape,
            jax.ShapeDtypeStruct((1, 1), f32),
            shape,
            shape,
            shape,
            jax.ShapeDtypeStruct((rows, width), bf16),
        ),
        in_specs=[in_hbm] * 6,
        out_specs=[in_hbm] * 8,
        scratch_shapes=[
            vmem(rows, width),
            vmem(rows, width),
            vmem(rows, width),
            vmem(*total.shape, dtype=bf16),
            vmem(*out.shape, dtype=bf16),
            vmem(*grad.shape),
            vmem(rows, width),
            vmem(1, 1),
            vmem(rows, width),
            vmem(rows, width),
            vmem(rows, width),
            vmem(rows, width, dtype=bf16),
            pltpu.SemaphoreType.DMA((6,)),
            pltpu.SemaphoreType.DMA((8,)),
        ],
        compiler_params=pltpu.CompilerParams(vmem_limit_bytes=63 * 2**20),
        name="finish",
    )(prompt, first, second, total, out, grad)


def per_device(
    ids,
    segments,
    valid_rows,
    prompt,
    table,
    attn_gain,
    w_qkv,
    rel_bias,
    w_out,
    ff_gain,
    w_in,
    w_down,
    cotangent,
    first_moment,
    second_moment,
):
    groups = lax.axis_size("dp")
    rows, width = prompt.shape
    out, grad, total = run_layer(
        groups, valid_rows, ids, segments, attn_gain, ff_gain, rel_bias.T, prompt, cotangent, table,
        jnp.transpose(w_qkv, (1, 0, 2)), w_out, w_in, w_down,
    )
    clip_at = clip_share * math.sqrt(rows * width * groups)
    final, d_start, prompt_grad, norm, prompt_new, first_out, second_out, low = run_finish(
        clip_at, total, prompt, first_moment, second_moment, out, grad
    )
    return (final, d_start, prompt_grad, norm[0, 0], prompt_new, first_out, second_out, low)


def solution(mesh):
    in_specs = (
        P("dp", None),
        P("dp", None),
        P("dp"),
        P(),
        P("dp", None),
        P(),
        P(None, None, "head"),
        P(None, "head"),
        P("head", None),
        P(),
        P(None, "head"),
        P("head", None),
        P(("dp", "head"), None),
        P(),
        P(),
    )
    out_specs = (P(("dp", "head"), None), P(("dp", "head"), None), P(), P(), P(), P(), P(), P())
    return jax.shard_map(
        per_device, mesh=mesh, in_specs=in_specs, out_specs=out_specs, check_vma=False
    )
```

```python
import functools
import math

import jax
import jax.numpy as jnp
from jax import lax
from jax.experimental import pallas as pl
from jax.experimental.pallas import tpu as pltpu
from jax.sharding import PartitionSpec as P

STEP = 10
norm_epsilon = 1e-06
thresholds = (12, 16, 23, 32, 46, 64, 91)
masked_score = -1000000000.0
learn_rate = 0.5
first_decay = 0.5
second_decay = 0.75
weight_decay = 0.01
adam_epsilon = 1e-08
clip_share = 0.05
exact_mode = lax.Precision.HIGHEST
MESH = pl.DeviceIdType.MESH
LANES = 128
NT = (((1,), (1,)), ((), ()))
NN = (((1,), (0,)), ((), ()))
TN = (((0,), (0,)), ((), ()))
f32 = jnp.float32
bf16 = jnp.bfloat16
GELU_C = math.sqrt(2.0 / math.pi)


def dot(left, right, dims=NN, precision=None):
    return lax.dot_general(left, right, dims, preferred_element_type=f32, precision=precision)


def rms_scale(rows, gain):
    return rows * lax.rsqrt(jnp.mean(rows * rows, axis=1, keepdims=True) + norm_epsilon) * gain


def rms_back(rows, gain, grad):
    r = lax.rsqrt(jnp.mean(rows * rows, axis=1, keepdims=True) + norm_epsilon)
    scaled = grad * gain
    return r * scaled - rows * (r * r * r * jnp.mean(rows * scaled, axis=1, keepdims=True))


def bucket_of(relative):
    magnitude = jnp.abs(relative)
    larger = 8 + sum(((magnitude >= cutoff).astype(jnp.int32) for cutoff in thresholds))
    return jnp.where(magnitude < 8, magnitude, larger) + 16 * (relative > 0).astype(jnp.int32)


def each(count, body):
    if count <= 16:
        for i in range(count):
            body(i)
    else:
        lax.fori_loop(0, count, lambda i, carry: (body(i), carry)[1], 0)


def layer_kernel(
    groups, inner, block, rows,
    valid_ref, ids_hbm, seg_hbm, ag_hbm, fg_hbm, rel_hbm, prompt_hbm, cot_hbm, table_hbm, wqkv_hbm, wout_hbm, win_hbm, wdown_hbm,
    out_hbm, grad_hbm, total_hbm,
    ids_ref, seg_ref, ag_ref, fg_ref, rel_ref,
    table, wqkv, wout, win, wdown,
    req_out, req_in, found, fetched, rel_all, prompt_in, prompt_pad, cot, seg_pad, seg_here, mask_k, mask_q,
    x0, x0_prompt, d_act, act, d_scores, out_buf, grad_buf,
    k_all, v_all, kt, vt, qs, bias, probs, att_t, acc_dn, out_low,
    dk_own, dv_own, d_send, d_recv, dxb,
    rs_send, parts, across_buf, total,
    load_sem, far_send, far_recv, req_send, req_recv, row_send, row_recv,
    kv_send, kv_recv, dkv_send, dkv_recv,
    send1, recv1, send2, recv2, send3, recv3, send4, recv4, out_sem,
):
    dp = lax.axis_index("dp")
    head = lax.axis_index("head")
    other = (dp, 1 - head)
    share, width = x0.shape
    slot = 2 * share
    pairs = width // LANES
    half_width = width // 2
    ff = win.shape[1]
    half_ff = ff // 2
    ff_block = d_act.shape[2]
    vocab = table.shape[0]
    spots = groups * block
    outer = groups // inner
    my_in = lax.rem(dp, inner)
    my_out = dp // inner
    mine = pl.ds(pl.multiple_of(head * share, share), share)

    def remote(src, dst, send, recv, device):
        return pltpu.make_async_remote_copy(
            src, dst, send, recv, device_id=device, device_id_type=MESH
        )

    barrier = pltpu.get_barrier_semaphore()

    def peer_of(k):
        if groups > 16:
            return lax.rem(dp + 1 + k, groups)
        flip, peer = groups - 1 - k, dp
        for bit in range(groups.bit_length() - 1):
            if flip >> bit & 1:
                peer = peer + (1 - 2 * lax.rem(dp // (1 << bit), 2)) * (1 << bit)
        return peer

    def greet(k):
        pl.semaphore_signal(barrier, inc=1, device_id=(peer_of(k), head), device_id_type=MESH)

    each(groups - 1, greet)
    pl.semaphore_signal(barrier, inc=1, device_id=other, device_id_type=MESH)

    small_copies = [
        pltpu.make_async_copy(src, dst, load_sem.at[7 + i])
        for i, (src, dst) in enumerate(
            (
                (ids_hbm, ids_ref), (seg_hbm, seg_ref), (rel_hbm, rel_ref), (ag_hbm, ag_ref),
                (fg_hbm, fg_ref),
            )
        )
    ]
    for copy in small_copies:
        copy.start()
    my_cols = pl.ds(pl.multiple_of(head * half_width, half_width), half_width)
    my_ff = pl.ds(pl.multiple_of(head * half_ff, half_ff), half_ff)
    weight_pairs = (
        (wdown_hbm, wdown.at[my_ff, :]),
        (wqkv_hbm, wqkv.at[:, :, my_cols]),
        (wout_hbm, wout.at[my_cols, :]),
        (win_hbm, win.at[:, my_ff]),
    )
    cot_copy = pltpu.make_async_copy(cot_hbm, cot, load_sem.at[4])
    cot_copy.start()
    table_copy = pltpu.make_async_copy(table_hbm, table, load_sem.at[5])
    table_copy.start()
    local_copies = [
        pltpu.make_async_copy(src, dst, load_sem.at[i]) for i, (src, dst) in enumerate(weight_pairs)
    ]
    for copy in local_copies:
        copy.start()
    prompt_copy = pltpu.make_async_copy(prompt_hbm, prompt_in, load_sem.at[6])
    prompt_copy.start()
    far_copies = [
        remote(src, dst, far_send.at[i], far_recv.at[i], other)
        for i, (src, dst) in enumerate(weight_pairs)
    ]

    lane = lax.broadcasted_iota(jnp.int32, (share, LANES), 1)
    row = lax.broadcasted_iota(jnp.int32, (share, LANES), 0) + head * share
    lane_f = lane.astype(f32)
    small_copies[0].wait()
    row_ids = ids_ref[:, mine].astype(f32)
    ids_col = jnp.concatenate(
        [
            jnp.broadcast_to(row_ids[:, i * LANES : (i + 1) * LANES], (LANES, LANES)).T
            for i in range(share // LANES)
        ],
        axis=0,
    )
    is_text = row >= rows
    owner = jnp.where(is_text, jnp.floor((ids_col + 0.5) * (1.0 / vocab)), -1.0)
    hot = (owner == lane_f).astype(f32)
    tri_row = lax.broadcasted_iota(jnp.int32, (share, share), 0)
    tri_col = lax.broadcasted_iota(jnp.int32, (share, share), 1)
    earlier = (tri_row > tri_col).astype(f32).astype(bf16)
    rank = jnp.sum(dot(earlier, hot.astype(bf16)) * hot, axis=1, keepdims=True)
    place = jnp.where(is_text[:, :1], owner[:, :1] * block + rank, -1.0)
    ranked = (rank == lane_f).astype(f32)
    wanted = dot(hot * (ids_col - owner * vocab), ranked, TN, exact_mode)
    for o in range(groups):
        req_out[o] = wanted[o : o + 1, :]

    order = jnp.where(is_text[:LANES], 0.0, (ids_col[:LANES] == lane_f[:LANES]).astype(f32))

    small_copies[2].wait()
    rel_all[head] = jnp.zeros((8, LANES), f32)
    rel_all[head, : rel_ref.shape[0], : rel_ref.shape[1]] = rel_ref[...].astype(f32)

    small_copies[1].wait()
    seg_pad[:, : seg_ref.shape[1]] = seg_ref[...]
    lanes_slot = lax.broadcasted_iota(jnp.int32, (1, slot), 1)
    seg_row = jnp.where(lanes_slot < rows, -1, pltpu.roll(seg_pad[...], rows, 1)).astype(f32)
    seg_here[...] = seg_row
    limit = valid_ref[0] + rows
    square_lane = lax.broadcasted_iota(jnp.int32, (LANES, LANES), 1).astype(f32) - 1.0
    square_row = lax.broadcasted_iota(jnp.int32, (LANES, LANES), 0)
    for qb in range(share // LANES):
        spot = pl.ds(pl.multiple_of(head * share + qb * LANES, LANES), LANES)
        seg_col = jnp.broadcast_to(seg_here[:, spot], (LANES, LANES)).T
        mask_q[qb * LANES : (qb + 1) * LANES, :] = (
            (seg_col == square_lane).astype(f32).astype(bf16)
        )
    for kb in range(slot // LANES):
        at = kb * LANES
        seg_col = jnp.broadcast_to(seg_row[:, at : at + LANES], (LANES, LANES)).T
        same = seg_col == square_lane
        key = square_row + at
        allowed = (key < rows) | (same & (key < limit))
        mask_k[at // share, at % share : at % share + LANES, :] = jnp.where(allowed, 0.0, masked_score).astype(bf16)

    live = row[:, :1] < limit
    cot_copy.wait()
    dy = jnp.where(live, cot[...].astype(f32), 0.0).astype(bf16)

    pl.semaphore_wait(barrier, groups)
    req_in[dp] = req_out[dp]

    def request_to(k):
        peer = peer_of(k)
        return remote(
            req_out.at[peer], req_in.at[dp], req_send.at[peer], req_recv.at[dp], (peer, head)
        )

    def request_from(k):
        peer = peer_of(k)
        return remote(
            req_out.at[peer], req_in.at[peer], req_send.at[peer], req_recv.at[peer], (peer, head)
        )

    each(groups - 1, lambda k: request_to(k).start())
    rel_copy = remote(
        rel_all.at[head], rel_all.at[head], far_send.at[4], far_recv.at[4], other
    )
    rel_copy.start()
    for copy in far_copies:
        copy.start()

    local_copies[0].wait()

    def activation_grad(index):
        at = pl.ds(pl.multiple_of(index * ff_block, ff_block), ff_block)
        d_act[index] = dot(dy, wdown[at, :], NT)

    half_blocks = half_ff // ff_block
    for i in range(half_blocks):
        activation_grad(head * half_blocks + i)

    table_copy.wait()
    each(groups - 1, lambda k: request_from(k).wait_recv())
    vocab_lane = lax.broadcasted_iota(jnp.int32, (block, vocab), 1).astype(f32)
    bunch = max(4, groups // 16)
    bunches = groups // bunch
    half_bunches = bunches // 2
    half_groups = groups // 2
    side_of = dp // half_groups

    def row_to(peer):
        return remote(
            found.at[peer], fetched.at[dp], row_send.at[peer], row_recv.at[dp], (peer, head)
        )

    def row_from(peer):
        return remote(
            found.at[peer], fetched.at[peer], row_send.at[peer], row_recv.at[peer], (peer, head)
        )

    def serve(g):
        side = jnp.where(g < half_bunches, 1 - side_of, side_of)
        base = (side * half_bunches + lax.rem(g, half_bunches)) * bunch
        wants = jnp.concatenate(
            [req_in[base + j] for j in range(bunch)] + [jnp.zeros((LANES - bunch, LANES), f32)],
            axis=0,
        ).T
        picks = jnp.concatenate(
            [
                (wants[:block, j : j + 1] == vocab_lane).astype(f32).astype(bf16)
                for j in range(bunch)
            ],
            axis=0,
        )
        picked = dot(picks, table[...]).astype(bf16)
        for j in range(bunch):
            found[base + j] = picked[j * block : (j + 1) * block]

            @pl.when(base + j != dp)
            def _():
                row_to(base + j).start()

    each(bunches, serve)
    fetched[dp] = found[dp]

    prompt_copy.wait()

    prompt_pad[...] = jnp.zeros_like(prompt_pad)
    prompt_pad[:rows, :] = prompt_in[...]
    x0_prompt[...] = dot(order, prompt_pad[...], NN, exact_mode)

    rel_copy.wait()
    spread = lax.broadcasted_iota(jnp.int32, (1, 2 * LANES), 1)
    lag = jnp.where(spread >= LANES, spread - 2 * LANES, spread)
    bucket_row = lax.broadcasted_iota(jnp.int32, (LANES, 2 * LANES), 0)
    for d in range(5):
        if d == 0:
            near = jnp.full((1, 2 * LANES), 15, jnp.int32)
        elif d == 4:
            near = jnp.full((1, 2 * LANES), 31, jnp.int32)
        else:
            near = bucket_of((d - 2) * LANES - lag)
        pick = (bucket_row == near).astype(f32).astype(bf16)
        for side in range(2):
            lines = dot(rel_all[side].astype(bf16), pick)
            for h in range(pairs):
                line = jnp.broadcast_to(lines[h : h + 1, :], (LANES, 2 * LANES))
                if d not in (0, 4):
                    line = pltpu.roll(line, 0, 1, stride=1, stride_axis=0)
                bias[side * pairs + h, d] = line[:, :LANES]

    far_copies[0].wait()
    for i in range(half_blocks):
        activation_grad((1 - head) * half_blocks + i)
    for copy in local_copies[1:]:
        copy.wait()
    far_copies[1].wait()

    spot_lane = lax.broadcasted_iota(jnp.int32, (share, half_groups * block), 1).astype(f32)

    def rows_of(side):
        base = side * half_groups
        take = (place - (base * block).astype(f32) == spot_lane).astype(f32).astype(bf16)
        return dot(
            take, fetched[pl.ds(base, half_groups)].reshape(half_groups * block, width)
        )

    def near_wait(j):
        peer = side_of * half_groups + j

        @pl.when(peer != dp)
        def _():
            row_from(peer).wait_recv()

    each(half_groups, near_wait)
    near_rows = rows_of(side_of)
    x0[...] = near_rows
    x0[:LANES, :] = near_rows[:LANES] + x0_prompt[...]

    each(half_groups, lambda j: row_from((1 - side_of) * half_groups + j).wait_recv())
    x0[...] = x0[...] + rows_of(1 - side_of)

    small_copies[3].wait()
    small_copies[4].wait()
    attn_gain = ag_ref[...].reshape(1, width)
    ff_gain = fg_ref[...].reshape(1, width)
    n1 = rms_scale(x0[...], attn_gain).astype(bf16)
    k_all[head] = dot(n1, wqkv[1]).astype(bf16)
    k_copy = remote(k_all.at[head], k_all.at[head], kv_send.at[0], kv_recv.at[0], other)
    k_copy.start()
    v_all[head] = dot(n1, wqkv[2]).astype(bf16)
    v_copy = remote(v_all.at[head], v_all.at[head], kv_send.at[1], kv_recv.at[1], other)
    v_copy.start()
    q = dot(n1, wqkv[0]).astype(bf16) * jnp.asarray(0.125, bf16)
    for p in range(pairs):
        part = q[:, p * LANES : (p + 1) * LANES]
        qs[p, :share, :] = jnp.where(lane < LANES // 2, part, jnp.zeros_like(part))
        qs[p, share:, :] = jnp.where(lane >= LANES // 2, part, jnp.zeros_like(part))

    far = 1 - head
    blocks = share // LANES
    half = LANES // 2

    def raw_scores(p, side, shift):
        left = jnp.concatenate(
            [k_all[side, :, p * LANES : (p + 1) * LANES], mask_k[side]], axis=1
        )
        right = jnp.concatenate(
            [qs[p], jnp.concatenate([mask_q[...], mask_q[...]], axis=0)], axis=1
        )
        raw = dot(left, right, NT)
        bands = []
        for kb in range(blocks):
            parts_of = []
            for a in range(2):
                for qb in range(blocks):
                    apart = shift + (kb - qb)
                    if isinstance(apart, int):
                        spot = min(max(apart, -2), 2) + 2
                    else:
                        spot = jnp.clip(apart, -2, 2) + 2
                    lo = a * share + qb * LANES
                    parts_of.append(
                        raw[kb * LANES : (kb + 1) * LANES, lo : lo + LANES] + bias[2 * p + a, spot]
                    )
            bands.append(jnp.concatenate(parts_of, axis=1))
        return jnp.concatenate(bands, axis=0)

    for p in range(pairs):
        probs[p, head] = raw_scores(p, head, 0)
    kt[head] = k_all[head].T
    vt[head] = v_all[head].T
    k_copy.wait()
    kt[far] = k_all[far].T
    v_copy.wait()
    vt[far] = v_all[far].T

    far_next = raw_scores(0, far, (1 - 2 * head) * blocks)
    for p in range(pairs):
        near_raw, far_raw = probs[p, head], far_next
        if p + 1 < pairs:
            far_next = raw_scores(p + 1, far, (1 - 2 * head) * blocks)
        top = jnp.maximum(
            jnp.max(near_raw, axis=0, keepdims=True), jnp.max(far_raw, axis=0, keepdims=True)
        )
        near_exp, far_exp = jnp.exp(near_raw - top), jnp.exp(far_raw - top)
        inverse = 1.0 / (
            jnp.sum(near_exp, axis=0, keepdims=True) + jnp.sum(far_exp, axis=0, keepdims=True)
        )
        near_prob, far_prob = near_exp * inverse, far_exp * inverse
        probs[p, head] = near_prob
        probs[p, far] = far_prob
        near_low, far_low = near_prob.astype(bf16), far_prob.astype(bf16)
        for a in range(2):
            feat = slice(p * LANES + a * half, p * LANES + (a + 1) * half)
            side = slice(a * share, (a + 1) * share)
            att_t[feat, :] = (
                dot(vt[head, feat, :], near_low[:, side]) + dot(vt[far, feat, :], far_low[:, side])
            ).astype(bf16)

    far_copies[2].wait()
    x1 = x0[...] + dot(att_t[...].T, wout[...])
    n2 = rms_scale(x1, ff_gain).astype(bf16)
    far_copies[3].wait()
    out_buf[...] = x1
    d_n2 = None
    ff_blocks = ff // ff_block
    units = [slice(i * ff_block, (i + 1) * ff_block) for i in range(ff_blocks)]
    u_next = dot(n2, win[:, units[0]])
    for i in range(ff_blocks):
        u = u_next
        if i + 1 < ff_blocks:
            u_next = dot(n2, win[:, units[i + 1]])
        square = u * u
        t = jnp.tanh(u * (GELU_C + (GELU_C * 0.044715) * square))
        half_u = 0.5 * u
        act[i] = (half_u + half_u * t).astype(bf16)
        slope = (0.5 + 0.5 * t) + (half_u * (1.0 - t * t)) * (
            GELU_C + (GELU_C * 3 * 0.044715) * square
        )
        d_hidden = (d_act[i] * slope).astype(bf16)
        piece = dot(d_hidden, win[:, units[i]], NT)
        d_n2 = piece if d_n2 is None else d_n2 + piece
    dx1 = dy.astype(f32) + rms_back(x1, ff_gain, d_n2)
    grad_buf[...] = dx1
    d_att = dot(dx1.astype(bf16), wout[...], NT).astype(bf16)
    for p in range(pairs):
        part = d_att[:, p * LANES : (p + 1) * LANES]
        dxb[p, :share, :] = jnp.where(lane < LANES // 2, part, jnp.zeros_like(part))
        dxb[p, share:, :] = jnp.where(lane >= LANES // 2, part, jnp.zeros_like(part))

    def first_send(p):
        return remote(d_send.at[0, p], d_recv.at[0, p], dkv_send.at[p], dkv_recv.at[p], other)

    last_send = remote(
        d_send.at[1], d_recv.at[1], dkv_send.at[pairs], dkv_recv.at[pairs], other
    )
    first_rows, last_rows = slice(0, LANES), slice(LANES, share)

    def query_grad(p, begin, end):
        for a in range(2):
            feat = slice(p * LANES + a * half, p * LANES + (a + 1) * half)
            side = slice(a * share + begin, a * share + end)
            att_t[feat, begin:end] = (
                (
                    dot(kt[head, feat, :], d_scores[p, head, :, side])
                    + dot(kt[far, feat, :], d_scores[p, far, :, side])
                )
                * 0.125
            ).astype(bf16)

    def prob_grads(p):
        cols = slice(p * LANES, (p + 1) * LANES)
        return [dot(v_all[side, :, cols], dxb[p], NT) for side in (head, far)]

    d_next = prob_grads(0)
    for p in range(pairs):
        d_out = dxb[p]
        near_d, far_d = d_next
        if p + 1 < pairs:
            d_next = prob_grads(p + 1)
        near_prob, far_prob = probs[p, head], probs[p, far]
        delta = jnp.sum(near_prob * near_d, axis=0, keepdims=True) + jnp.sum(
            far_prob * far_d, axis=0, keepdims=True
        )
        far_score = (far_prob * (far_d - delta)).astype(bf16)
        d_scores[p, far] = far_score
        d_scores[p, head] = (near_prob * (near_d - delta)).astype(bf16)
        d_send[0, p, 1] = dot(far_prob[first_rows].astype(bf16), d_out)
        d_send[0, p, 0] = dot(far_score[first_rows], qs[p])
        first_send(p).start()
    for p in range(pairs):
        dv_own[0, p] = dot(probs[p, head, first_rows].astype(bf16), dxb[p])
        dk_own[0, p] = dot(d_scores[p, head, first_rows], qs[p])
        query_grad(p, 0, LANES)

    def input_grad(index, part):
        d_k = jnp.concatenate(
            [(dk_own[index, p] + d_recv[index, p, 0]).astype(bf16) for p in range(pairs)], axis=1
        )
        d_v = jnp.concatenate(
            [(dv_own[index, p] + d_recv[index, p, 1]).astype(bf16) for p in range(pairs)], axis=1
        )
        d_n1 = acc_dn[part] + dot(d_k, wqkv[1], NT) + dot(d_v, wqkv[2], NT)
        grad_buf[part] = grad_buf[part] + rms_back(x0[part], attn_gain, d_n1)

    acc_dn[first_rows] = dot(att_t[:, first_rows].T, wqkv[0], NT)
    for p in range(pairs):
        first_send(p).wait()
    input_grad(0, first_rows)

    chunks, chunk_rows, chunk_cols = total.shape

    def forward_of(index):
        return remote(
            total.at[index], total.at[index], send4.at[index], recv4.at[index], (dp, 1)
        )

    def in_peer(k):
        target, flip = my_in, inner - k
        for bit in range(inner.bit_length() - 1):
            if flip >> bit & 1:
                target = target + (1 - 2 * lax.rem(my_in // (1 << bit), 2)) * (1 << bit)
        return target, (my_out * inner + target, head)

    def out_peer(k):
        target = lax.rem(my_out + k, outer)
        return target, (target * inner + my_in, head)

    skip = (inner - chunks) // 2

    def chunk_of(place):
        index = place - skip
        return jnp.clip(index, 0, chunks - 1), (index >= 0) & (index < chunks)

    mine_in, sums = chunk_of(my_in)

    def scatter_to(k):
        target, device = in_peer(k)
        at, holds = chunk_of(target)
        return holds, remote(rs_send.at[at], parts.at[my_in], send1.at[k], recv1.at[my_in], device)

    def scatter_from(k):
        source, device = in_peer(k)
        return remote(rs_send.at[0], parts.at[source], send1.at[k], recv1.at[source], device)

    def gather_to(k):
        return remote(
            total.at[mine_in], total.at[mine_in], send2.at[k], recv2.at[mine_in], in_peer(k)[1]
        )

    def gather_from(k):
        source, device = in_peer(k)
        at, holds = chunk_of(source)
        return holds, at, remote(total.at[at], total.at[at], send2.at[k], recv2.at[at], device)

    def across(k):
        return remote(
            across_buf.at[my_out], across_buf.at[my_out], send3.at[k], recv3.at[my_out],
            out_peer(k)[1],
        )

    def across_from(k):
        source, device = out_peer(k)
        return remote(
            across_buf.at[source], across_buf.at[source], send3.at[k], recv3.at[source], device
        )

    @pl.when(head == 0)
    def _():
        rounded = grad_buf[first_rows].astype(bf16)
        local = dot(order.astype(bf16), rounded, TN).astype(bf16)
        for c in range(chunks):
            rs_send[c] = local[c * chunk_rows : (c + 1) * chunk_rows]

        for k in range(1, inner):
            holds, copy = scatter_to(k)

            @pl.when(holds)
            def _():
                copy.start()

    for p in range(pairs):
        d_send[1, p, 1] = dot(probs[p, far, last_rows].astype(bf16), dxb[p])
        d_send[1, p, 0] = dot(d_scores[p, far, last_rows], qs[p])
    last_send.start()
    for p in range(pairs):
        dv_own[1, p] = dot(probs[p, head, last_rows].astype(bf16), dxb[p])
        dk_own[1, p] = dot(d_scores[p, head, last_rows], qs[p])
        query_grad(p, LANES, share)
    for i in range(ff // ff_block):
        out_buf[...] = out_buf[...] + dot(act[i], wdown[i * ff_block : (i + 1) * ff_block, :])
    out_low[...] = out_buf[...].astype(bf16)
    out_copy = pltpu.make_async_copy(out_low, out_hbm, out_sem.at[0])
    out_copy.start()

    @pl.when((head == 0) & sums)
    def _():
        parts[my_in] = rs_send[mine_in]
        for k in range(1, inner):
            scatter_from(k).wait_recv()
        summed = parts[0].astype(f32)
        for source in range(1, inner):
            summed = summed + parts[source].astype(f32)
        if outer > 1:
            across_buf[my_out] = summed
            for k in range(1, outer):
                across(k).start()
            for k in range(1, outer):
                across_from(k).wait_recv()
            summed = across_buf[0]
            for source in range(1, outer):
                summed = summed + across_buf[source]
            for k in range(1, outer):
                across(k).wait_send()
        total[mine_in] = summed.astype(bf16)
        for k in range(1, inner):
            gather_to(k).start()
        forward_of(mine_in).start()

    acc_dn[last_rows] = dot(att_t[:, last_rows].T, wqkv[0], NT)
    last_send.wait()
    input_grad(1, last_rows)
    grad_copy = pltpu.make_async_copy(grad_buf, grad_hbm, out_sem.at[1])
    grad_copy.start()

    @pl.when(head == 0)
    def _():
        for k in range(1, inner):
            holds, at, copy = gather_from(k)

            @pl.when(holds)
            def _():
                copy.wait_recv()
                forward_of(at).start()

    @pl.when(head == 1)
    def _():
        for index in range(chunks):
            forward_of(index).wait_recv()

    total_copy = pltpu.make_async_copy(total, total_hbm, out_sem.at[2])
    total_copy.start()

    each(groups - 1, lambda k: request_to(k).wait_send())
    each(groups - 1, lambda k: row_to(peer_of(k)).wait_send())

    @pl.when(head == 0)
    def _():
        for k in range(1, inner):
            holds, copy = scatter_to(k)

            @pl.when(holds)
            def _():
                copy.wait_send()

        @pl.when(sums)
        def _():
            for k in range(1, inner):
                gather_to(k).wait_send()

        for index in range(chunks):
            forward_of(index).wait_send()

    out_copy.wait()
    grad_copy.wait()
    total_copy.wait()


def vmem(*shape, dtype=f32):
    return pltpu.VMEM(shape, dtype)


def run_layer(
    groups, valid, ids, segments, ag, fg, rel, prompt, cot, table, wqkv, wout, win, wdown
):
    share, width = cot.shape
    ff = 2 * win.shape[1]
    slot = 2 * share
    pairs = width // LANES
    rows = prompt.shape[0]
    ff_block = 768
    capacity = max(2, 2 * slot // (2 * groups))
    block = -(-capacity // 16) * 16
    inner = math.gcd(groups, 16)
    outer = groups // inner
    chunk_rows, chunk_cols = 16, width
    chunks = -(-rows // chunk_rows)
    in_vmem = pl.BlockSpec(memory_space=pltpu.VMEM)
    in_hbm = pl.BlockSpec(memory_space=pl.ANY)
    dma = pltpu.SemaphoreType.DMA
    return pl.pallas_call(
        functools.partial(layer_kernel, groups, inner, block, rows),
        out_shape=(
            jax.ShapeDtypeStruct((share, width), bf16),
            jax.ShapeDtypeStruct((share, width), f32),
            jax.ShapeDtypeStruct((chunks, chunk_rows, chunk_cols), bf16),
        ),
        in_specs=[pl.BlockSpec(memory_space=pltpu.SMEM)] + [in_hbm] * 12,
        out_specs=[in_hbm] * 3,
        scratch_shapes=[
            vmem(*ids.shape, dtype=jnp.int32),
            vmem(*segments.shape, dtype=jnp.int32),
            vmem(*ag.shape),
            vmem(*fg.shape),
            vmem(*rel.shape, dtype=bf16),
            vmem(*table.shape, dtype=bf16),
            vmem(3, width, width, dtype=bf16),
            vmem(width, width, dtype=bf16),
            vmem(width, ff, dtype=bf16),
            vmem(ff, width, dtype=bf16),
            vmem(groups, 1, LANES),
            vmem(groups, 1, LANES),
            vmem(groups, block, width, dtype=bf16),
            vmem(groups, block, width, dtype=bf16),
            vmem(2, 8, LANES),
            vmem(rows, width),
            vmem(LANES, width),
            vmem(share, width, dtype=bf16),
            vmem(1, slot, dtype=jnp.int32),
            vmem(1, slot),
            vmem(2, share, LANES, dtype=bf16),
            vmem(share, LANES, dtype=bf16),
            vmem(share, width),
            vmem(LANES, width),
            vmem(ff // ff_block, share, ff_block),
            vmem(ff // ff_block, share, ff_block, dtype=bf16),
            vmem(pairs, 2, share, slot, dtype=bf16),
            vmem(share, width),
            vmem(share, width),
            vmem(2, share, width, dtype=bf16),
            vmem(2, share, width, dtype=bf16),
            vmem(2, width, share, dtype=bf16),
            vmem(2, width, share, dtype=bf16),
            vmem(pairs, slot, LANES, dtype=bf16),
            vmem(2 * pairs, 5, LANES, LANES),
            vmem(pairs, 2, share, slot),
            vmem(width, share, dtype=bf16),
            vmem(share, width),
            vmem(share, width, dtype=bf16),
        ]
        + [vmem(2, pairs, LANES, LANES)] * 2
        + [vmem(2, pairs, 2, LANES, LANES)] * 2
        + [
            vmem(pairs, slot, LANES, dtype=bf16),
            vmem(chunks, chunk_rows, chunk_cols, dtype=bf16),
            vmem(inner, chunk_rows, chunk_cols, dtype=bf16),
            vmem(outer, chunk_rows, chunk_cols),
            vmem(chunks, chunk_rows, chunk_cols, dtype=bf16),
            dma((12,)),
            dma((5,)),
            dma((5,)),
            dma((groups,)),
            dma((groups,)),
            dma((groups,)),
            dma((groups,)),
            dma((2,)),
            dma((2,)),
            dma((pairs + 1,)),
            dma((pairs + 1,)),
            dma((inner,)),
            dma((inner,)),
            dma((inner,)),
            dma((inner,)),
            dma((outer,)),
            dma((outer,)),
            dma((chunks,)),
            dma((chunks,)),
            dma((3,)),
        ],
        compiler_params=pltpu.CompilerParams(
            collective_id=1, has_side_effects=True, vmem_limit_bytes=60 * 2**20
        ),
        name="layer",
    )(valid, ids, segments, ag, fg, rel, prompt, cot, table, wqkv, wout, win, wdown)


def finish_kernel(
    clip_at, prompt_hbm, first_hbm, second_hbm, total_hbm, out_hbm, grad_hbm,
    *refs,
):
    results, (prompt_ref, first_ref, second_ref, total_ref, out_buf, grad_buf), (
        grad_ref, norm_ref, new_ref, first_out_ref, second_out_ref, low_ref,
    ), (load_sem, store_sem) = refs[:8], refs[8:14], refs[14:20], refs[20:]
    loads = [
        pltpu.make_async_copy(src, dst, load_sem.at[i])
        for i, (src, dst) in enumerate(
            (
                (total_hbm, total_ref), (first_hbm, first_ref), (second_hbm, second_ref),
                (prompt_hbm, prompt_ref), (out_hbm, out_buf), (grad_hbm, grad_buf),
            )
        )
    ]
    for copy in loads:
        copy.start()
    stores = []

    def store(src, index):
        stores.append(pltpu.make_async_copy(src, results[index], store_sem.at[index]))
        stores[-1].start()

    rows = prompt_ref.shape[0]
    loads[0].wait()
    summed = total_ref[...].reshape(-1, total_ref.shape[2]).astype(f32)[:rows]
    grad_ref[...] = summed
    store(grad_ref, 2)
    norm = jnp.sqrt(jnp.sum(summed * summed, keepdims=True))
    norm_ref[...] = norm
    store(norm_ref, 3)
    clipped = summed * jnp.minimum(1.0, clip_at / (norm + 1e-06))
    loads[1].wait()
    first_out = first_decay * first_ref[...] + (1.0 - first_decay) * clipped
    first_out_ref[...] = first_out
    store(first_out_ref, 5)
    loads[2].wait()
    second_out = second_decay * second_ref[...] + (1.0 - second_decay) * clipped * clipped
    second_out_ref[...] = second_out
    store(second_out_ref, 6)
    loads[4].wait()
    store(out_buf, 0)
    loads[5].wait()
    store(grad_buf, 1)
    first_hat = first_out / (1.0 - first_decay**STEP)
    second_hat = second_out / (1.0 - second_decay**STEP)
    loads[3].wait()
    prompt = prompt_ref[...]
    new = prompt - learn_rate * (
        first_hat / (jnp.sqrt(second_hat) + adam_epsilon) + weight_decay * prompt
    )
    new_ref[...] = new
    store(new_ref, 4)
    low_ref[...] = new.astype(bf16)
    store(low_ref, 7)
    for copy in stores:
        copy.wait()


def run_finish(clip_at, total, prompt, first, second, out, grad):
    rows, width = prompt.shape
    shape = jax.ShapeDtypeStruct((rows, width), f32)
    in_hbm = pl.BlockSpec(memory_space=pl.ANY)
    return pl.pallas_call(
        functools.partial(finish_kernel, clip_at),
        out_shape=(
            jax.ShapeDtypeStruct(out.shape, out.dtype),
            jax.ShapeDtypeStruct(grad.shape, grad.dtype),
            shape,
            jax.ShapeDtypeStruct((1, 1), f32),
            shape,
            shape,
            shape,
            jax.ShapeDtypeStruct((rows, width), bf16),
        ),
        in_specs=[in_hbm] * 6,
        out_specs=[in_hbm] * 8,
        scratch_shapes=[
            vmem(rows, width),
            vmem(rows, width),
            vmem(rows, width),
            vmem(*total.shape, dtype=bf16),
            vmem(*out.shape, dtype=bf16),
            vmem(*grad.shape),
            vmem(rows, width),
            vmem(1, 1),
            vmem(rows, width),
            vmem(rows, width),
            vmem(rows, width),
            vmem(rows, width, dtype=bf16),
            pltpu.SemaphoreType.DMA((6,)),
            pltpu.SemaphoreType.DMA((8,)),
        ],
        compiler_params=pltpu.CompilerParams(vmem_limit_bytes=63 * 2**20),
        name="finish",
    )(prompt, first, second, total, out, grad)


def per_device(
    ids,
    segments,
    valid_rows,
    prompt,
    table,
    attn_gain,
    w_qkv,
    rel_bias,
    w_out,
    ff_gain,
    w_in,
    w_down,
    cotangent,
    first_moment,
    second_moment,
):
    groups = lax.axis_size("dp")
    rows, width = prompt.shape
    out, grad, total = run_layer(
        groups, valid_rows, ids, segments, attn_gain, ff_gain, rel_bias.T, prompt, cotangent, table,
        jnp.transpose(w_qkv, (1, 0, 2)), w_out, w_in, w_down,
    )
    clip_at = clip_share * math.sqrt(rows * width * groups)
    final, d_start, prompt_grad, norm, prompt_new, first_out, second_out, low = run_finish(
        clip_at, total, prompt, first_moment, second_moment, out, grad
    )
    return (final, d_start, prompt_grad, norm[0, 0], prompt_new, first_out, second_out, low)


def solution(mesh):
    in_specs = (
        P("dp", None),
        P("dp", None),
        P("dp"),
        P(),
        P("dp", None),
        P(),
        P(None, None, "head"),
        P(None, "head"),
        P("head", None),
        P(),
        P(None, "head"),
        P("head", None),
        P(("dp", "head"), None),
        P(),
        P(),
    )
    out_specs = (P(("dp", "head"), None), P(("dp", "head"), None), P(), P(), P(), P(), P(), P())
    return jax.shard_map(
        per_device, mesh=mesh, in_specs=in_specs, out_specs=out_specs, check_vma=False
    )
```
